128 devices in a mesh: dp: 16 (over z_lo, x, core), ctx: 8 (over y, z_hi).
Axes of the slice: x: 4, y: 4, z: 4 (z_hi: 2, z_lo: 2; z = z_hi * 2 + z_lo), core: 2. Of those that a mesh axis runs over, the one named last changes fastest.
Arguments:
- inputs: bfloat16 [32, 1024, 576], P('dp', 'ctx'), may hold values from -6 to 6
- segments: int32 [32, 1024], P('dp', 'ctx'), may hold values from 0 to 2, as said below
- cotangent: bfloat16 [32, 1024, 576], P('dp', 'ctx'), may hold values from -6 to 6
- attention_gain: float32 [1, 576], replicated, may hold values from 0.1 to 1.9
- query_weight: bfloat16 [1, 576, 576], P(None, 'dp', 'ctx'), may hold values from -0.25 to 0.25
- key_weight: bfloat16 [1, 576, 192], P(None, 'dp', 'ctx'), may hold values from -0.25 to 0.25
- value_weight: bfloat16 [1, 576, 192], P(None, 'dp', 'ctx'), may hold values from -0.25 to 0.25
- out_weight: bfloat16 [1, 576, 576], P(None, 'dp', 'ctx'), may hold values from -2 to 2
- swiglu_gain: float32 [1, 576], replicated, may hold values from 0.1 to 1.9
- gate_weight: bfloat16 [1, 576, 1536], P(None, 'dp', 'ctx'), may hold values from -0.25 to 0.25
- up_weight: bfloat16 [1, 576, 1536], P(None, 'dp', 'ctx'), may hold values from -0.25 to 0.25
- down_weight: bfloat16 [1, 1536, 576], P(None, 'dp', 'ctx'), may hold values from -0.3125 to 0.3125
Outputs:
- outputs: bfloat16 [32, 1024, 576], P('dp', 'ctx')
- input_grad: float32 [32, 1024, 576], P('dp', 'ctx')
- attention_gain_grad: float32 [1, 576], replicated
- query_grad: float32 [1, 576, 576], P(None, 'dp', 'ctx')
- key_grad: float32 [1, 576, 192], P(None, 'dp', 'ctx')
- value_grad: float32 [1, 576, 192], P(None, 'dp', 'ctx')
- out_grad: float32 [1, 576, 576], P(None, 'dp', 'ctx')
- swiglu_gain_grad: float32 [1, 576], replicated
- gate_grad: float32 [1, 576, 1536], P(None, 'dp', 'ctx')
- up_grad: float32 [1, 576, 1536], P(None, 'dp', 'ctx')
- down_grad: float32 [1, 1536, 576], P(None, 'dp', 'ctx')
The draws below stay inside these ranges and needn't reach their ends.
Inputs may be any that keep to these rules, and one draw needn't show every extreme that they name: `segments`: segment numbers never fall along a sequence and rise by one at each new document, from 0; every document has 204 positions or more; of the 2 sequences of each index of dp one is a single document and each other holds three.
All inputs are finite; a program needn't handle non-finite values.
Results may differ from the reference program's by a relative error of at most 0.025.
Values may be sent and summed in bfloat16 or wider, within the bound.
No kernel may reach another device: no remote copies, remote signals or barrier semaphores. Data moves between devices by JAX's collectives and lax.ppermute only.
A program may use at most 128 MiB of HBM per device.

```python
import jax
import jax.numpy as jnp
from jax import lax

D = 576
FF = 1536
HEADS = 9
KV_HEADS = 3
HEAD_DIM = 64
LAYERS = 1
SEQ = 1024
MICRO = 2
SEQS = 32
Q = 576
KV = 192
N_DP = 16


def draw_segments(key, part):
    first_key, second_key, third_key = jax.random.split(key, 3)
    shortest = SEQ // 5
    first_end = jax.random.randint(first_key, (SEQS, 1), shortest, SEQ - 2 * shortest + 1)
    second_len = jax.random.randint(second_key, (SEQS, 1), shortest, SEQ - shortest - first_end + 1)
    second_end = first_end + second_len
    places = jnp.arange(SEQ, dtype=jnp.int32)[None, :]
    packed = (places >= first_end).astype(jnp.int32) + (places >= second_end).astype(jnp.int32)
    chosen = jax.random.randint(third_key, (N_DP, 1), 0, MICRO)
    single = (jnp.arange(MICRO, dtype=jnp.int32)[None, :] == chosen).reshape(SEQS, 1)
    return jnp.where(single, 0, packed).astype(jnp.int32)


def steps_of(rng, extent, cuts, low, largest):
    level = 1.0
    for dim, shards_of in cuts:
        steps = jax.random.uniform(jax.random.fold_in(jax.random.fold_in(rng, 6), dim), (shards_of,), jnp.float32, low / len(cuts), largest / len(cuts))
        level = level * jnp.repeat(jnp.exp(steps), extent[dim] // shards_of).reshape((-1,) + (1,) * (len(extent) - 1 - dim))
    return level


def gaussian(rng, dims, scale, reach, pieces=(), held_as=jnp.bfloat16):
    values = scale * jax.random.normal(rng, dims, jnp.float32)
    if pieces:
        values = values * steps_of(rng, dims, pieces, -0.22, 0.18)
    return jnp.clip(values, -reach, reach).astype(held_as)


def setup_inputs(seed: int = 0) -> dict:
    keys = jax.random.split(jax.random.key(seed), 13)
    return {
        "inputs": gaussian(keys[0], (SEQS, SEQ, D), 1.0, 6.0, ((0, 16), (1, 8))),
        "segments": draw_segments(jax.random.fold_in(keys[12], 71), 0),
        "cotangent": gaussian(keys[2], (SEQS, SEQ, D), 1.0, 6.0, ((0, 16), (1, 8))),
        "attention_gain": jnp.clip(1.0 + 0.18 * jax.random.normal(keys[3], (LAYERS, D), jnp.float32), 0.1, 1.9),
        "query_weight": gaussian(keys[4], (LAYERS, D, Q), D ** -0.5, 0.25, ((1, 16), (2, 8))),
        "key_weight": gaussian(keys[5], (LAYERS, D, KV), D ** -0.5, 0.25, ((1, 16), (2, 8))),
        "value_weight": gaussian(keys[6], (LAYERS, D, KV), D ** -0.5, 0.25, ((1, 16), (2, 8))),
        "out_weight": gaussian(keys[7], (LAYERS, Q, D), (max(D // 64, 1)) ** -0.5, 2.0, ((1, 16), (2, 8))),
        "swiglu_gain": jnp.clip(1.0 + 0.18 * jax.random.normal(keys[8], (LAYERS, D), jnp.float32), 0.1, 1.9),
        "gate_weight": gaussian(keys[9], (LAYERS, D, FF), D ** -0.5, 0.25, ((1, 16), (2, 8))),
        "up_weight": gaussian(keys[10], (LAYERS, D, FF), D ** -0.5, 0.25, ((1, 16), (2, 8))),
        "down_weight": gaussian(keys[11], (LAYERS, FF, D), (FF // 4) ** -0.5, 0.3125, ((1, 16), (2, 8))),
    }


@jax.custom_vjp
def low(v):
    return lax.optimization_barrier(v.astype(jnp.bfloat16)).astype(jnp.float32)

@jax.custom_vjp
def low_back(v):
    return v

def low_keep(v):
    return (low(v), None)

def low_pass(kept, grad):
    return (grad,)

def back_keep(v):
    return (v, None)

def back_low(kept, grad):
    return (low(grad),)
low.defvjp(low_keep, low_pass)
low_back.defvjp(back_keep, back_low)
eps = 1e-05
theta = 10000.0
masked = -1e+30

def product(left, right):
    return jnp.dot(left, right, precision=lax.Precision.HIGHEST, preferred_element_type=jnp.float32)

def rms_scale(hidden, gain):
    return hidden * lax.rsqrt(lax.optimization_barrier(jnp.mean(hidden * hidden, axis=-1, keepdims=True)) + eps) * gain

def rotary_tables(positions):
    half_dim = HEAD_DIM // 2
    inverse_freq = theta ** (-(jnp.arange(half_dim, dtype=jnp.float32) * 2.0) / HEAD_DIM)
    angles = positions.astype(jnp.float32)[:, None] * inverse_freq[None, :]
    cosine = jnp.concatenate([jnp.cos(angles), jnp.cos(angles)], axis=-1)
    sine_table = jnp.concatenate([jnp.sin(angles), jnp.sin(angles)], axis=-1)
    return (cosine, sine_table)

def rotate(values, cosine, sine_table):
    half_dim = values.shape[-1] // 2
    turned = jnp.concatenate([-values[..., half_dim:], values[..., :half_dim]], axis=-1)
    return values * cosine[:, None, :] + turned * sine_table[:, None, :]

def attention(queries, key_rows, values, doc_row):
    seq_len = queries.shape[0]
    block_len = min(512, seq_len)
    group_size = HEADS // KV_HEADS
    score_scale = HEAD_DIM ** (-0.5)
    key_pos = jnp.arange(seq_len, dtype=jnp.int32)
    grouped_keys = key_rows.reshape(seq_len, KV_HEADS, HEAD_DIM)
    grouped_values = values.reshape(seq_len, KV_HEADS, HEAD_DIM)

    def one_block(block_index):
        offset = (block_index * block_len).astype(jnp.int32)
        block_query = lax.dynamic_slice_in_dim(queries, offset, block_len).reshape(block_len, KV_HEADS, group_size, HEAD_DIM)
        query_seg = lax.dynamic_slice_in_dim(doc_row, offset, block_len)
        query_pos = offset + jnp.arange(block_len, dtype=jnp.int32)
        allowed = (query_seg[:, None] == doc_row[None, :]) & (query_pos[:, None] >= key_pos[None, :])
        scores = jnp.einsum('qhgd,thd->hgqt', block_query, grouped_keys, precision=lax.Precision.HIGHEST) * score_scale
        scores = low_back(scores)
        scores = jnp.where(allowed[None, None], scores, masked)
        maxima = lax.optimization_barrier(jnp.max(scores, axis=-1, keepdims=True))
        exponent = jnp.where(allowed[None, None], jnp.exp(scores - maxima), 0.0)
        weights_f = exponent / lax.optimization_barrier(jnp.sum(exponent, axis=-1, keepdims=True))
        mixed_out = jnp.einsum('hgqt,thd->qhgd', weights_f, grouped_values, precision=lax.Precision.HIGHEST)
        return mixed_out.reshape(block_len, HEADS * HEAD_DIM)
    blocks = lax.map(jax.checkpoint(one_block), jnp.arange(seq_len // block_len, dtype=jnp.int32))
    return blocks.reshape(seq_len, HEADS * HEAD_DIM)

def layer_forward(hidden, layer_params, doc_row, cosine, sine_table):
    attention_gain, query_weight, key_weight, value_weight, out_weight, swiglu_gain, gate_weight, up_weight, down_weight = layer_params
    seq_len = hidden.shape[0]
    normed = low(rms_scale(hidden, attention_gain))
    query_pre = low_back(product(normed, query_weight))
    key_pre = low_back(product(normed, key_weight))
    values = low(low_back(product(normed, value_weight)))
    queries = low(rotate(query_pre.reshape(seq_len, HEADS, HEAD_DIM), cosine, sine_table).reshape(seq_len, HEADS * HEAD_DIM))
    key_rows = low(rotate(key_pre.reshape(seq_len, KV_HEADS, HEAD_DIM), cosine, sine_table).reshape(seq_len, KV_HEADS * HEAD_DIM))
    mixed_out = low(low_back(attention(queries, key_rows, values, doc_row)))
    middle = hidden + low_back(product(mixed_out, out_weight))
    second = low(rms_scale(middle, swiglu_gain))
    gate_pre = low_back(product(second, gate_weight))
    up_pre = low_back(product(second, up_weight))
    inner_act = low(jax.nn.silu(gate_pre) * up_pre)
    return middle + low_back(product(inner_act, down_weight))

def reference(inputs, segments, cotangent, attention_gain, query_weight, key_weight, value_weight, out_weight, swiglu_gain, gate_weight, up_weight, down_weight):
    params = tuple((stacked.astype(jnp.float32) for stacked in (attention_gain, query_weight, key_weight, value_weight, out_weight, swiglu_gain, gate_weight, up_weight, down_weight)))
    cosine, sine_table = rotary_tables(jnp.arange(SEQ, dtype=jnp.int32))

    def one_sequence(totals, batch_items):
        seq_in, seq_seg, seq_cot = batch_items

        def forward(hidden, weights):
            for layer_index in range(LAYERS):
                hidden = layer_forward(hidden, tuple((stacked[layer_index] for stacked in weights)), seq_seg, cosine, sine_table)
            return hidden
        result, pullback = jax.vjp(forward, seq_in.astype(jnp.float32), params)
        grad_in, grad_params = pullback(seq_cot.astype(jnp.float32))
        totals = tuple((running + added for running, added in zip(totals, grad_params)))
        return (totals, (result.astype(jnp.bfloat16), grad_in))
    zeros = tuple((jnp.zeros_like(stacked) for stacked in params))
    totals, (outputs, input_grad) = lax.scan(one_sequence, zeros, (inputs, segments, cotangent))
    return (outputs, input_grad, totals[0], totals[1], totals[2], totals[3], totals[4], totals[5], totals[6], totals[7], totals[8])
```

```python
import jax
import jax.numpy as jnp
import numpy as np
from jax import lax
from jax.sharding import PartitionSpec as P

HEADS = 9
KV_HEADS = 3
HEAD_DIM = 64
GROUP = HEADS // KV_HEADS
D = 576
FF = 1536
KV = KV_HEADS * HEAD_DIM

eps = 1e-05
theta = 10000.0
masked = -1e30
bf16 = jnp.bfloat16
f32 = jnp.float32

N_CTX = 8
N_DP = 16
EVERY = ("dp", "ctx")
SAME_CORE = [
    [(zx * 2 + core) * N_CTX + ctx for ctx in range(N_CTX) for zx in range(N_DP // 2)]
    for core in range(2)
]
OTHER_CORE = [(dp * N_CTX + ctx, (dp ^ 1) * N_CTX + ctx) for dp in range(N_DP) for ctx in range(N_CTX)]
WIDTHS = (72, 24, 24, 72, 192, 192)


def matmul(left, right):
    return jnp.dot(left, right, preferred_element_type=f32)


def matmul_tn(left, right):
    return lax.dot_general(left, right, (((0,), (0,)), ((), ())), preferred_element_type=f32)


def matmul_nt(left, right):
    return lax.dot_general(left, right, (((1,), (1,)), ((), ())), preferred_element_type=f32)


def rms_scale(hidden, gain):
    return hidden * lax.rsqrt(jnp.mean(hidden * hidden, axis=-1, keepdims=True) + eps) * gain


def norm_back(x, gain, c):
    rho = lax.rsqrt(jnp.mean(x * x, axis=-1, keepdims=True) + eps)
    w = c * gain
    grad = rho * (w - x * (rho * rho * jnp.mean(w * x, axis=-1, keepdims=True)))
    return grad, jnp.sum(c * x * rho, axis=0, keepdims=True)


def rotary_tables(positions):
    half_dim = HEAD_DIM // 2
    inverse_freq = theta ** (-(jnp.arange(half_dim, dtype=f32) * 2.0) / HEAD_DIM)
    angles = positions.astype(f32)[:, None] * inverse_freq[None, :]
    cosine = jnp.concatenate([jnp.cos(angles), jnp.cos(angles)], axis=-1)
    sine_table = jnp.concatenate([jnp.sin(angles), jnp.sin(angles)], axis=-1)
    return (cosine, sine_table)


def rotate(values, cosine, sine_table):
    rows, width = values.shape
    shaped = values.reshape(rows, width // HEAD_DIM, HEAD_DIM)
    half = HEAD_DIM // 2
    turned = jnp.concatenate([-shaped[..., half:], shaped[..., :half]], axis=-1)
    return (shaped * cosine[:, None, :] + turned * sine_table[:, None, :]).reshape(rows, width)


def rotate_back(values, cosine, sine_table):
    rows, width = values.shape
    shaped = values.reshape(rows, width // HEAD_DIM, HEAD_DIM)
    half = HEAD_DIM // 2
    scaled = shaped * sine_table[:, None, :]
    turned = jnp.concatenate([scaled[..., half:], -scaled[..., :half]], axis=-1)
    return (shaped * cosine[:, None, :] + turned).reshape(rows, width)


def gather_weights(shards):
    core = lax.axis_index("dp") % 2
    down = shards[6][0].reshape(36, 192)
    payload = jnp.concatenate([s[0] for s in shards[:6]] + [down], axis=1)
    slots = jnp.broadcast_to(payload[None], (64, 36, 768))
    mine = lax.all_to_all(slots, EVERY, 0, 0, tiled=True, axis_index_groups=SAME_CORE)
    other = lax.ppermute(mine, EVERY, OTHER_CORE)
    first = jnp.where(core == 0, mine, other)
    second = jnp.where(core == 0, other, mine)
    whole = jnp.stack([first, second]).reshape(2, N_CTX, 8, 36, 768)
    weights = []
    start = 0
    for width in WIDTHS:
        part = whole[..., start : start + width].transpose(2, 0, 3, 1, 4)
        weights.append(part.reshape(D, N_CTX * width))
        start += width
    down = whole[..., D:].reshape(2, N_CTX, 8, 96, 72).transpose(2, 0, 3, 1, 4)
    weights.append(down.reshape(FF, D))
    return weights


def reduce_grads(grads, gains):
    core = lax.axis_index("dp") % 2
    pieces = [
        g.astype(bf16).reshape(8, 2, 36, N_CTX, width).transpose(1, 3, 0, 2, 4)
        for g, width in zip(grads[:6], WIDTHS)
    ]
    down = grads[6].astype(bf16).reshape(8, 2, 96, N_CTX, 72).transpose(1, 3, 0, 2, 4)
    pieces.append(down.reshape(2, N_CTX, 8, 36, 192))
    whole = jnp.concatenate(pieces, axis=-1).reshape(2, 64, 36, 768)
    keep = lax.dynamic_index_in_dim(whole, core, 0, keepdims=False)
    give = lax.dynamic_index_in_dim(whole, 1 - core, 0, keepdims=False)
    got = lax.ppermute(give, EVERY, OTHER_CORE)
    pair = (keep.astype(f32) + got.astype(f32)).astype(bf16)
    high = gains.astype(bf16)
    low = (gains - high.astype(f32)).astype(bf16)
    extra = jnp.concatenate(
        [jnp.pad(p, ((0, 0), (0, 192))) for p in (high, low)], axis=0
    )
    slots = jnp.concatenate([pair, jnp.broadcast_to(extra[None], (64, 4, 768))], axis=1)
    came = lax.all_to_all(slots, EVERY, 0, 0, tiled=True, axis_index_groups=SAME_CORE)
    total = jnp.sum(came.astype(f32), axis=0)
    gain_half = total[36:38, :D] + total[38:40, :D]
    gain_total = gain_half + lax.ppermute(gain_half, EVERY, OTHER_CORE)
    outs = []
    start = 0
    for width in WIDTHS:
        outs.append(total[None, :36, start : start + width])
        start += width
    outs.append(total[:36, D:].reshape(1, 96, 72))
    return outs, gain_total


def body(
    inputs,
    segments,
    cotangent,
    attention_gain,
    query_weight,
    key_weight,
    value_weight,
    out_weight,
    swiglu_gain,
    gate_weight,
    up_weight,
    down_weight,
):
    batch, rows, _ = inputs.shape
    seq = rows * N_CTX
    score_scale = HEAD_DIM ** (-0.5)
    ctx = lax.axis_index("ctx")
    sent = jnp.concatenate([inputs, segments.astype(bf16)[..., None]], axis=-1)
    came = lax.all_gather(sent, "ctx", axis=1, tiled=True)
    wq, wk, wv, wo, wg, wu, wd = gather_weights(
        (query_weight, key_weight, value_weight, out_weight, gate_weight, up_weight, down_weight)
    )
    first_gain = attention_gain[0]
    second_gain = swiglu_gain[0]
    whole = came[..., :D].reshape(batch * seq, D).astype(f32)
    doc = came[..., D].astype(f32)
    hidden = inputs.reshape(batch * rows, D).astype(f32)
    gradient = cotangent.reshape(batch * rows, D).astype(f32)
    grad_b = cotangent.reshape(batch * rows, D)

    query_pos = ctx * rows + jnp.arange(rows, dtype=jnp.int32)
    key_pos = jnp.arange(seq, dtype=jnp.int32)
    allowed = (segments.astype(f32)[:, :, None] == doc[:, None, :]) & (
        query_pos[:, None] >= key_pos[None, :]
    )[None]
    allowed = allowed[:, None, None]
    cos_k, sin_k = rotary_tables(key_pos)
    cos_q, sin_q = rotary_tables(query_pos)
    cos_k, sin_k = jnp.tile(cos_k, (batch, 1)), jnp.tile(sin_k, (batch, 1))
    cos_q, sin_q = jnp.tile(cos_q, (batch, 1)), jnp.tile(sin_q, (batch, 1))

    normed_all = rms_scale(whole, first_gain).astype(bf16)
    normed = rms_scale(hidden, first_gain).astype(bf16)
    keys = rotate(matmul(normed_all, wk), cos_k, sin_k).astype(bf16)
    values = matmul(normed_all, wv).astype(bf16)
    queries = rotate(matmul(normed, wq), cos_q, sin_q).astype(bf16)

    def heads_q(x):
        return x.reshape(batch, rows, KV_HEADS, GROUP, HEAD_DIM).transpose(0, 2, 3, 1, 4)

    def heads_k(x):
        return x.reshape(batch, seq, KV_HEADS, HEAD_DIM).transpose(0, 2, 1, 3)

    def from_q(x):
        return x.transpose(0, 3, 1, 2, 4).reshape(batch * rows, D)

    def from_k(x):
        return x.transpose(0, 2, 1, 3).reshape(batch * seq, KV)

    qh, kh, vh = heads_q(queries), heads_k(keys), heads_k(values)

    def ein(spec, a, b):
        return jnp.einsum(spec, a, b, preferred_element_type=f32)

    scores = jnp.where(allowed, ein("bhgsd,bhtd->bhgst", qh, kh) * score_scale, masked)
    top = jnp.max(scores, axis=-1, keepdims=True)
    expo = jnp.where(allowed, jnp.exp(scores - top), 0.0)
    probs = expo / jnp.sum(expo, axis=-1, keepdims=True)
    probs_b = probs.astype(bf16)
    mixed_h = ein("bhgst,bhtd->bhgsd", probs_b, vh)
    mixed_b = from_q(mixed_h).astype(bf16)
    middle = hidden + matmul(mixed_b, wo)
    second = rms_scale(middle, second_gain).astype(bf16)
    gate = matmul(second, wg)
    up = matmul(second, wu)
    logistic = jax.nn.sigmoid(gate)
    silu = gate * logistic
    inner_b = (silu * up).astype(bf16)
    result = middle + matmul(inner_b, wd)

    down_term = matmul_tn(inner_b, grad_b)
    inner_grad = matmul_nt(grad_b, wd)
    gate_grad_b = (inner_grad * up * (logistic * (1 + gate * (1 - logistic)))).astype(bf16)
    up_grad_b = (inner_grad * silu).astype(bf16)
    gate_term = matmul_tn(second, gate_grad_b)
    up_term = matmul_tn(second, up_grad_b)
    second_grad = matmul_nt(gate_grad_b, wg) + matmul_nt(up_grad_b, wu)
    middle_norm, second_gain_term = norm_back(middle, second_gain, second_grad)
    middle_grad = gradient + middle_norm
    middle_b = middle_grad.astype(bf16)
    out_term = matmul_tn(mixed_b, middle_b)
    mixed_grad = matmul_nt(middle_b, wo).astype(bf16)

    gh = heads_q(mixed_grad)
    prob_grad = ein("bhgsd,bhtd->bhgst", gh, vh)
    delta = jnp.sum(gh.astype(f32) * mixed_h, axis=-1, keepdims=True)
    ds = (probs * (prob_grad - delta)).astype(bf16)
    turned_query = from_q(ein("bhgst,bhtd->bhgsd", ds, kh)) * score_scale
    turned_key = from_k(ein("bhgst,bhgsd->bhtd", ds, qh)) * score_scale
    value_pre = from_k(ein("bhgst,bhgsd->bhtd", probs_b, gh)).astype(bf16)
    query_pre = rotate_back(turned_query, cos_q, sin_q).astype(bf16)
    key_pre = rotate_back(turned_key, cos_k, sin_k).astype(bf16)

    query_term = matmul_tn(normed, query_pre)
    key_term = matmul_tn(normed_all, key_pre)
    value_term = matmul_tn(normed_all, value_pre)

    both = jnp.concatenate([key_pre, value_pre], axis=-1).reshape(batch, N_CTX, rows, 2 * KV)
    both = lax.all_to_all(both.transpose(1, 0, 2, 3), "ctx", 0, 0, tiled=True)
    both = jnp.sum(both.astype(f32), axis=0).reshape(batch * rows, 2 * KV).astype(bf16)
    normed_grad = (
        matmul_nt(query_pre, wq) + matmul_nt(both[:, :KV], wk) + matmul_nt(both[:, KV:], wv)
    )
    hidden_norm, first_gain_term = norm_back(hidden, first_gain, normed_grad)
    input_grad = middle_grad + hidden_norm

    outs, gains = reduce_grads(
        (query_term, key_term, value_term, out_term, gate_term, up_term, down_term),
        jnp.concatenate([first_gain_term, second_gain_term], axis=0),
    )
    return (
        result.astype(bf16).reshape(batch, rows, D),
        input_grad.reshape(batch, rows, D),
        gains[0:1],
        outs[0],
        outs[1],
        outs[2],
        outs[3],
        gains[1:2],
        outs[4],
        outs[5],
        outs[6],
    )


def solution(mesh):
    weight = P(None, "dp", "ctx")
    rows = P("dp", "ctx", None)
    return jax.shard_map(
        body,
        mesh=mesh,
        in_specs=(rows, P("dp", "ctx"), rows, P(), weight, weight, weight, weight, P(), weight, weight, weight),
        out_specs=(rows, rows, P(), weight, weight, weight, weight, P(), weight, weight, weight),
        check_vma=False,
    )
```

```python
import functools

import jax
import jax.numpy as jnp
from jax import lax
from jax.experimental import pallas as pl
from jax.experimental.pallas import tpu as pltpu
from jax.sharding import PartitionSpec as P

HEADS = 9
KV_HEADS = 3
HEAD_DIM = 64
GROUP = HEADS // KV_HEADS
D = 576
FF = 1536
KV = KV_HEADS * HEAD_DIM
BATCH = 2
ROWS = 128
SEQ = 1024
OWN = BATCH * ROWS
ALL = BATCH * SEQ
N_CTX = 8
N_DP = 16
N_ZX = N_DP // 2
SLOTS = N_CTX * N_ZX
SLOT_ROWS = 48
PAD_D = N_DP * SLOT_ROWS
RAW = N_CTX * 128
PAD_Q = HEADS * 128
PAD_KV = KV_HEADS * 128
STACK = GROUP * ROWS
PAIRS = BATCH * KV_HEADS

eps = 1e-05
theta = 10000.0
masked = -1e30
bf16 = jnp.bfloat16
f32 = jnp.float32

EVERY = ("dp", "ctx")
SAME_CORE = [
    [(zx * 2 + core) * N_CTX + ctx for ctx in range(N_CTX) for zx in range(N_ZX)]
    for core in range(2)
]
OTHER_CORE = [
    (dp * N_CTX + ctx, (dp ^ 1) * N_CTX + ctx) for dp in range(N_DP) for ctx in range(N_CTX)
]


def nn(left, right):
    return jnp.dot(left, right, preferred_element_type=f32)


def tn(left, right):
    return lax.dot_general(left, right, (((0,), (0,)), ((), ())), preferred_element_type=f32)


def nt(left, right):
    return lax.dot_general(left, right, (((1,), (1,)), ((), ())), preferred_element_type=f32)


def halves(x):
    high = x.astype(bf16)
    return high, (x - high.astype(f32)).astype(bf16)


def rho_of(x):
    return lax.rsqrt(jnp.mean(x * x, axis=-1, keepdims=True) + eps)


def norm_back(x, gain, c):
    rho = rho_of(x)
    w = c * gain
    grad = rho * (w - x * (rho * rho * jnp.mean(w * x, axis=-1, keepdims=True)))
    return grad, jnp.sum(c * (x * rho), axis=0, keepdims=True)


def lanes(shape):
    return lax.broadcasted_iota(jnp.int32, shape, 1)


def turn(x, cosine, sine):
    first = lanes(x.shape) < HEAD_DIM // 2
    turned = jnp.where(first, -pltpu.roll(x, 96, 1), pltpu.roll(x, 32, 1))
    return x * cosine + turned * sine


def turn_back(x, cosine, sine):
    lane = lanes(x.shape)
    w = x * sine
    second = jnp.where(lane < HEAD_DIM, -pltpu.roll(w, 32, 1), 0.0)
    turned = jnp.where(lane < HEAD_DIM // 2, pltpu.roll(w, 96, 1), second)
    return x * cosine + turned


def triple(x, axis):
    return jnp.concatenate([x] * GROUP, axis=axis)


def from_slots(core, mine, other, part, dest, width):
    for ref, who in ((mine, core), (other, 1 - core)):
        for zx in range(N_ZX):
            row = pl.multiple_of((2 * zx + who) * SLOT_ROWS, SLOT_ROWS)
            for c in range(N_CTX):
                dest[pl.ds(row, SLOT_ROWS), c * width : (c + 1) * width] = ref[
                    c * N_ZX + zx, :, part : part + width
                ]


def to_slots(core, src, keep, give, part, width, ctxs=range(N_CTX), base=0):
    for ref, who in ((keep, core), (give, 1 - core)):
        for zx in range(N_ZX):
            row = pl.multiple_of((2 * zx + who) * SLOT_ROWS, SLOT_ROWS)
            for c in ctxs:
                at = (c - base) * width
                ref[c * N_ZX + zx, :, part : part + width] = src[
                    pl.ds(row, SLOT_ROWS), at : at + width
                ]


def hidden_place(unit):
    n = unit * 16
    c, m = divmod(n, 192)
    base = (c // 2) * 384
    if m < 128:
        return base + (c % 2) * 128 + m
    return base + 256 + (c % 2) * 64 + (m - 128)


def forward_kernel(
    place, mine, other, xall, xown, gain, segq, segk, cosk, sink, cosq, sinq, pr, sq, so, po,
    wq, wkv, wo, nall, nown, qs, kp, vp, pt, mixr, middle,
    araw, oraw, wpad, wmid, bias, mixp,
):
    core = place[0]
    ctx = place[1]
    from_slots(core, mine, other, 0, araw, 128)
    from_slots(core, mine, other, 128, oraw, 128)
    wmid[...] = nn(pr[...], araw[...]).astype(bf16)
    wq[...] = nn(wmid[...], sq[:, :PAD_Q]).astype(bf16)
    wpad[...] = nn(wmid[...], sq[:, PAD_Q : PAD_Q + 2 * PAD_KV]).astype(bf16)
    wkv[...] = nn(wmid[...], sq[:, PAD_Q + 2 * PAD_KV :]).astype(bf16)
    wo[...] = nn(oraw[...], so[...]).astype(bf16)

    x = xown[...].astype(f32)
    normed = (x * rho_of(x) * gain[...]).astype(bf16)
    nown[...] = normed
    for head in range(HEADS):
        pre = nn(normed, wq[:, head * 128 : (head + 1) * 128])
        h, g = divmod(head, GROUP)
        for b in range(BATCH):
            turned = turn(pre[b * ROWS : (b + 1) * ROWS], cosq[...], sinq[...])
            qs[b * KV_HEADS + h, g * ROWS : (g + 1) * ROWS, :] = (
                turned.astype(bf16) * bf16(HEAD_DIM**-0.5)
            )

    for b in range(BATCH):

        def chunk(i, carry, b=b):
            at = pl.multiple_of(i * 256, 256)
            x = xall[pl.ds(b * SEQ + at, 256), :].astype(f32)
            normed = (x * rho_of(x) * gain[...]).astype(bf16)
            nall[pl.ds(b * SEQ + at, 256), :] = normed
            pre = nn(normed, wpad[...])
            cosine, sine = cosk[pl.ds(at, 256), :], sink[pl.ds(at, 256), :]
            for h in range(KV_HEADS):
                kp[b * KV_HEADS + h, pl.ds(at, 256), :] = turn(
                    pre[:, h * 128 : (h + 1) * 128], cosine, sine
                ).astype(bf16)
                vp[b * KV_HEADS + h, pl.ds(at, 256), :] = pre[
                    :, PAD_KV + h * 128 : PAD_KV + (h + 1) * 128
                ].astype(bf16)
            return carry

        lax.fori_loop(0, SEQ // 256, chunk, 0)
        key_pos = lax.broadcasted_iota(jnp.int32, (SEQ, ROWS), 0)
        query_pos = ctx * ROWS + lanes((SEQ, ROWS))
        same = segk[b * SEQ : (b + 1) * SEQ, :].astype(f32) == segq[b : b + 1, :]
        bias[b] = jnp.where(same & (key_pos <= query_pos), 0.0, masked)

    def attend(i, carry):
        b = i // KV_HEADS
        h = i - b * KV_HEADS
        scores = nt(kp[i], qs[i]) + triple(bias[b], 1)
        top = jnp.max(scores, axis=0, keepdims=True)
        expo = jnp.exp(scores - top)
        total = jnp.sum(expo, axis=0, keepdims=True)
        probs = (expo * (1.0 / total)).astype(bf16)
        pt[i] = probs
        mixed = tn(vp[i], probs).T.astype(bf16)
        for g in range(GROUP):
            mixp[
                pl.ds(pl.multiple_of(b * ROWS, ROWS), ROWS),
                pl.ds(pl.multiple_of((h * GROUP + g) * 128, 128), 128),
            ] = mixed[g * ROWS : (g + 1) * ROWS]
        return carry

    lax.fori_loop(0, PAIRS, attend, 0)
    placed = nn(mixp[...], po[...]).astype(bf16)
    mixr[...] = placed
    middle[...] = xown[...].astype(f32) + nn(placed, wo[...])


def feed_kernel(
    place, mine, other, tile1, tile1_other, middle, mixr, cot, gain, wo, pr, so, po,
    result, gs, keep, give, middle_grad, gain_grad,
    gu, down, dgu, dt, d1, dd,
):
    core = place[0]
    from_slots(core, mine, other, 0, gu, 384)
    low = lanes((SLOT_ROWS, 128)) < 64
    tail = lanes((SLOT_ROWS, 128)) < 72
    for main, extra, who in ((mine, tile1, core), (other, tile1_other, 1 - core)):

        def unpack(zx, carry, main=main, extra=extra, who=who):
            dp = 2 * zx + who
            for c in range(N_CTX):
                t = main[c * N_ZX + zx, :, 384:512].astype(f32)
                e = extra[c * N_ZX + zx, :, 128:256].astype(f32)
                first = jnp.where(low, t, jnp.where(tail, pltpu.roll(e, 128 - 8, 1), 0.0))
                second = jnp.where(
                    low, pltpu.roll(t, 64, 1), jnp.where(tail, pltpu.roll(e, 128 - 16, 1), 0.0)
                )
                at = pl.multiple_of(dp * 96, 16)
                dd[pl.ds(at, 48), c * 128 : (c + 1) * 128] = first.astype(bf16)
                dd[pl.ds(at + 48, 48), c * 128 : (c + 1) * 128] = second.astype(bf16)
            return carry

        lax.fori_loop(0, N_ZX, unpack, 0)
    for unit in range(FF // 16):
        at = hidden_place(unit)
        down[at : at + 16, :] = dd[unit * 16 : unit * 16 + 16, :]

    mid = middle[...]
    rho = rho_of(mid)
    second = (mid * rho * gain[...]).astype(bf16)
    second_r = nn(second, pr[...]).astype(bf16)
    e_b = cot[...]
    e_raw = nt(e_b, so[...]).astype(bf16)
    low = lanes((OWN, 128)) < 64
    grad_sum = jnp.zeros((OWN, PAD_D), f32)
    result_sum = jnp.zeros((OWN, RAW), f32)
    for pair in range(N_CTX // 2):
        weight = gu[:, pair * 768 : (pair + 1) * 768]
        pre = nn(second_r, weight)
        a, u, t, a2, u2, t2 = (pre[:, i * 128 : (i + 1) * 128] for i in range(6))
        gate = jnp.concatenate([a, a2, jnp.where(low, t, pltpu.roll(t2, 64, 1))], axis=1)
        up = jnp.concatenate([u, u2, jnp.where(low, pltpu.roll(t, 64, 1), t2)], axis=1)
        logistic = 1.0 / (1.0 + jnp.exp(-gate))
        silu = gate * logistic
        inner = (silu * up).astype(bf16)
        rows = down[pair * 384 : (pair + 1) * 384, :]
        result_sum += nn(inner, rows)
        inner_grad = nt(e_raw, rows)
        gate_grad = inner_grad * up * (logistic * (1.0 + gate * (1.0 - logistic)))
        up_grad = inner_grad * silu
        a, a2, gt = (gate_grad[:, i * 128 : (i + 1) * 128] for i in range(3))
        u, u2, ut = (up_grad[:, i * 128 : (i + 1) * 128] for i in range(3))
        t = jnp.where(low, gt, pltpu.roll(ut, 64, 1))
        t2 = jnp.where(low, pltpu.roll(gt, 64, 1), ut)
        grads = jnp.concatenate([a, u, t, a2, u2, t2], axis=1).astype(bf16)
        grad_sum += nt(grads, weight)
        dgu[...] = tn(second_r, grads).astype(bf16)
        to_slots(core, dgu, keep, give, 128, 384, (2 * pair, 2 * pair + 1), 2 * pair)
        dd_pair = tn(inner, e_raw).astype(bf16)
        for unit in range(pair * 24, pair * 24 + 24):
            at = hidden_place(unit) - pair * 384
            dd[unit * 16 : unit * 16 + 16, :] = dd_pair[at : at + 16, :]

    high, rest = halves(result_sum)
    result[...] = (mid + (nn(high, so[...]) + nn(rest, so[...]))).astype(bf16)
    high, rest = halves(grad_sum)
    second_grad = nt(high, pr[...]) + nt(rest, pr[...])
    norm_grad, gain_term = norm_back(mid, gain[...], second_grad)
    gain_grad[...] = gain_term
    total = e_b.astype(f32) + norm_grad
    middle_grad[...] = total
    middle_b = total.astype(bf16)
    middle_raw = nt(middle_b, so[...]).astype(bf16)
    d1[...] = tn(mixr[...], middle_raw)
    back = nt(nt(middle_b, wo[...]).astype(bf16), po[...]).astype(bf16)
    for head in range(HEADS):
        h, g = divmod(head, GROUP)
        for b in range(BATCH):
            gs[b * KV_HEADS + h, g * ROWS : (g + 1) * ROWS, :] = back[
                b * ROWS : (b + 1) * ROWS, head * 128 : (head + 1) * 128
            ]

    lane = lanes((SLOT_ROWS, 128))
    for ref, who in ((keep, core), (give, 1 - core)):

        def pack(zx, carry, ref=ref, who=who):
            dp = 2 * zx + who
            for c in range(N_CTX):
                at = pl.multiple_of(dp * 96, 16)
                first = dd[pl.ds(at, 48), c * 128 : (c + 1) * 128].astype(f32)
                second = dd[pl.ds(at + 48, 48), c * 128 : (c + 1) * 128].astype(f32)
                t = jnp.where(lane < 64, first, pltpu.roll(second, 64, 1))
                own = d1[
                    pl.ds(pl.multiple_of(dp * SLOT_ROWS, SLOT_ROWS), SLOT_ROWS),
                    c * 128 : (c + 1) * 128,
                ]
                e = jnp.where(
                    lane < 72,
                    own,
                    jnp.where(
                        lane < 80,
                        pltpu.roll(first, 8, 1),
                        jnp.where(lane < 88, pltpu.roll(second, 16, 1), 0.0),
                    ),
                )
                ref[c * N_ZX + zx, :, 0:128] = e.astype(bf16)
                ref[c * N_ZX + zx, :, 512:640] = t.astype(bf16)
            return carry

        lax.fori_loop(0, N_ZX, pack, 0)


def backward_kernel(
    place, pt, qs, kp, vp, gs, nall, nown, xall, xown, wq, wkv, gain_grad, cosk, sink, cosq, sinq, pr, sq,
    keep, give, dkv, query_part,
    dqp, dk, dv, dw, raw,
):
    core = place[0]

    def attend(i, carry):
        b = i // KV_HEADS
        h = i - b * KV_HEADS
        g_b = gs[i]
        probs_b = pt[i]
        probs = probs_b.astype(f32)
        weighted = probs * nt(vp[i], g_b)
        delta = jnp.sum(weighted, axis=0, keepdims=True)
        ds = (weighted - probs * delta).astype(bf16)
        dk[i] = turn_back(nn(ds, qs[i]), cosk[...], sink[...]).astype(bf16)
        dv[i] = nn(probs_b, g_b).astype(bf16)
        dq = tn(kp[i], ds).T * HEAD_DIM**-0.5
        for g in range(GROUP):
            dqp[
                pl.ds(pl.multiple_of(b * ROWS, ROWS), ROWS),
                pl.ds(pl.multiple_of((h * GROUP + g) * 128, 128), 128),
            ] = turn_back(dq[g * ROWS : (g + 1) * ROWS], cosq[...], sinq[...]).astype(bf16)
        return carry

    lax.fori_loop(0, PAIRS, attend, 0)

    dw[...] = jnp.zeros(dw.shape, f32)
    raw[...] = jnp.zeros(raw.shape, f32)
    term = jnp.zeros((1, D), f32)
    for b in range(BATCH):

        def chunk(i, term, b=b):
            at = pl.multiple_of(i * 256, 256)
            tiles = [dk[b * 3 + h, pl.ds(at, 256), :].astype(f32) for h in range(3)]
            tiles += [dv[b * 3 + h, pl.ds(at, 256), :].astype(f32) for h in range(3)]
            packed = jnp.concatenate(
                [tiles[2 * j] + pltpu.roll(tiles[2 * j + 1], 64, 1) for j in range(3)], axis=1
            ).astype(bf16)
            for k in range(2):
                dkv[i * 2 + k, b * ROWS : (b + 1) * ROWS, :] = packed[k * ROWS : (k + 1) * ROWS]
            dw[...] += tn(nall[pl.ds(b * SEQ + at, 256), :], packed)
            x = xall[pl.ds(b * SEQ + at, 256), :].astype(f32)
            part = nt(packed, wkv[...])
            return term + jnp.sum(part * (x * rho_of(x)), axis=0, keepdims=True)

        term = lax.fori_loop(0, SEQ // 256, chunk, term)

    dq = dqp[...]
    part = nt(dq, wq[...])
    query_part[...] = part
    x = xown[...].astype(f32)
    term = term + jnp.sum(part * (x * rho_of(x)), axis=0, keepdims=True)

    dq_raw = nt(dq, sq[:, :PAD_Q]).astype(bf16)
    normed_r = nn(nown[...], pr[...]).astype(bf16)
    rows = tn(pr[...], dw[...].astype(bf16)).astype(bf16)
    raw[...] = tn(normed_r, dq_raw) + nt(rows, sq[:, PAD_Q + 2 * PAD_KV :])
    row = lax.broadcasted_iota(jnp.int32, (16, 128), 0)
    block = jnp.zeros((16, 128), f32)
    for n, values in enumerate((term, gain_grad[...])):
        wide = jnp.concatenate([values, jnp.zeros((1, 64), f32)], axis=1)
        for j in range(5):
            block = jnp.where(row == 4 + n * 5 + j, wide[:, j * 128 : (j + 1) * 128], block)
    for dp in range(N_DP):
        for c in range(N_CTX):
            raw[dp * SLOT_ROWS + 32 : dp * SLOT_ROWS + 48, c * 128 : (c + 1) * 128] += block
    for ref, who in ((keep, core), (give, 1 - core)):
        for zx in range(N_ZX):
            at = pl.multiple_of((2 * zx + who) * SLOT_ROWS, SLOT_ROWS)
            for c in range(N_CTX):
                ref[c * N_ZX + zx] = raw[
                    pl.ds(at, SLOT_ROWS), c * 128 : (c + 1) * 128
                ].astype(bf16)


def input_kernel(dkv, query_part, xown, gain, wkv, middle_grad, out):
    total = dkv[0].astype(f32)
    for c in range(1, N_CTX):
        total = total + dkv[c].astype(f32)
    normed_grad = query_part[...] + nt(total.astype(bf16), wkv[...])
    grad, _ = norm_back(xown[...].astype(f32), gain[...], normed_grad)
    out[...] = middle_grad[...] + grad


def call(kernel, outs, scratch, *args, place=None, flops=0):
    specs = [pl.BlockSpec(memory_space=pltpu.VMEM)] * len(args)
    if place is not None:
        specs = [pl.BlockSpec(memory_space=pltpu.SMEM)] + specs
        args = (place,) + args
    shapes = [jax.ShapeDtypeStruct(s, t) for s, t in outs]
    moved = sum(a.size * a.dtype.itemsize for a in (*args, *shapes))
    return pl.pallas_call(
        kernel,
        out_shape=shapes,
        in_specs=specs,
        out_specs=[pl.BlockSpec(memory_space=pltpu.VMEM)] * len(shapes),
        scratch_shapes=[pltpu.VMEM(s, t) for s, t in scratch],
        compiler_params=pltpu.CompilerParams(vmem_limit_bytes=60 * 1024 * 1024),
        cost_estimate=pl.CostEstimate(flops=flops, bytes_accessed=moved, transcendentals=0),
    )(*args)


def rotary_tables(positions):
    inverse_freq = theta ** (-(jnp.arange(HEAD_DIM // 2, dtype=f32) * 2.0) / HEAD_DIM)
    angles = positions.astype(f32)[:, None] * inverse_freq[None, :]
    rest = jnp.zeros((positions.shape[0], HEAD_DIM), f32)
    cosine, sine = jnp.cos(angles), jnp.sin(angles)
    return (
        jnp.concatenate([cosine, cosine, rest], axis=-1),
        jnp.concatenate([sine, sine, rest], axis=-1),
    )


def placements():
    def ones(rows, columns, wanted):
        return (wanted[:, None] == jnp.arange(columns)[None, :]).astype(bf16)

    feature = jnp.arange(D)
    pr = ones(D, PAD_D, feature // 36 * SLOT_ROWS + feature % 36)
    raw = jnp.arange(RAW)
    c, l = raw // 128, raw % 128
    q = jnp.where(l < 72, c * 72 + l, -1)
    k = jnp.where((l >= 72) & (l < 96), c * 24 + l - 72, -1)
    v = jnp.where((l >= 96) & (l < 120), c * 24 + l - 96, -1)

    def padded(n):
        return jnp.where(n < 0, -1, n // 64 * 128 + n % 64)

    sq = jnp.concatenate(
        [
            ones(RAW, PAD_Q, padded(q)),
            ones(RAW, PAD_KV, padded(k)),
            ones(RAW, PAD_KV, padded(v)),
            ones(RAW, KV, k),
            ones(RAW, KV, v),
        ],
        axis=1,
    )
    so = ones(RAW, D, q)
    head = jnp.arange(PAD_Q)
    n = head // 128 * 64 + head % 128
    po = ones(PAD_Q, PAD_D, jnp.where(head % 128 < 64, n // 36 * SLOT_ROWS + n % 36, -1))
    return pr, sq, so, po


def exchange(slots):
    return lax.all_to_all(slots, EVERY, 0, 0, tiled=True, axis_index_groups=SAME_CORE)


def swap(x):
    return lax.ppermute(x, EVERY, OTHER_CORE)


def pad_rows(x):
    return jnp.pad(x, ((0, SLOT_ROWS - x.shape[0]), (0, 0)))


def body(
    inputs,
    segments,
    cotangent,
    attention_gain,
    query_weight,
    key_weight,
    value_weight,
    out_weight,
    swiglu_gain,
    gate_weight,
    up_weight,
    down_weight,
):
    ctx = lax.axis_index("ctx")
    place = jnp.stack([lax.axis_index("dp") % 2, ctx]).astype(jnp.int32)
    down = down_weight[0]
    gate, up = gate_weight[0], up_weight[0]
    head = jnp.concatenate(
        [
            pad_rows(
                jnp.concatenate(
                    [
                        query_weight[0],
                        key_weight[0],
                        value_weight[0],
                        jnp.zeros((36, 8), bf16),
                        out_weight[0],
                    ],
                    axis=1,
                )
            ),
            down[:48, 64:],
            down[48:, 64:],
            jnp.zeros((48, 40), bf16),
        ],
        axis=1,
    )
    feed = jnp.concatenate(
        [
            pad_rows(
                jnp.concatenate(
                    [gate[:, :128], up[:, :128], gate[:, 128:], up[:, 128:]], axis=1
                )
            ),
            down[:48, :64],
            down[48:, :64],
        ],
        axis=1,
    )
    head_mine = exchange(jnp.broadcast_to(head[None], (SLOTS, SLOT_ROWS, 256)))
    head_other = swap(head_mine)
    feed_mine = exchange(jnp.broadcast_to(feed[None], (SLOTS, SLOT_ROWS, 512)))
    feed_other = swap(feed_mine)

    sent = jnp.concatenate([inputs, segments.astype(bf16)[..., None]], axis=-1)
    came = lax.all_gather(sent, "ctx", axis=1, tiled=True)
    xall = came[..., :D].reshape(ALL, D)
    segk = jnp.broadcast_to(came[..., D:], (BATCH, SEQ, 128)).reshape(ALL, 128)
    xown = inputs.reshape(OWN, D)
    cot = cotangent.reshape(OWN, D)
    cosk, sink = rotary_tables(jnp.arange(SEQ, dtype=jnp.int32))
    cosq, sinq = rotary_tables(ctx * ROWS + jnp.arange(ROWS, dtype=jnp.int32))
    pr, sq, so, po = placements()

    wq, wkv, wo, nall, nown, qs, kp, vp, pt, mixr, middle = call(
        forward_kernel,
        [
            ((D, PAD_Q), bf16),
            ((D, 2 * KV), bf16),
            ((PAD_D, D), bf16),
            ((ALL, D), bf16),
            ((OWN, D), bf16),
            ((PAIRS, STACK, 128), bf16),
            ((PAIRS, SEQ, 128), bf16),
            ((PAIRS, SEQ, 128), bf16),
            ((PAIRS, SEQ, STACK), bf16),
            ((OWN, PAD_D), bf16),
            ((OWN, D), f32),
        ],
        [
            ((PAD_D, RAW), bf16),
            ((PAD_D, RAW), bf16),
            ((D, 2 * PAD_KV), bf16),
            ((D, RAW), bf16),
            ((BATCH, SEQ, ROWS), f32),
            ((OWN, PAD_Q), bf16),
        ],
        head_mine, head_other, xall, xown, attention_gain, segments.astype(f32), segk,
        cosk, sink, cosq, sinq, pr, sq, so, po,
        place=place,
        flops=12 * 10**9,
    )

    result, gs, feed_keep, feed_give, middle_grad, gain_grad = call(
        feed_kernel,
        [
            ((OWN, D), bf16),
            ((PAIRS, STACK, 128), bf16),
            ((SLOTS, SLOT_ROWS, 640), bf16),
            ((SLOTS, SLOT_ROWS, 640), bf16),
            ((OWN, D), f32),
            ((1, D), f32),
        ],
        [
            ((PAD_D, N_CTX * 384), bf16),
            ((FF, RAW), bf16),
            ((PAD_D, 768), bf16),
            ((8, 128), f32),
            ((PAD_D, RAW), f32),
            ((FF, RAW), bf16),
        ],
        feed_mine, feed_other, head_mine, head_other, middle, mixr, cot, swiglu_gain, wo, pr, so, po,
        place=place,
        flops=12 * 10**9,
    )
    feed_sum = (feed_keep.astype(f32) + swap(feed_give).astype(f32)).astype(bf16)
    feed_came = exchange(feed_sum)

    keep, give, dkv, query_part = call(
        backward_kernel,
        [
            ((SLOTS, SLOT_ROWS, 128), bf16),
            ((SLOTS, SLOT_ROWS, 128), bf16),
            ((N_CTX, OWN, 2 * KV), bf16),
            ((OWN, D), f32),
        ],
        [
            ((OWN, PAD_Q), bf16),
            ((PAIRS, SEQ, 128), bf16),
            ((PAIRS, SEQ, 128), bf16),
            ((D, 2 * KV), f32),
            ((PAD_D, RAW), f32),
        ],
        pt, qs, kp, vp, gs, nall, nown, xall, xown, wq, wkv, gain_grad,
        cosk, sink, cosq, sinq, pr, sq,
        place=place,
        flops=12 * 10**9,
    )
    head_came = exchange((keep.astype(f32) + swap(give).astype(f32)).astype(bf16))
    dkv_came = lax.all_to_all(dkv, "ctx", 0, 0, tiled=True)
    (input_grad,) = call(
        input_kernel,
        [((OWN, D), f32)],
        [],
        dkv_came, query_part, xown, attention_gain, wkv, middle_grad,
        flops=10**9,
    )

    qkv = jnp.sum(head_came.astype(f32), axis=0)
    rest = jnp.sum(feed_came.astype(f32), axis=0)
    first_total = qkv[36:41].reshape(1, 640)[:, :D]
    second_total = qkv[41:46].reshape(1, 640)[:, :D]
    gu = rest[:36, 128:512]
    gate_total = jnp.concatenate([gu[:, :128], gu[:, 256:320]], axis=1)
    up_total = jnp.concatenate([gu[:, 128:256], gu[:, 320:]], axis=1)
    down_total = jnp.concatenate(
        [
            jnp.concatenate([rest[:, 512:576], rest[:, 72:80]], axis=1),
            jnp.concatenate([rest[:, 576:640], rest[:, 80:88]], axis=1),
        ],
        axis=0,
    )
    return (
        result.reshape(BATCH, ROWS, D),
        input_grad.reshape(BATCH, ROWS, D),
        first_total,
        qkv[None, :36, :72],
        qkv[None, :36, 72:96],
        qkv[None, :36, 96:120],
        rest[None, :36, :72],
        second_total,
        gate_total[None],
        up_total[None],
        down_total[None],
    )


def solution(mesh):
    weight = P(None, "dp", "ctx")
    rows = P("dp", "ctx", None)
    return jax.shard_map(
        body,
        mesh=mesh,
        in_specs=(rows, P("dp", "ctx"), rows, P(), weight, weight, weight, weight, P(), weight, weight, weight),
        out_specs=(rows, rows, P(), weight, weight, weight, weight, P(), weight, weight, weight),
        check_vma=False,
    )
```

```python
import functools

import jax
import jax.numpy as jnp
from jax import lax
from jax.experimental import pallas as pl
from jax.experimental.pallas import tpu as pltpu
from jax.sharding import PartitionSpec as P

HEADS = 9
KV_HEADS = 3
HEAD_DIM = 64
GROUP = HEADS // KV_HEADS
D = 576
FF = 1536
KV = KV_HEADS * HEAD_DIM
BATCH = 2
ROWS = 128
SEQ = 1024
OWN = BATCH * ROWS
ALL = BATCH * SEQ
N_CTX = 8
N_DP = 16
N_ZX = N_DP // 2
SLOTS = N_CTX * N_ZX
SLOT_ROWS = 48
PAD_D = N_DP * SLOT_ROWS
RAW = N_CTX * 128
PAD_Q = HEADS * 128
STACK = GROUP * ROWS
PAIRS = BATCH * KV_HEADS

eps = 1e-05
theta = 10000.0
masked = -1e30
bf16 = jnp.bfloat16
f32 = jnp.float32

EVERY = ("dp", "ctx")
SAME_CORE = [
    [(zx * 2 + core) * N_CTX + ctx for ctx in range(N_CTX) for zx in range(N_ZX)]
    for core in range(2)
]
OTHER_CORE = [
    (dp * N_CTX + ctx, (dp ^ 1) * N_CTX + ctx) for dp in range(N_DP) for ctx in range(N_CTX)
]


def nn(left, right):
    return jnp.dot(left, right, preferred_element_type=f32)


def tn(left, right):
    return lax.dot_general(left, right, (((0,), (0,)), ((), ())), preferred_element_type=f32)


def nt(left, right):
    return lax.dot_general(left, right, (((1,), (1,)), ((), ())), preferred_element_type=f32)


def halves(x):
    high = x.astype(bf16)
    return high, (x - high.astype(f32)).astype(bf16)


def rho_of(x):
    return lax.rsqrt(jnp.mean(x * x, axis=-1, keepdims=True) + eps)


def norm_back(x, gain, c):
    rho = rho_of(x)
    w = c * gain
    grad = rho * (w - x * (rho * rho * jnp.mean(w * x, axis=-1, keepdims=True)))
    return grad, jnp.sum(c * (x * rho), axis=0, keepdims=True)


def lanes(shape):
    return lax.broadcasted_iota(jnp.int32, shape, 1)


def turn(x, cosine, sine):
    first = lanes(x.shape) % HEAD_DIM < HEAD_DIM // 2
    turned = jnp.where(first, -pltpu.roll(x, 96, 1), pltpu.roll(x, 32, 1))
    return x * cosine + turned * sine


def turn_back(x, cosine, sine):
    first = lanes(x.shape) % HEAD_DIM < HEAD_DIM // 2
    w = x * sine
    turned = jnp.where(first, pltpu.roll(w, 96, 1), -pltpu.roll(w, 32, 1))
    return x * cosine + turned


def triple(x, axis):
    return jnp.concatenate([x] * GROUP, axis=axis)


def slot_row(zx, who):
    return pl.multiple_of((2 * zx + who) * SLOT_ROWS, SLOT_ROWS)


def hidden_place(unit):
    n = unit * 16
    c, m = divmod(n, 192)
    base = (c // 2) * 384
    if m < 128:
        return base + (c % 2) * 128 + m
    return base + 256 + (c % 2) * 64 + (m - 128)


def project_kernel(
    place, mine, other, xown, gain, cosq, sinq, pr, sq,
    wq, wkv, nown, qs, kv, segs,
    raw, wmid,
):
    core, zx_own = place[0], place[2]
    for ref, who in ((mine, core), (other, 1 - core)):
        for zx in range(N_ZX):
            for c in range(N_CTX):
                raw[pl.ds(slot_row(zx, who), SLOT_ROWS), c * 128 : (c + 1) * 128] = ref[
                    c * N_ZX + zx
                ]
    for c in range(N_CTX):
        segs[c] = mine[c * N_ZX + zx_own][32:].astype(f32)
    wmid[...] = nn(pr[...], raw[...]).astype(bf16)
    wkv[...] = nn(wmid[...], sq[:, PAD_Q:]).astype(bf16)
    wq[...] = nn(wmid[...], sq[:, :PAD_Q]).astype(bf16)

    x = xown[...].astype(f32)
    normed = (x * rho_of(x) * gain[...]).astype(bf16)
    nown[...] = normed
    low = lanes((ROWS, 128)) < HEAD_DIM
    pre = nn(normed, wkv[...])
    for b in range(BATCH):
        rows = pre[b * ROWS : (b + 1) * ROWS]
        tile = rows[:, 128:256]
        kv[b * ROWS : (b + 1) * ROWS, :128] = turn(rows[:, :128], cosq[...], sinq[...]).astype(bf16)
        kv[b * ROWS : (b + 1) * ROWS, 128:256] = jnp.where(
            low, turn(tile, cosq[...], sinq[...]), tile
        ).astype(bf16)
        kv[b * ROWS : (b + 1) * ROWS, 256:] = rows[:, 256:].astype(bf16)
    pre = nn(normed, wq[...])
    for head in range(HEADS):
        h, g = divmod(head, GROUP)
        for b in range(BATCH):
            turned = turn(
                pre[b * ROWS : (b + 1) * ROWS, head * 128 : (head + 1) * 128], cosq[...], sinq[...]
            )
            qs[b * KV_HEADS + h, g * ROWS : (g + 1) * ROWS, :] = (
                turned.astype(bf16) * bf16(HEAD_DIM**-0.5)
            )


def unpack_kernel(place, mine, other, so, gu, down, wo, oraw):
    core = place[0]
    lane = lanes((SLOT_ROWS, 128))
    for ref, who in ((mine, core), (other, 1 - core)):
        for zx in range(N_ZX):
            row = slot_row(zx, who)
            for c in range(N_CTX):
                slot = c * N_ZX + zx
                gu[pl.ds(row, SLOT_ROWS), c * 384 : (c + 1) * 384] = ref[slot, :, 128:]
                oraw[pl.ds(row, SLOT_ROWS), c * 128 : (c + 1) * 128] = ref[slot, :, :128]

        def unpack(zx, carry, ref=ref, who=who):
            for c in range(N_CTX):
                tiles = [
                    ref[c * N_ZX + zx, :, j * 128 : (j + 1) * 128].astype(f32) for j in range(4)
                ]
                t = jnp.concatenate([tile[36:] for tile in tiles], axis=0)
                e = jnp.concatenate([tiles[0][:36], pltpu.roll(tiles[0], 112, 1)[:12]], axis=0)
                first = jnp.where(lane < 64, t, jnp.where(lane < 72, pltpu.roll(e, 120, 1), 0.0))
                second = jnp.where(
                    lane < 64,
                    pltpu.roll(t, 64, 1),
                    jnp.where(lane < 72, pltpu.roll(e, 112, 1), 0.0),
                )
                for half, values in enumerate((first, second)):
                    values = values.astype(bf16)
                    for unit in range(3):
                        n = half * 48 + unit * 16
                        at = place_of(2 * zx + who, n)
                        down[pl.ds(at, 16), c * 128 : (c + 1) * 128] = values[
                            unit * 16 : unit * 16 + 16
                        ]
            return carry

        lax.fori_loop(0, N_ZX, unpack, 0)
    wo[...] = nn(oraw[...], so[...]).astype(bf16)


def place_of(dp, n):
    c = dp // 2
    m = (dp - 2 * c) * 96 + n
    odd = c - (c // 2) * 2
    base = (c // 2) * 384
    at = jnp.where(m < 128, base + odd * 128 + m, base + 256 + odd * 64 + (m - 128))
    return pl.multiple_of(at, 16)


def attend_kernel(
    place, kv, qs, segs, segq, xown, po, wo,
    kvs, pt, mixr, middle,
    bias, mixp,
):
    ctx = place[1]
    for b in range(BATCH):
        for c in range(N_CTX):
            kvs[b, c * ROWS : (c + 1) * ROWS, :] = kv[c, b * ROWS : (b + 1) * ROWS, :]
            keys = jnp.broadcast_to(segs[c, 4 + b : 5 + b, :], (ROWS, ROWS)).T
            key_pos = c * ROWS + lax.broadcasted_iota(jnp.int32, (ROWS, ROWS), 0)
            query_pos = ctx * ROWS + lanes((ROWS, ROWS))
            allowed = (keys == segq[b : b + 1, :]) & (key_pos <= query_pos)
            bias[b, c * ROWS : (c + 1) * ROWS, :] = jnp.where(allowed, 0.0, masked)

    def attend(i, carry):
        b = i // KV_HEADS
        h = i - b * KV_HEADS
        keys = kvs[b, :, pl.ds(pl.multiple_of(h // 2 * 128, 128), 128)]
        values = kvs[b, :, pl.ds(pl.multiple_of((h + 3) // 2 * 128, 128), 128)]
        scores = nt(keys, qs[i]) + triple(bias[b], 1)
        top = jnp.max(scores, axis=0, keepdims=True)
        expo = jnp.exp(scores - top)
        total = jnp.sum(expo, axis=0, keepdims=True)
        probs = (expo * (1.0 / total)).astype(bf16)
        pt[i] = probs
        mixed = tn(values, probs).T.astype(bf16)
        for g in range(GROUP):
            mixp[
                pl.ds(pl.multiple_of(b * ROWS, ROWS), ROWS),
                pl.ds(pl.multiple_of((h * GROUP + g) * 128, 128), 128),
            ] = mixed[g * ROWS : (g + 1) * ROWS]
        return carry

    lax.fori_loop(0, PAIRS, attend, 0)
    placed = nn(mixp[...], po[...]).astype(bf16)
    mixr[...] = placed
    middle[...] = xown[...].astype(f32) + nn(placed, wo[...])


def feed_kernel(
    place, gu, down, middle, mixr, cot, gain, wo, pr, so, po,
    result, gs, keep, give, middle_grad, gain_grad,
    dgu, d1, dd,
):
    core = place[0]
    mid = middle[...]
    rho = rho_of(mid)
    second = (mid * rho * gain[...]).astype(bf16)
    second_r = nn(second, pr[...]).astype(bf16)
    e_b = cot[...]
    e_raw = nt(e_b, so[...]).astype(bf16)
    low = lanes((OWN, 128)) < 64
    grad_sum = jnp.zeros((OWN, PAD_D), f32)
    result_sum = jnp.zeros((OWN, RAW), f32)
    for pair in range(N_CTX // 2):
        weight = gu[:, pair * 768 : (pair + 1) * 768]
        pre = nn(second_r, weight)
        a, u, t, a2, u2, t2 = (pre[:, i * 128 : (i + 1) * 128] for i in range(6))
        gate = jnp.concatenate([a, a2, jnp.where(low, t, pltpu.roll(t2, 64, 1))], axis=1)
        up = jnp.concatenate([u, u2, jnp.where(low, pltpu.roll(t, 64, 1), t2)], axis=1)
        logistic = 1.0 / (1.0 + jnp.exp(-gate))
        silu = gate * logistic
        inner = (silu * up).astype(bf16)
        rows = down[pair * 384 : (pair + 1) * 384, :]
        result_sum += nn(inner, rows)
        inner_grad = nt(e_raw, rows)
        gate_grad = inner_grad * up * (logistic * (1.0 + gate * (1.0 - logistic)))
        up_grad = inner_grad * silu
        a, a2, gt = (gate_grad[:, i * 128 : (i + 1) * 128] for i in range(3))
        u, u2, ut = (up_grad[:, i * 128 : (i + 1) * 128] for i in range(3))
        t = jnp.where(low, gt, pltpu.roll(ut, 64, 1))
        t2 = jnp.where(low, pltpu.roll(gt, 64, 1), ut)
        grads = jnp.concatenate([a, u, t, a2, u2, t2], axis=1).astype(bf16)
        grad_sum += nt(grads, weight)
        dgu[:, pair * 768 : (pair + 1) * 768] = tn(second_r, grads).astype(bf16)
        dd_pair = tn(inner, e_raw).astype(bf16)
        for unit in range(pair * 24, pair * 24 + 24):
            at = hidden_place(unit) - pair * 384
            dd[unit * 16 : unit * 16 + 16, :] = dd_pair[at : at + 16, :]

    high, rest = halves(result_sum)
    result[...] = (mid + (nn(high, so[...]) + nn(rest, so[...]))).astype(bf16)
    high, rest = halves(grad_sum)
    second_grad = nt(high, pr[...]) + nt(rest, pr[...])
    norm_grad, gain_term = norm_back(mid, gain[...], second_grad)
    gain_grad[...] = gain_term
    total = e_b.astype(f32) + norm_grad
    middle_grad[...] = total
    middle_b = total.astype(bf16)
    middle_raw = nt(middle_b, so[...]).astype(bf16)
    d1[...] = tn(mixr[...], middle_raw)
    back = nt(nt(middle_b, wo[...]).astype(bf16), po[...]).astype(bf16)
    for head in range(HEADS):
        h, g = divmod(head, GROUP)
        for b in range(BATCH):
            gs[b * KV_HEADS + h, g * ROWS : (g + 1) * ROWS, :] = back[
                b * ROWS : (b + 1) * ROWS, head * 128 : (head + 1) * 128
            ]

    lane = lanes((SLOT_ROWS, 128))
    for ref, who in ((keep, core), (give, 1 - core)):

        def pack(zx, carry, ref=ref, who=who):
            dp = 2 * zx + who
            row = slot_row(zx, who)
            for c in range(N_CTX):
                at = pl.multiple_of(dp * 96, 16)
                first = dd[pl.ds(at, 48), c * 128 : (c + 1) * 128].astype(f32)
                second = dd[pl.ds(at + 48, 48), c * 128 : (c + 1) * 128].astype(f32)
                t = jnp.where(lane < 64, first, pltpu.roll(second, 64, 1))
                own = d1[pl.ds(row, SLOT_ROWS), c * 128 : (c + 1) * 128]
                e = jnp.where(
                    lane < 72,
                    own,
                    jnp.where(lane < 80, pltpu.roll(first, 8, 1), pltpu.roll(second, 16, 1)),
                )
                last = pltpu.roll(e, 16, 1)
                rest = jnp.concatenate([last[36:], last[12:]], axis=0)
                e = jnp.where(lane < 88, e, jnp.where(lane < 104, rest, 0.0))
                ref[c * N_ZX + zx, :, 0:128] = jnp.concatenate([e[:36], t[:12]], axis=0).astype(bf16)
                for j in range(3):
                    g = dgu[
                        pl.ds(row, SLOT_ROWS), c * 384 + j * 128 : c * 384 + (j + 1) * 128
                    ].astype(f32)
                    ref[c * N_ZX + zx, :, 128 + j * 128 : 256 + j * 128] = jnp.concatenate(
                        [g[:36], t[12 * j + 12 : 12 * j + 24]], axis=0
                    ).astype(bf16)
            return carry

        lax.fori_loop(0, N_ZX, pack, 0)


def backward_kernel(
    place, pt, qs, kvs, gs, nown, xall, xown, gain, wq, wkv, gain_grad, cosk, sink, cosq, sinq, pr, sq,
    keep, give, dkv, query_part,
    dqp, dk, dv, dw, raw,
):
    core = place[0]

    def attend(i, carry):
        b = i // KV_HEADS
        h = i - b * KV_HEADS
        keys = kvs[b, :, pl.ds(pl.multiple_of(h // 2 * 128, 128), 128)]
        values = kvs[b, :, pl.ds(pl.multiple_of((h + 3) // 2 * 128, 128), 128)]
        g_b = gs[i]
        probs_b = pt[i]
        probs = probs_b.astype(f32)
        weighted = probs * nt(values, g_b)
        delta = jnp.sum(weighted, axis=0, keepdims=True)
        ds = (weighted - probs * delta).astype(bf16)
        dk[i] = turn_back(nn(ds, qs[i]), cosk[...], sink[...]).astype(bf16)
        dv[i] = nn(probs_b, g_b).astype(bf16)
        dq = tn(keys, ds).T * HEAD_DIM**-0.5
        for g in range(GROUP):
            dqp[
                pl.ds(pl.multiple_of(b * ROWS, ROWS), ROWS),
                pl.ds(pl.multiple_of((h * GROUP + g) * 128, 128), 128),
            ] = turn_back(dq[g * ROWS : (g + 1) * ROWS], cosq[...], sinq[...]).astype(bf16)
        return carry

    lax.fori_loop(0, PAIRS, attend, 0)

    dw[...] = jnp.zeros(dw.shape, f32)
    term = jnp.zeros((1, D), f32)
    for b in range(BATCH):

        def chunk(i, term, b=b):
            at = pl.multiple_of(i * 256, 256)
            k = [dk[b * 3 + h, pl.ds(at, 256), :] for h in range(3)]
            v = [dv[b * 3 + h, pl.ds(at, 256), :] for h in range(3)]
            packed = jnp.concatenate([k[0] + k[1], k[2] + v[0], v[1] + v[2]], axis=1)
            for n in range(2):
                dkv[i * 2 + n, b * ROWS : (b + 1) * ROWS, :] = packed[n * ROWS : (n + 1) * ROWS]
            x = xall[pl.ds(b * SEQ + at, 256), :].astype(f32)
            scaled = x * rho_of(x)
            dw[...] += tn((scaled * gain[...]).astype(bf16), packed)
            part = nt(packed, wkv[...])
            return term + jnp.sum(part * scaled, axis=0, keepdims=True)

        term = lax.fori_loop(0, SEQ // 256, chunk, term)

    dq = dqp[...]
    part = nt(dq, wq[...])
    query_part[...] = part
    x = xown[...].astype(f32)
    term = term + jnp.sum(part * (x * rho_of(x)), axis=0, keepdims=True)

    dq_raw = nt(dq, sq[:, :PAD_Q]).astype(bf16)
    normed_r = nn(nown[...], pr[...]).astype(bf16)
    rows = tn(pr[...], dw[...].astype(bf16)).astype(bf16)
    raw[...] = tn(normed_r, dq_raw) + nt(rows, sq[:, PAD_Q:])
    row = lax.broadcasted_iota(jnp.int32, (16, 128), 0)
    block = jnp.zeros((16, 128), f32)
    for n, values in enumerate((term, gain_grad[...])):
        wide = jnp.concatenate([values, jnp.zeros((1, 64), f32)], axis=1)
        for j in range(5):
            block = jnp.where(row == 4 + n * 5 + j, wide[:, j * 128 : (j + 1) * 128], block)
    for dp in range(N_DP):
        for c in range(N_CTX):
            raw[dp * SLOT_ROWS + 32 : dp * SLOT_ROWS + 48, c * 128 : (c + 1) * 128] += block
    for ref, who in ((keep, core), (give, 1 - core)):
        for zx in range(N_ZX):
            for c in range(N_CTX):
                ref[c * N_ZX + zx] = raw[
                    pl.ds(slot_row(zx, who), SLOT_ROWS), c * 128 : (c + 1) * 128
                ].astype(bf16)


def input_kernel(dkv, query_part, xown, gain, wkv, middle_grad, out):
    total = dkv[0].astype(f32)
    for c in range(1, N_CTX):
        total = total + dkv[c].astype(f32)
    normed_grad = query_part[...] + nt(total.astype(bf16), wkv[...])
    grad, _ = norm_back(xown[...].astype(f32), gain[...], normed_grad)
    out[...] = middle_grad[...] + grad


def call(kernel, outs, scratch, *args, place=None, flops=0):
    specs = [pl.BlockSpec(memory_space=pltpu.VMEM)] * len(args)
    if place is not None:
        specs = [pl.BlockSpec(memory_space=pltpu.SMEM)] + specs
        args = (place,) + args
    shapes = [jax.ShapeDtypeStruct(s, t) for s, t in outs]
    moved = sum(a.size * a.dtype.itemsize for a in (*args, *shapes))
    return pl.pallas_call(
        kernel,
        out_shape=shapes,
        in_specs=specs,
        out_specs=[pl.BlockSpec(memory_space=pltpu.VMEM)] * len(shapes),
        scratch_shapes=[pltpu.VMEM(s, t) for s, t in scratch],
        compiler_params=pltpu.CompilerParams(vmem_limit_bytes=60 * 1024 * 1024),
        cost_estimate=pl.CostEstimate(flops=flops, bytes_accessed=moved, transcendentals=0),
    )(*args)


def rotary_tables(positions):
    inverse_freq = theta ** (-(jnp.arange(HEAD_DIM // 2, dtype=f32) * 2.0) / HEAD_DIM)
    angles = positions.astype(f32)[:, None] * inverse_freq[None, :]
    return (
        jnp.concatenate([jnp.cos(angles)] * 4, axis=-1),
        jnp.concatenate([jnp.sin(angles)] * 4, axis=-1),
    )


def placements():
    def ones(rows, columns, wanted):
        return (wanted[:, None] == jnp.arange(columns)[None, :]).astype(bf16)

    feature = jnp.arange(D)
    pr = ones(D, PAD_D, feature // 36 * SLOT_ROWS + feature % 36)
    raw = jnp.arange(RAW)
    c, l = raw // 128, raw % 128
    q = jnp.where(l < 72, c * 72 + l, -1)
    k = jnp.where((l >= 72) & (l < 96), c * 24 + l - 72, -1)
    v = jnp.where((l >= 96) & (l < 120), c * 24 + l - 96, -1)
    head = q // HEAD_DIM
    upper = head // GROUP % 2
    padded = jnp.where(q < 0, -1, head * 128 + upper * HEAD_DIM + q % HEAD_DIM)
    sq = jnp.concatenate(
        [ones(RAW, PAD_Q, padded), ones(RAW, KV, k), ones(RAW, KV, v)], axis=1
    )
    so = ones(RAW, D, q)
    place = jnp.arange(PAD_Q)
    head, l = place // 128, place % 128
    upper = 1 - head // GROUP % 2
    inside = l // HEAD_DIM == upper
    n = head * HEAD_DIM + l % HEAD_DIM
    po = ones(PAD_Q, PAD_D, jnp.where(inside, n // 36 * SLOT_ROWS + n % 36, -1))
    return pr, sq, so, po


def exchange(slots):
    return lax.all_to_all(slots, EVERY, 0, 0, tiled=True, axis_index_groups=SAME_CORE)


def swap(x):
    return lax.ppermute(x, EVERY, OTHER_CORE)


def pad_rows(x):
    return jnp.pad(x, ((0, SLOT_ROWS - x.shape[0]), (0, 0)))


def body(
    inputs,
    segments,
    cotangent,
    attention_gain,
    query_weight,
    key_weight,
    value_weight,
    out_weight,
    swiglu_gain,
    gate_weight,
    up_weight,
    down_weight,
):
    ctx, dp = lax.axis_index("ctx"), lax.axis_index("dp")
    place = jnp.stack([dp % 2, ctx, dp // 2]).astype(jnp.int32)
    down = down_weight[0]
    gate, up = gate_weight[0], up_weight[0]
    zero = functools.partial(jnp.zeros, dtype=bf16)
    head = jnp.concatenate(
        [
            jnp.concatenate([query_weight[0], key_weight[0], value_weight[0], zero((36, 8))], axis=1),
            segments.astype(bf16),
            zero((10, 128)),
        ],
        axis=0,
    )
    head_mine = exchange(jnp.broadcast_to(head[None], (SLOTS, SLOT_ROWS, 128)))
    main = jnp.concatenate([down[:48, :64], down[48:, :64]], axis=1)
    extra = jnp.concatenate([down[:48, 64:], down[48:, 64:]], axis=1)
    feed = jnp.concatenate(
        [
            jnp.concatenate(
                [
                    out_weight[0],
                    extra[:36],
                    jnp.concatenate([extra[36:], zero((24, 16))], axis=0),
                    zero((36, 24)),
                    gate[:, :128],
                    up[:, :128],
                    gate[:, 128:],
                    up[:, 128:],
                ],
                axis=1,
            ),
            jnp.concatenate([main[12 * j : 12 * j + 12] for j in range(4)], axis=1),
        ],
        axis=0,
    )
    feed, head_mine = lax.optimization_barrier((feed, head_mine))
    head_other = swap(head_mine)
    feed_mine = exchange(jnp.broadcast_to(feed[None], (SLOTS, SLOT_ROWS, 512)))

    xown = inputs.reshape(OWN, D)
    cot = cotangent.reshape(OWN, D)
    cosk, sink = rotary_tables(jnp.arange(SEQ, dtype=jnp.int32))
    cosq, sinq = rotary_tables(ctx * ROWS + jnp.arange(ROWS, dtype=jnp.int32))
    pr, sq, so, po = placements()

    wq, wkv, nown, qs, kv, segs = call(
        project_kernel,
        [
            ((D, PAD_Q), bf16),
            ((D, 2 * KV), bf16),
            ((OWN, D), bf16),
            ((PAIRS, STACK, 128), bf16),
            ((OWN, 2 * KV), bf16),
            ((N_CTX, 16, 128), f32),
        ],
        [((PAD_D, RAW), bf16), ((D, RAW), bf16)],
        head_mine, head_other, xown, attention_gain, cosq, sinq, pr, sq,
        place=place,
        flops=10 * 10**9,
    )
    kv, feed_mine = lax.optimization_barrier((kv, feed_mine))
    feed_other = swap(feed_mine)
    kv_all = lax.all_to_all(
        jnp.broadcast_to(kv[None], (N_CTX, OWN, 2 * KV)), "ctx", 0, 0, tiled=True
    )
    gu, down_raw, wo = call(
        unpack_kernel,
        [((PAD_D, N_CTX * 384), bf16), ((FF, RAW), bf16), ((PAD_D, D), bf16)],
        [((PAD_D, RAW), bf16)],
        feed_mine, feed_other, so,
        place=place,
        flops=12 * 10**9,
    )
    late, kv_all = lax.optimization_barrier((inputs, kv_all))
    xall = lax.all_gather(late, "ctx", axis=1, tiled=True).reshape(ALL, D)

    kvs, pt, mixr, middle = call(
        attend_kernel,
        [
            ((BATCH, SEQ, 2 * KV), bf16),
            ((PAIRS, SEQ, STACK), bf16),
            ((OWN, PAD_D), bf16),
            ((OWN, D), f32),
        ],
        [((BATCH, SEQ, ROWS), f32), ((OWN, PAD_Q), bf16)],
        kv_all, qs, segs, segments.astype(f32), xown, po, wo,
        place=place,
        flops=12 * 10**9,
    )

    result, gs, feed_keep, feed_give, middle_grad, gain_grad = call(
        feed_kernel,
        [
            ((OWN, D), bf16),
            ((PAIRS, STACK, 128), bf16),
            ((SLOTS, SLOT_ROWS, 512), bf16),
            ((SLOTS, SLOT_ROWS, 512), bf16),
            ((OWN, D), f32),
            ((1, D), f32),
        ],
        [((PAD_D, N_CTX * 384), bf16), ((PAD_D, RAW), f32), ((FF, RAW), bf16)],
        gu, down_raw, middle, mixr, cot, swiglu_gain, wo, pr, so, po,
        place=place,
        flops=20 * 10**9,
    )
    feed_sum = (feed_keep.astype(f32) + swap(feed_give).astype(f32)).astype(bf16)
    feed_sum, gs = lax.optimization_barrier((feed_sum, gs))
    feed_came = exchange(feed_sum)

    keep, give, dkv, query_part = call(
        backward_kernel,
        [
            ((SLOTS, SLOT_ROWS, 128), bf16),
            ((SLOTS, SLOT_ROWS, 128), bf16),
            ((N_CTX, OWN, 2 * KV), bf16),
            ((OWN, D), f32),
        ],
        [
            ((OWN, PAD_Q), bf16),
            ((PAIRS, SEQ, 128), bf16),
            ((PAIRS, SEQ, 128), bf16),
            ((D, 2 * KV), f32),
            ((PAD_D, RAW), f32),
        ],
        pt, qs, kvs, gs, nown, xall, xown, attention_gain, wq, wkv, gain_grad,
        cosk, sink, cosq, sinq, pr, sq,
        place=place,
        flops=25 * 10**9,
    )
    dkv, give, feed_came = lax.optimization_barrier((dkv, give, feed_came))
    dkv_came = lax.all_to_all(dkv, "ctx", 0, 0, tiled=True)
    head_sum = (keep.astype(f32) + swap(give).astype(f32)).astype(bf16)
    head_sum, dkv_came = lax.optimization_barrier((head_sum, dkv_came))
    head_came = exchange(head_sum)
    (input_grad,) = call(
        input_kernel,
        [((OWN, D), f32)],
        [],
        dkv_came, query_part, xown, attention_gain, wkv, middle_grad,
        flops=10**9,
    )

    qkv = jnp.sum(head_came.astype(f32), axis=0)
    rest = jnp.sum(feed_came.astype(f32), axis=0)
    first_total = qkv[36:41].reshape(1, 640)[:, :D]
    second_total = qkv[41:46].reshape(1, 640)[:, :D]
    gu = rest[:36, 128:]
    gate_total = jnp.concatenate([gu[:, :128], gu[:, 256:320]], axis=1)
    up_total = jnp.concatenate([gu[:, 128:256], gu[:, 320:]], axis=1)
    main = jnp.concatenate([rest[36:, j * 128 : (j + 1) * 128] for j in range(4)], axis=0)
    extra = jnp.concatenate([rest[:36, 72:88], rest[:12, 88:104]], axis=0)
    down_total = jnp.concatenate(
        [
            jnp.concatenate([main[:, :64], extra[:, :8]], axis=1),
            jnp.concatenate([main[:, 64:], extra[:, 8:]], axis=1),
        ],
        axis=0,
    )
    return (
        result.reshape(BATCH, ROWS, D),
        input_grad.reshape(BATCH, ROWS, D),
        first_total,
        qkv[None, :36, :72],
        qkv[None, :36, 72:96],
        qkv[None, :36, 96:120],
        rest[None, :36, :72],
        second_total,
        gate_total[None],
        up_total[None],
        down_total[None],
    )


def solution(mesh):
    weight = P(None, "dp", "ctx")
    rows = P("dp", "ctx", None)
    return jax.shard_map(
        body,
        mesh=mesh,
        in_specs=(rows, P("dp", "ctx"), rows, P(), weight, weight, weight, weight, P(), weight, weight, weight),
        out_specs=(rows, rows, P(), weight, weight, weight, weight, P(), weight, weight, weight),
        check_vma=False,
    )
```

```python
import functools

import jax
import jax.numpy as jnp
from jax import lax
from jax.experimental import pallas as pl
from jax.experimental.pallas import tpu as pltpu
from jax.sharding import PartitionSpec as P

HEADS = 9
KV_HEADS = 3
HEAD_DIM = 64
GROUP = HEADS // KV_HEADS
D = 576
FF = 1536
KV = KV_HEADS * HEAD_DIM
BATCH = 2
ROWS = 128
SEQ = 1024
OWN = BATCH * ROWS
ALL = BATCH * SEQ
N_CTX = 8
N_DP = 16
N_ZX = N_DP // 2
SLOTS = N_CTX * N_ZX
SLOT_ROWS = 48
HALF = N_ZX * SLOT_ROWS
PAD_D = 2 * HALF
RAW = N_CTX * 128
PAD_Q = HEADS * 128
STACK = GROUP * ROWS
PAIRS = BATCH * KV_HEADS

eps = 1e-05
theta = 10000.0
masked = -1e30
bf16 = jnp.bfloat16
f32 = jnp.float32

EVERY = ("dp", "ctx")
SAME_CORE = [
    [(zx * 2 + core) * N_CTX + ctx for ctx in range(N_CTX) for zx in range(N_ZX)]
    for core in range(2)
]
OTHER_CORE = [
    (dp * N_CTX + ctx, (dp ^ 1) * N_CTX + ctx) for dp in range(N_DP) for ctx in range(N_CTX)
]


def nn(left, right):
    return jnp.dot(left, right, preferred_element_type=f32)


def tn(left, right):
    return lax.dot_general(left, right, (((0,), (0,)), ((), ())), preferred_element_type=f32)


def nt(left, right):
    return lax.dot_general(left, right, (((1,), (1,)), ((), ())), preferred_element_type=f32)


def halves(x):
    high = x.astype(bf16)
    return high, (x - high.astype(f32)).astype(bf16)


def rho_of(x):
    return lax.rsqrt(jnp.mean(x * x, axis=-1, keepdims=True) + eps)


def norm_back(x, gain, c):
    rho = rho_of(x)
    w = c * gain
    grad = rho * (w - x * (rho * rho * jnp.mean(w * x, axis=-1, keepdims=True)))
    return grad, jnp.sum(c * (x * rho), axis=0, keepdims=True)


def lanes(shape):
    return lax.broadcasted_iota(jnp.int32, shape, 1)


def turn(x, cosine, sine):
    first = lanes(x.shape) % HEAD_DIM < HEAD_DIM // 2
    turned = jnp.where(first, -pltpu.roll(x, 96, 1), pltpu.roll(x, 32, 1))
    return x * cosine + turned * sine


def turn_back(x, cosine, sine):
    first = lanes(x.shape) % HEAD_DIM < HEAD_DIM // 2
    w = x * sine
    turned = jnp.where(first, pltpu.roll(w, 96, 1), -pltpu.roll(w, 32, 1))
    return x * cosine + turned


def triple(x, axis):
    return jnp.concatenate([x] * GROUP, axis=axis)


def block(ref, c, start, width):
    return ref[c * N_ZX : (c + 1) * N_ZX, :, start : start + width].reshape(HALF, width)


def hidden_place(unit):
    n = unit * 16
    c, m = divmod(n, 192)
    base = (c // 2) * 384
    if m < 128:
        return base + (c % 2) * 128 + m
    return base + 256 + (c % 2) * 64 + (m - 128)


def project_kernel(
    place, mine, other, xown, gain, cosq, sinq, pr, sq,
    wq, wkv, nown, qs, kv, segs,
    raw, wmid,
):
    zx_own = place[2]
    for c in range(N_CTX):
        raw[:HALF, c * 128 : (c + 1) * 128] = block(mine, c, 0, 128)
        raw[HALF:, c * 128 : (c + 1) * 128] = block(other, c, 0, 128)
        segs[c] = mine[c * N_ZX + zx_own][32:].astype(f32)
    wmid[...] = nn(pr[...], raw[...]).astype(bf16)
    wkv[...] = nn(wmid[...], sq[:, PAD_Q:]).astype(bf16)
    wq[...] = nn(wmid[...], sq[:, :PAD_Q]).astype(bf16)

    x = xown[...].astype(f32)
    normed = (x * rho_of(x) * gain[...]).astype(bf16)
    nown[...] = normed
    low = lanes((ROWS, 128)) < HEAD_DIM
    pre = nn(normed, wkv[...])
    for b in range(BATCH):
        rows = pre[b * ROWS : (b + 1) * ROWS]
        tile = rows[:, 128:256]
        kv[b * ROWS : (b + 1) * ROWS, :128] = turn(rows[:, :128], cosq[...], sinq[...]).astype(bf16)
        kv[b * ROWS : (b + 1) * ROWS, 128:256] = jnp.where(
            low, turn(tile, cosq[...], sinq[...]), tile
        ).astype(bf16)
        kv[b * ROWS : (b + 1) * ROWS, 256:] = rows[:, 256:].astype(bf16)
    pre = nn(normed, wq[...])
    for head in range(HEADS):
        h, g = divmod(head, GROUP)
        for b in range(BATCH):
            turned = turn(
                pre[b * ROWS : (b + 1) * ROWS, head * 128 : (head + 1) * 128], cosq[...], sinq[...]
            )
            qs[b * KV_HEADS + h, g * ROWS : (g + 1) * ROWS, :] = (
                turned.astype(bf16) * bf16(HEAD_DIM**-0.5)
            )


def unpack_kernel(place, mine, other, so, down, wo, oraw):
    core = place[0]
    lane = lanes((SLOT_ROWS, 128))
    for who, ref in enumerate((mine, other)):
        for c in range(N_CTX):
            oraw[who * HALF : (who + 1) * HALF, c * 128 : (c + 1) * 128] = block(ref, c, 0, 128)

        def unpack(zx, carry, ref=ref, who=who):
            for c in range(N_CTX):
                o = ref[c * N_ZX + zx, :, :128].astype(f32)
                t = jnp.concatenate(
                    [o[36:]]
                    + [
                        ref[c * N_ZX + zx, 32:, j * 128 : (j + 1) * 128].astype(f32)[4:]
                        for j in range(1, 4)
                    ],
                    axis=0,
                )
                e = jnp.concatenate([o[:36], pltpu.roll(o[:16], 112, 1)[:12]], axis=0)
                first = jnp.where(lane < 64, t, jnp.where(lane < 72, pltpu.roll(e, 120, 1), 0.0))
                second = jnp.where(
                    lane < 64,
                    pltpu.roll(t, 64, 1),
                    jnp.where(lane < 72, pltpu.roll(e, 112, 1), 0.0),
                )
                for half, values in enumerate((first, second)):
                    values = values.astype(bf16)
                    for unit in range(3):
                        at = place_of(zx, who ^ core, half * 48 + unit * 16)
                        down[pl.ds(at, 16), c * 128 : (c + 1) * 128] = values[
                            unit * 16 : unit * 16 + 16
                        ]
            return carry

        lax.fori_loop(0, N_ZX, unpack, 0)
    wo[...] = nn(oraw[...], so[...]).astype(bf16)


def place_of(c, odd_dp, n):
    m = odd_dp * 96 + n
    odd = c - (c // 2) * 2
    base = (c // 2) * 384
    at = jnp.where(m < 128, base + odd * 128 + m, base + 256 + odd * 64 + (m - 128))
    return pl.multiple_of(at, 16)


def attend_kernel(
    place, kv, qs, segs, segq, xown, po, wo,
    kvs, pt, mixr, middle,
    bias, mixp,
):
    ctx = place[1]
    for b in range(BATCH):
        for c in range(N_CTX):
            kvs[b, c * ROWS : (c + 1) * ROWS, :] = kv[c, b * ROWS : (b + 1) * ROWS, :]
            keys = jnp.broadcast_to(segs[c, 4 + b : 5 + b, :], (ROWS, ROWS)).T
            key_pos = c * ROWS + lax.broadcasted_iota(jnp.int32, (ROWS, ROWS), 0)
            query_pos = ctx * ROWS + lanes((ROWS, ROWS))
            allowed = (keys == segq[b : b + 1, :]) & (key_pos <= query_pos)
            bias[b, c * ROWS : (c + 1) * ROWS, :] = jnp.where(allowed, 0.0, masked)

    def attend(i, carry):
        b = i // KV_HEADS
        h = i - b * KV_HEADS
        keys = kvs[b, :, pl.ds(pl.multiple_of(h // 2 * 128, 128), 128)]
        values = kvs[b, :, pl.ds(pl.multiple_of((h + 3) // 2 * 128, 128), 128)]
        scores = nt(keys, qs[i]) + triple(bias[b], 1)
        top = jnp.max(scores, axis=0, keepdims=True)
        expo = jnp.exp(scores - top)
        total = jnp.sum(expo, axis=0, keepdims=True)
        probs = (expo * (1.0 / total)).astype(bf16)
        pt[i] = probs
        mixed = tn(values, probs).T.astype(bf16)
        for g in range(GROUP):
            mixp[
                pl.ds(pl.multiple_of(b * ROWS, ROWS), ROWS),
                pl.ds(pl.multiple_of((h * GROUP + g) * 128, 128), 128),
            ] = mixed[g * ROWS : (g + 1) * ROWS]
        return carry

    lax.fori_loop(0, PAIRS, attend, 0)
    placed = nn(mixp[...], po[...]).astype(bf16)
    mixr[...] = placed
    middle[...] = xown[...].astype(f32) + nn(placed, wo[...])


def feed_kernel(
    place, mine, other, down, middle, mixr, cot, gain, wo, pr, so, po,
    result, gs, keep, give, middle_grad, gain_grad,
    d1, dd,
):
    core = place[0]
    mid = middle[...]
    rho = rho_of(mid)
    second = (mid * rho * gain[...]).astype(bf16)
    second_r = nn(second, pr[...]).astype(bf16)
    e_b = cot[...]
    e_raw = nt(e_b, so[...]).astype(bf16)
    low = lanes((OWN, 128)) < 64
    grad_sum = jnp.zeros((OWN, PAD_D), f32)
    result_sum = jnp.zeros((OWN, RAW), f32)
    for pair in range(N_CTX // 2):
        weights = [
            jnp.concatenate([block(ref, c, 128, 384) for ref in (mine, other)], axis=0)
            for c in (2 * pair, 2 * pair + 1)
        ]
        pre = [nn(second_r, weight) for weight in weights]
        a, u, t, a2, u2, t2 = (pre[i // 3][:, i % 3 * 128 : (i % 3 + 1) * 128] for i in range(6))
        gate = jnp.concatenate([a, a2, jnp.where(low, t, pltpu.roll(t2, 64, 1))], axis=1)
        up = jnp.concatenate([u, u2, jnp.where(low, pltpu.roll(t, 64, 1), t2)], axis=1)
        logistic = 1.0 / (1.0 + jnp.exp(-gate))
        silu = gate * logistic
        inner = (silu * up).astype(bf16)
        rows = down[pair * 384 : (pair + 1) * 384, :]
        result_sum += nn(inner, rows)
        inner_grad = nt(e_raw, rows)
        gate_grad = inner_grad * up * (logistic * (1.0 + gate * (1.0 - logistic)))
        up_grad = inner_grad * silu
        a, a2, gt = (gate_grad[:, i * 128 : (i + 1) * 128] for i in range(3))
        u, u2, ut = (up_grad[:, i * 128 : (i + 1) * 128] for i in range(3))
        t = jnp.where(low, gt, pltpu.roll(ut, 64, 1))
        t2 = jnp.where(low, pltpu.roll(gt, 64, 1), ut)
        for k, tiles in enumerate(((a, u, t), (a2, u2, t2))):
            grads = jnp.concatenate(tiles, axis=1).astype(bf16)
            grad_sum += nt(grads, weights[k])
            terms = tn(second_r, grads).astype(bf16)
            c = 2 * pair + k
            for ref, part in ((keep, terms[:HALF]), (give, terms[HALF:])):
                ref[c * N_ZX : (c + 1) * N_ZX, :, 128:] = part.reshape(N_ZX, SLOT_ROWS, 384)
        dd_pair = tn(inner, e_raw).astype(bf16)
        for unit in range(pair * 24, pair * 24 + 24):
            at = hidden_place(unit) - pair * 384
            dd[unit * 16 : unit * 16 + 16, :] = dd_pair[at : at + 16, :]

    high, rest = halves(result_sum)
    result[...] = (mid + (nn(high, so[...]) + nn(rest, so[...]))).astype(bf16)
    high, rest = halves(grad_sum)
    second_grad = nt(high, pr[...]) + nt(rest, pr[...])
    norm_grad, gain_term = norm_back(mid, gain[...], second_grad)
    gain_grad[...] = gain_term
    total = e_b.astype(f32) + norm_grad
    middle_grad[...] = total
    middle_b = total.astype(bf16)
    middle_raw = nt(middle_b, so[...]).astype(bf16)
    d1[...] = tn(mixr[...], middle_raw)
    back = nt(nt(middle_b, wo[...]).astype(bf16), po[...]).astype(bf16)
    for head in range(HEADS):
        h, g = divmod(head, GROUP)
        for b in range(BATCH):
            gs[b * KV_HEADS + h, g * ROWS : (g + 1) * ROWS, :] = back[
                b * ROWS : (b + 1) * ROWS, head * 128 : (head + 1) * 128
            ]

    lane = lanes((SLOT_ROWS, 128))
    for who, ref in enumerate((keep, give)):

        def pack(zx, carry, ref=ref, who=who):
            row = pl.multiple_of(who * HALF + zx * SLOT_ROWS, SLOT_ROWS)
            at = pl.multiple_of((2 * zx + (who ^ core)) * 96, 16)
            for c in range(N_CTX):
                slot = c * N_ZX + zx
                first = dd[pl.ds(at, 48), c * 128 : (c + 1) * 128].astype(f32)
                second = dd[pl.ds(at + 48, 48), c * 128 : (c + 1) * 128].astype(f32)
                t = jnp.where(lane < 64, first, pltpu.roll(second, 64, 1))
                own = d1[pl.ds(row, SLOT_ROWS), c * 128 : (c + 1) * 128]
                e = jnp.where(
                    lane < 72,
                    own,
                    jnp.where(lane < 80, pltpu.roll(first, 8, 1), pltpu.roll(second, 16, 1)),
                )
                rest = pltpu.roll(e[32:], 16, 1)[4:]
                head = jnp.concatenate([rest, e[12:36]], axis=0)
                head = jnp.where(lane[:36] < 88, e[:36], jnp.where(lane[:36] < 104, head, 0.0))
                ref[slot, :, 0:128] = jnp.concatenate([head, t[:12]], axis=0).astype(bf16)
                for j in range(1, 4):
                    g = ref[slot, 32:, j * 128 : (j + 1) * 128].astype(f32)
                    ref[slot, 32:, j * 128 : (j + 1) * 128] = jnp.concatenate(
                        [g[:4], t[12 * j : 12 * j + 12]], axis=0
                    ).astype(bf16)
            return carry

        lax.fori_loop(0, N_ZX, pack, 0)


def backward_kernel(
    pt, qs, kvs, gs, nown, xall, xown, gain, wq, wkv, gain_grad, cosk, sink, cosq, sinq, pr, sq,
    keep, give, dkv, query_part,
    dqp, dk, dv, dw, raw,
):
    def attend(i, carry):
        b = i // KV_HEADS
        h = i - b * KV_HEADS
        keys = kvs[b, :, pl.ds(pl.multiple_of(h // 2 * 128, 128), 128)]
        values = kvs[b, :, pl.ds(pl.multiple_of((h + 3) // 2 * 128, 128), 128)]
        g_b = gs[i]
        probs_b = pt[i]
        probs = probs_b.astype(f32)
        weighted = probs * nt(values, g_b)
        delta = jnp.sum(weighted, axis=0, keepdims=True)
        ds = (weighted - probs * delta).astype(bf16)
        dk[i] = turn_back(nn(ds, qs[i]), cosk[...], sink[...]).astype(bf16)
        dv[i] = nn(probs_b, g_b).astype(bf16)
        dq = tn(keys, ds).T * HEAD_DIM**-0.5
        for g in range(GROUP):
            dqp[
                pl.ds(pl.multiple_of(b * ROWS, ROWS), ROWS),
                pl.ds(pl.multiple_of((h * GROUP + g) * 128, 128), 128),
            ] = turn_back(dq[g * ROWS : (g + 1) * ROWS], cosq[...], sinq[...]).astype(bf16)
        return carry

    lax.fori_loop(0, PAIRS, attend, 0)

    dw[...] = jnp.zeros(dw.shape, f32)

    def chunk(c, term):
        at = pl.multiple_of(c * ROWS, ROWS)
        for b in range(BATCH):
            k = [dk[b * 3 + h, pl.ds(at, ROWS), :] for h in range(3)]
            v = [dv[b * 3 + h, pl.ds(at, ROWS), :] for h in range(3)]
            dkv[c, b * ROWS : (b + 1) * ROWS, :] = jnp.concatenate(
                [k[0] + k[1], k[2] + v[0], v[1] + v[2]], axis=1
            )
        packed = dkv[c]
        x = xall[c].astype(f32)
        scaled = x * rho_of(x)
        dw[...] += tn((scaled * gain[...]).astype(bf16), packed)
        part = nt(packed, wkv[...])
        return term + jnp.sum(part * scaled, axis=0, keepdims=True)

    term = lax.fori_loop(0, N_CTX, chunk, jnp.zeros((1, D), f32))

    dq = dqp[...]
    part = nt(dq, wq[...])
    query_part[...] = part
    x = xown[...].astype(f32)
    term = term + jnp.sum(part * (x * rho_of(x)), axis=0, keepdims=True)

    dq_raw = nt(dq, sq[:, :PAD_Q]).astype(bf16)
    normed_r = nn(nown[...], pr[...]).astype(bf16)
    rows = tn(pr[...], dw[...].astype(bf16)).astype(bf16)
    raw[...] = tn(normed_r, dq_raw) + nt(rows, sq[:, PAD_Q:])
    row = lax.broadcasted_iota(jnp.int32, (16, 128), 0)
    ends = jnp.zeros((16, 128), f32)
    for n, values in enumerate((term, gain_grad[...])):
        wide = jnp.concatenate([values, jnp.zeros((1, 64), f32)], axis=1)
        for j in range(5):
            ends = jnp.where(row == 4 + n * 5 + j, wide[:, j * 128 : (j + 1) * 128], ends)
    for who, ref in enumerate((keep, give)):
        for zx in range(N_ZX):
            row = who * HALF + zx * SLOT_ROWS
            for c in range(N_CTX):
                values = raw[row : row + SLOT_ROWS, c * 128 : (c + 1) * 128]
                ref[c * N_ZX + zx] = jnp.concatenate(
                    [values[:32], values[32:] + ends], axis=0
                ).astype(bf16)


def input_kernel(dkv, query_part, xown, gain, wkv, middle_grad, out):
    total = dkv[0].astype(f32)
    for c in range(1, N_CTX):
        total = total + dkv[c].astype(f32)
    normed_grad = query_part[...] + nt(total.astype(bf16), wkv[...])
    grad, _ = norm_back(xown[...].astype(f32), gain[...], normed_grad)
    out[...] = middle_grad[...] + grad


def call(kernel, outs, scratch, *args, place=None):
    specs = [pl.BlockSpec(memory_space=pltpu.VMEM)] * len(args)
    if place is not None:
        specs = [pl.BlockSpec(memory_space=pltpu.SMEM)] + specs
        args = (place,) + args
    shapes = [jax.ShapeDtypeStruct(s, t) for s, t in outs]
    return pl.pallas_call(
        kernel,
        out_shape=shapes,
        in_specs=specs,
        out_specs=[pl.BlockSpec(memory_space=pltpu.VMEM)] * len(shapes),
        scratch_shapes=[pltpu.VMEM(s, t) for s, t in scratch],
        compiler_params=pltpu.CompilerParams(vmem_limit_bytes=60 * 1024 * 1024),
        cost_estimate=pl.CostEstimate(flops=1, bytes_accessed=1, transcendentals=0),
    )(*args)


def rotary_tables(positions):
    inverse_freq = theta ** (-(jnp.arange(HEAD_DIM // 2, dtype=f32) * 2.0) / HEAD_DIM)
    angles = positions.astype(f32)[:, None] * inverse_freq[None, :]
    return (
        jnp.concatenate([jnp.cos(angles)] * 4, axis=-1),
        jnp.concatenate([jnp.sin(angles)] * 4, axis=-1),
    )


def placements(core):
    def ones(rows, columns, wanted):
        return (wanted[:, None] == jnp.arange(columns)[None, :]).astype(bf16)

    def row(n):
        dp = n // 36
        return (dp % 2 ^ core) * HALF + dp // 2 * SLOT_ROWS + n % 36

    pr = ones(D, PAD_D, row(jnp.arange(D)))
    raw = jnp.arange(RAW)
    c, l = raw // 128, raw % 128
    q = jnp.where(l < 72, c * 72 + l, -1)
    k = jnp.where((l >= 72) & (l < 96), c * 24 + l - 72, -1)
    v = jnp.where((l >= 96) & (l < 120), c * 24 + l - 96, -1)
    head = q // HEAD_DIM
    upper = head // GROUP % 2
    padded = jnp.where(q < 0, -1, head * 128 + upper * HEAD_DIM + q % HEAD_DIM)
    sq = jnp.concatenate(
        [ones(RAW, PAD_Q, padded), ones(RAW, KV, k), ones(RAW, KV, v)], axis=1
    )
    so = ones(RAW, D, q)
    place = jnp.arange(PAD_Q)
    head, l = place // 128, place % 128
    upper = 1 - head // GROUP % 2
    inside = l // HEAD_DIM == upper
    n = head * HEAD_DIM + l % HEAD_DIM
    po = ones(PAD_Q, PAD_D, jnp.where(inside, row(n), -1))
    return pr, sq, so, po


def exchange(slots):
    return lax.all_to_all(slots, EVERY, 0, 0, tiled=True, axis_index_groups=SAME_CORE)


def swap(x):
    return lax.ppermute(x, EVERY, OTHER_CORE)


def pad_rows(x):
    return jnp.pad(x, ((0, SLOT_ROWS - x.shape[0]), (0, 0)))


def body(
    inputs,
    segments,
    cotangent,
    attention_gain,
    query_weight,
    key_weight,
    value_weight,
    out_weight,
    swiglu_gain,
    gate_weight,
    up_weight,
    down_weight,
):
    ctx, dp = lax.axis_index("ctx"), lax.axis_index("dp")
    place = jnp.stack([dp % 2, ctx, dp // 2]).astype(jnp.int32)
    down = down_weight[0]
    gate, up = gate_weight[0], up_weight[0]
    zero = functools.partial(jnp.zeros, dtype=bf16)
    head = jnp.concatenate(
        [
            jnp.concatenate([query_weight[0], key_weight[0], value_weight[0], zero((36, 8))], axis=1),
            segments.astype(bf16),
            zero((10, 128)),
        ],
        axis=0,
    )
    head_mine = exchange(jnp.broadcast_to(head[None], (SLOTS, SLOT_ROWS, 128)))
    main = jnp.concatenate([down[:48, :64], down[48:, :64]], axis=1)
    extra = jnp.concatenate([down[:48, 64:], down[48:, 64:]], axis=1)
    feed = jnp.concatenate(
        [
            jnp.concatenate(
                [
                    out_weight[0],
                    extra[:36],
                    jnp.concatenate([extra[36:], zero((24, 16))], axis=0),
                    zero((36, 24)),
                    gate[:, :128],
                    up[:, :128],
                    gate[:, 128:],
                    up[:, 128:],
                ],
                axis=1,
            ),
            jnp.concatenate([main[12 * j : 12 * j + 12] for j in range(4)], axis=1),
        ],
        axis=0,
    )
    feed, head_mine = lax.optimization_barrier((feed, head_mine))
    head_other = swap(head_mine)
    feed_mine = exchange(jnp.broadcast_to(feed[None], (SLOTS, SLOT_ROWS, 512)))

    xown = inputs.reshape(OWN, D)
    cot = cotangent.reshape(OWN, D)
    cosk, sink = rotary_tables(jnp.arange(SEQ, dtype=jnp.int32))
    cosq, sinq = rotary_tables(ctx * ROWS + jnp.arange(ROWS, dtype=jnp.int32))
    pr, sq, so, po = placements(dp % 2)

    wq, wkv, nown, qs, kv, segs = call(
        project_kernel,
        [
            ((D, PAD_Q), bf16),
            ((D, 2 * KV), bf16),
            ((OWN, D), bf16),
            ((PAIRS, STACK, 128), bf16),
            ((OWN, 2 * KV), bf16),
            ((N_CTX, 16, 128), f32),
        ],
        [((PAD_D, RAW), bf16), ((D, RAW), bf16)],
        head_mine, head_other, xown, attention_gain, cosq, sinq, pr, sq,
        place=place,
    )
    kv, feed_mine = lax.optimization_barrier((kv, feed_mine))
    feed_other = swap(feed_mine)
    kv_all = lax.all_to_all(
        jnp.broadcast_to(kv[None], (N_CTX, OWN, 2 * KV)), "ctx", 0, 0, tiled=True
    )
    down_raw, wo = call(
        unpack_kernel,
        [((FF, RAW), bf16), ((PAD_D, D), bf16)],
        [((PAD_D, RAW), bf16)],
        feed_mine, feed_other, so,
        place=place,
    )
    late, kv_all = lax.optimization_barrier((xown, kv_all))
    xall = lax.all_to_all(
        jnp.broadcast_to(late[None], (N_CTX, OWN, D)), "ctx", 0, 0, tiled=True
    )

    kvs, pt, mixr, middle = call(
        attend_kernel,
        [
            ((BATCH, SEQ, 2 * KV), bf16),
            ((PAIRS, SEQ, STACK), bf16),
            ((OWN, PAD_D), bf16),
            ((OWN, D), f32),
        ],
        [((BATCH, SEQ, ROWS), f32), ((OWN, PAD_Q), bf16)],
        kv_all, qs, segs, segments.astype(f32), xown, po, wo,
        place=place,
    )

    result, gs, feed_keep, feed_give, middle_grad, gain_grad = call(
        feed_kernel,
        [
            ((OWN, D), bf16),
            ((PAIRS, STACK, 128), bf16),
            ((SLOTS, SLOT_ROWS, 512), bf16),
            ((SLOTS, SLOT_ROWS, 512), bf16),
            ((OWN, D), f32),
            ((1, D), f32),
        ],
        [((PAD_D, RAW), f32), ((FF, RAW), bf16)],
        feed_mine, feed_other, down_raw, middle, mixr, cot, swiglu_gain, wo, pr, so, po,
        place=place,
    )
    feed_keep, feed_give, gs, xall = lax.optimization_barrier((feed_keep, feed_give, gs, xall))
    feed_sum = (feed_keep.astype(f32) + swap(feed_give).astype(f32)).astype(bf16)
    feed_sum, gs = lax.optimization_barrier((feed_sum, gs))
    feed_came = exchange(feed_sum)

    keep, give, dkv, query_part = call(
        backward_kernel,
        [
            ((SLOTS, SLOT_ROWS, 128), bf16),
            ((SLOTS, SLOT_ROWS, 128), bf16),
            ((N_CTX, OWN, 2 * KV), bf16),
            ((OWN, D), f32),
        ],
        [
            ((OWN, PAD_Q), bf16),
            ((PAIRS, SEQ, 128), bf16),
            ((PAIRS, SEQ, 128), bf16),
            ((D, 2 * KV), f32),
            ((PAD_D, RAW), f32),
        ],
        pt, qs, kvs, gs, nown, xall, xown, attention_gain, wq, wkv, gain_grad,
        cosk, sink, cosq, sinq, pr, sq,
    )
    dkv, give, feed_came = lax.optimization_barrier((dkv, give, feed_came))
    dkv_came = lax.all_to_all(dkv, "ctx", 0, 0, tiled=True)
    head_sum = (keep.astype(f32) + swap(give).astype(f32)).astype(bf16)
    head_sum, dkv_came = lax.optimization_barrier((head_sum, dkv_came))
    head_came = exchange(head_sum)
    (input_grad,) = call(
        input_kernel,
        [((OWN, D), f32)],
        [],
        dkv_came, query_part, xown, attention_gain, wkv, middle_grad,
    )

    qkv = jnp.sum(head_came.astype(f32), axis=0)
    rest = jnp.sum(feed_came.astype(f32), axis=0)
    first_total = qkv[36:41].reshape(1, 640)[:, :D]
    second_total = qkv[41:46].reshape(1, 640)[:, :D]
    gu = rest[:36, 128:]
    gate_total = jnp.concatenate([gu[:, :128], gu[:, 256:320]], axis=1)
    up_total = jnp.concatenate([gu[:, 128:256], gu[:, 320:]], axis=1)
    main = jnp.concatenate([rest[36:, j * 128 : (j + 1) * 128] for j in range(4)], axis=0)
    extra = jnp.concatenate([rest[:36, 72:88], rest[:12, 88:104]], axis=0)
    down_total = jnp.concatenate(
        [
            jnp.concatenate([main[:, :64], extra[:, :8]], axis=1),
            jnp.concatenate([main[:, 64:], extra[:, 8:]], axis=1),
        ],
        axis=0,
    )
    return (
        result.reshape(BATCH, ROWS, D),
        input_grad.reshape(BATCH, ROWS, D),
        first_total,
        qkv[None, :36, :72],
        qkv[None, :36, 72:96],
        qkv[None, :36, 96:120],
        rest[None, :36, :72],
        second_total,
        gate_total[None],
        up_total[None],
        down_total[None],
    )


def solution(mesh):
    weight = P(None, "dp", "ctx")
    rows = P("dp", "ctx", None)
    return jax.shard_map(
        body,
        mesh=mesh,
        in_specs=(rows, P("dp", "ctx"), rows, P(), weight, weight, weight, weight, P(), weight, weight, weight),
        out_specs=(rows, rows, P(), weight, weight, weight, weight, P(), weight, weight, weight),
        check_vma=False,
    )
```

```python
import functools

import jax
import jax.numpy as jnp
from jax import lax
from jax.experimental import pallas as pl
from jax.experimental.pallas import tpu as pltpu
from jax.sharding import PartitionSpec as P

HEADS = 9
KV_HEADS = 3
HEAD_DIM = 64
GROUP = HEADS // KV_HEADS
D = 576
FF = 1536
KV = KV_HEADS * HEAD_DIM
BATCH = 2
ROWS = 128
SEQ = 1024
OWN = BATCH * ROWS
ALL = BATCH * SEQ
N_CTX = 8
N_DP = 16
N_ZX = N_DP // 2
SLOTS = N_CTX * N_ZX
SLOT_ROWS = 48
HALF = N_ZX * SLOT_ROWS
PAD_D = 2 * HALF
RAW = N_CTX * 128
PAD_Q = HEADS * 128
STACK = GROUP * ROWS
PAIRS = BATCH * KV_HEADS

eps = 1e-05
theta = 10000.0
masked = -1e30
bf16 = jnp.bfloat16
f32 = jnp.float32

EVERY = ("dp", "ctx")
SAME_CORE = [
    [(zx * 2 + core) * N_CTX + ctx for ctx in range(N_CTX) for zx in range(N_ZX)]
    for core in range(2)
]
OTHER_CORE = [
    (dp * N_CTX + ctx, (dp ^ 1) * N_CTX + ctx) for dp in range(N_DP) for ctx in range(N_CTX)
]


def nn(left, right):
    return jnp.dot(left, right, preferred_element_type=f32)


def tn(left, right):
    return lax.dot_general(left, right, (((0,), (0,)), ((), ())), preferred_element_type=f32)


def nt(left, right):
    return lax.dot_general(left, right, (((1,), (1,)), ((), ())), preferred_element_type=f32)


def halves(x):
    high = x.astype(bf16)
    return high, (x - high.astype(f32)).astype(bf16)


def rho_of(x):
    return lax.rsqrt(jnp.mean(x * x, axis=-1, keepdims=True) + eps)


def norm_back(x, gain, c):
    rho = rho_of(x)
    w = c * gain
    grad = rho * (w - x * (rho * rho * jnp.mean(w * x, axis=-1, keepdims=True)))
    return grad, jnp.sum(c * (x * rho), axis=0, keepdims=True)


def lanes(shape):
    return lax.broadcasted_iota(jnp.int32, shape, 1)


def turn(x, cosine, sine):
    first = lanes(x.shape) % HEAD_DIM < HEAD_DIM // 2
    turned = jnp.where(first, -pltpu.roll(x, 96, 1), pltpu.roll(x, 32, 1))
    return x * cosine + turned * sine


def turn_back(x, cosine, sine):
    first = lanes(x.shape) % HEAD_DIM < HEAD_DIM // 2
    w = x * sine
    turned = jnp.where(first, pltpu.roll(w, 96, 1), -pltpu.roll(w, 32, 1))
    return x * cosine + turned


def triple(x, axis):
    return jnp.concatenate([x] * GROUP, axis=axis)


def block(ref, c, start, width):
    return ref[c * N_ZX : (c + 1) * N_ZX, :, start : start + width].reshape(HALF, width)


def hidden_place(unit):
    n = unit * 16
    c, m = divmod(n, 192)
    base = (c // 2) * 384
    if m < 128:
        return base + (c % 2) * 128 + m
    return base + 256 + (c % 2) * 64 + (m - 128)


def attend_kernel(
    place, mine, other, xall, xown, gain, segq, cosk, sink, cosq, sinq, pr, sq, po,
    wq, wkv, nrow, qs, kvs, pt, mixr,
    raw, wmid, bias, mixp,
):
    ctx, zx_own = place[1], place[2]
    for c in range(N_CTX):
        raw[:HALF, c * 128 : (c + 1) * 128] = block(mine, c, 0, 128)
        raw[HALF:, c * 128 : (c + 1) * 128] = block(other, c, 0, 128)
    wmid[...] = nn(pr[...], raw[...]).astype(bf16)
    wkv[...] = nn(wmid[...], sq[:, PAD_Q:]).astype(bf16)
    wq[...] = nn(wmid[...], sq[:, :PAD_Q]).astype(bf16)

    x = xown[...].astype(f32)
    normed = (x * rho_of(x) * gain[...]).astype(bf16)
    nrow[...] = nn(normed, pr[...]).astype(bf16)
    pre = nn(normed, wq[...])
    for head in range(HEADS):
        h, g = divmod(head, GROUP)
        for b in range(BATCH):
            turned = turn(
                pre[b * ROWS : (b + 1) * ROWS, head * 128 : (head + 1) * 128], cosq[...], sinq[...]
            )
            qs[b * KV_HEADS + h, g * ROWS : (g + 1) * ROWS, :] = (
                turned.astype(bf16) * bf16(HEAD_DIM**-0.5)
            )

    low = lanes((ROWS, 128)) < HEAD_DIM

    def project(c, carry):
        at = pl.multiple_of(c * ROWS, ROWS)
        x = xall[c].astype(f32)
        normed = (x * rho_of(x) * gain[...]).astype(bf16)
        pre = nn(normed, wkv[...])
        cosine, sine = cosk[pl.ds(at, ROWS), :], sink[pl.ds(at, ROWS), :]
        ends = mine[c * N_ZX + zx_own][32:].astype(f32)
        for b in range(BATCH):
            rows = pre[b * ROWS : (b + 1) * ROWS]
            tile = rows[:, 128:256]
            kvs[b, pl.ds(at, ROWS), :128] = turn(rows[:, :128], cosine, sine).astype(bf16)
            kvs[b, pl.ds(at, ROWS), 128:256] = jnp.where(
                low, turn(tile, cosine, sine), tile
            ).astype(bf16)
            kvs[b, pl.ds(at, ROWS), 256:] = rows[:, 256:].astype(bf16)
            keys = jnp.broadcast_to(ends[4 + b : 5 + b, :], (ROWS, ROWS)).T
            key_pos = c * ROWS + lax.broadcasted_iota(jnp.int32, (ROWS, ROWS), 0)
            query_pos = ctx * ROWS + lanes((ROWS, ROWS))
            allowed = (keys == segq[b : b + 1, :]) & (key_pos <= query_pos)
            bias[b, pl.ds(at, ROWS), :] = jnp.where(allowed, 0.0, masked)
        return carry

    lax.fori_loop(0, N_CTX, project, 0)

    def attend(i, carry):
        b = i // KV_HEADS
        h = i - b * KV_HEADS
        keys = kvs[b, :, pl.ds(pl.multiple_of(h // 2 * 128, 128), 128)]
        values = kvs[b, :, pl.ds(pl.multiple_of((h + 3) // 2 * 128, 128), 128)]
        scores = nt(keys, qs[i]) + triple(bias[b], 1)
        top = jnp.max(scores, axis=0, keepdims=True)
        expo = jnp.exp(scores - top)
        total = jnp.sum(expo, axis=0, keepdims=True)
        probs = (expo * (1.0 / total)).astype(bf16)
        pt[i] = probs
        mixed = tn(values, probs).T.astype(bf16)
        for g in range(GROUP):
            mixp[
                pl.ds(pl.multiple_of(b * ROWS, ROWS), ROWS),
                pl.ds(pl.multiple_of((h * GROUP + g) * 128, 128), 128),
            ] = mixed[g * ROWS : (g + 1) * ROWS]
        return carry

    lax.fori_loop(0, PAIRS, attend, 0)
    mixr[...] = nn(mixp[...], po[...]).astype(bf16)


def unpack(mine, down, oraw):
    lane = lanes((SLOT_ROWS, 128))
    for c in range(N_CTX):
        oraw[:, c * 128 : (c + 1) * 128] = block(mine, c, 0, 128)

    def one(zx, carry):
        at = pl.multiple_of(zx * 96, 96)
        for c in range(N_CTX):
            o = mine[c * N_ZX + zx, :, :128].astype(f32)
            t = jnp.concatenate(
                [o[36:]]
                + [
                    mine[c * N_ZX + zx, 32:, j * 128 : (j + 1) * 128].astype(f32)[4:]
                    for j in range(1, 4)
                ],
                axis=0,
            )
            e = jnp.concatenate([o[:36], pltpu.roll(o[:16], 112, 1)[:12]], axis=0)
            first = jnp.where(lane < 64, t, jnp.where(lane < 72, pltpu.roll(e, 120, 1), 0.0))
            second = jnp.where(
                lane < 64,
                pltpu.roll(t, 64, 1),
                jnp.where(lane < 72, pltpu.roll(e, 112, 1), 0.0),
            )
            down[pl.ds(at, 96), c * 128 : (c + 1) * 128] = jnp.concatenate(
                [first, second], axis=0
            ).astype(bf16)
        return carry

    lax.fori_loop(0, N_ZX, one, 0)


def unpack_kernel(mine, so, down, wo, oraw):
    unpack(mine, down, oraw)
    wo[...] = nn(oraw[...], so[...]).astype(bf16)


def place_of(c, odd_dp, n):
    m = odd_dp * 96 + n
    base = (c // 2) * 384
    at = jnp.where(m < 128, base + c % 2 * 128 + m, base + 256 + c % 2 * 64 + (m - 128))
    return pl.multiple_of(at, 16)


def feed_kernel(
    place, mine, other, down_mine, xown, mixr, cot, gain, wo, pr, so, po,
    result, gs, keep, give, middle_grad, gain_grad,
    d1, dd, down, oraw, down_other, wo_other,
):
    core = place[0]
    unpack(other, down_other, oraw)
    wo_other[...] = nn(oraw[...], so[...]).astype(bf16)
    for who, ref in enumerate((down_mine, down_other)):
        for zx in range(N_ZX):
            for n in range(0, 96, 16):
                down[pl.ds(place_of(zx, who ^ core, n), 16), :] = ref[
                    zx * 96 + n : zx * 96 + n + 16, :
                ]
    mixed_r = mixr[...]
    mid = xown[...].astype(f32) + (
        nn(mixed_r[:, :HALF], wo[...]) + nn(mixed_r[:, HALF:], wo_other[...])
    )
    rho = rho_of(mid)
    second = (mid * rho * gain[...]).astype(bf16)
    second_r = nn(second, pr[...]).astype(bf16)
    e_b = cot[...]
    e_raw = nt(e_b, so[...]).astype(bf16)
    low = lanes((OWN, 128)) < 64
    grad_sum = jnp.zeros((OWN, PAD_D), f32)
    result_sum = jnp.zeros((OWN, RAW), f32)
    for pair in range(N_CTX // 2):
        weights = [
            jnp.concatenate([block(ref, c, 128, 384) for ref in (mine, other)], axis=0)
            for c in (2 * pair, 2 * pair + 1)
        ]
        pre = [nn(second_r, weight) for weight in weights]
        a, u, t, a2, u2, t2 = (pre[i // 3][:, i % 3 * 128 : (i % 3 + 1) * 128] for i in range(6))
        gate = jnp.concatenate([a, a2, jnp.where(low, t, pltpu.roll(t2, 64, 1))], axis=1)
        up = jnp.concatenate([u, u2, jnp.where(low, pltpu.roll(t, 64, 1), t2)], axis=1)
        logistic = 1.0 / (1.0 + jnp.exp(-gate))
        silu = gate * logistic
        inner = (silu * up).astype(bf16)
        rows = down[pair * 384 : (pair + 1) * 384, :]
        result_sum += nn(inner, rows)
        inner_grad = nt(e_raw, rows)
        gate_grad = inner_grad * up * (logistic * (1.0 + gate * (1.0 - logistic)))
        up_grad = inner_grad * silu
        a, a2, gt = (gate_grad[:, i * 128 : (i + 1) * 128] for i in range(3))
        u, u2, ut = (up_grad[:, i * 128 : (i + 1) * 128] for i in range(3))
        t = jnp.where(low, gt, pltpu.roll(ut, 64, 1))
        t2 = jnp.where(low, pltpu.roll(gt, 64, 1), ut)
        for k, tiles in enumerate(((a, u, t), (a2, u2, t2))):
            grads = jnp.concatenate(tiles, axis=1).astype(bf16)
            grad_sum += nt(grads, weights[k])
            terms = tn(second_r, grads).astype(bf16)
            c = 2 * pair + k
            for ref, part in ((keep, terms[:HALF]), (give, terms[HALF:])):
                ref[c * N_ZX : (c + 1) * N_ZX, :, 128:] = part.reshape(N_ZX, SLOT_ROWS, 384)
        dd_pair = tn(inner, e_raw).astype(bf16)
        for unit in range(pair * 24, pair * 24 + 24):
            at = hidden_place(unit) - pair * 384
            dd[unit * 16 : unit * 16 + 16, :] = dd_pair[at : at + 16, :]

    high, rest = halves(result_sum)
    result[...] = (mid + (nn(high, so[...]) + nn(rest, so[...]))).astype(bf16)
    high, rest = halves(grad_sum)
    second_grad = nt(high, pr[...]) + nt(rest, pr[...])
    norm_grad, gain_term = norm_back(mid, gain[...], second_grad)
    gain_grad[...] = gain_term
    total = e_b.astype(f32) + norm_grad
    middle_grad[...] = total
    middle_b = total.astype(bf16)
    middle_raw = nt(middle_b, so[...]).astype(bf16)
    d1[...] = tn(mixed_r, middle_raw)
    back = jnp.concatenate([nt(middle_b, wo[...]), nt(middle_b, wo_other[...])], axis=1)
    back = nt(back.astype(bf16), po[...]).astype(bf16)
    for head in range(HEADS):
        h, g = divmod(head, GROUP)
        for b in range(BATCH):
            gs[b * KV_HEADS + h, g * ROWS : (g + 1) * ROWS, :] = back[
                b * ROWS : (b + 1) * ROWS, head * 128 : (head + 1) * 128
            ]

    lane = lanes((SLOT_ROWS, 128))
    for who, ref in enumerate((keep, give)):

        def pack(zx, carry, ref=ref, who=who):
            row = pl.multiple_of(who * HALF + zx * SLOT_ROWS, SLOT_ROWS)
            at = pl.multiple_of((2 * zx + (who ^ core)) * 96, 16)
            for c in range(N_CTX):
                slot = c * N_ZX + zx
                first = dd[pl.ds(at, 48), c * 128 : (c + 1) * 128].astype(f32)
                second = dd[pl.ds(at + 48, 48), c * 128 : (c + 1) * 128].astype(f32)
                t = jnp.where(lane < 64, first, pltpu.roll(second, 64, 1))
                own = d1[pl.ds(row, SLOT_ROWS), c * 128 : (c + 1) * 128]
                e = jnp.where(
                    lane < 72,
                    own,
                    jnp.where(lane < 80, pltpu.roll(first, 8, 1), pltpu.roll(second, 16, 1)),
                )
                rest = pltpu.roll(e[32:], 16, 1)[4:]
                head = jnp.concatenate([rest, e[12:36]], axis=0)
                head = jnp.where(lane[:36] < 88, e[:36], jnp.where(lane[:36] < 104, head, 0.0))
                ref[slot, :, 0:128] = jnp.concatenate([head, t[:12]], axis=0).astype(bf16)
                for j in range(1, 4):
                    g = ref[slot, 32:, j * 128 : (j + 1) * 128].astype(f32)
                    ref[slot, 32:, j * 128 : (j + 1) * 128] = jnp.concatenate(
                        [g[:4], t[12 * j : 12 * j + 12]], axis=0
                    ).astype(bf16)
            return carry

        lax.fori_loop(0, N_ZX, pack, 0)


def backward_kernel(
    pt, qs, kvs, gs, cosk, sink, cosq, sinq,
    dkv, dqp,
    dk, dv,
):
    def attend(i, carry):
        b = i // KV_HEADS
        h = i - b * KV_HEADS
        keys = kvs[b, :, pl.ds(pl.multiple_of(h // 2 * 128, 128), 128)]
        values = kvs[b, :, pl.ds(pl.multiple_of((h + 3) // 2 * 128, 128), 128)]
        g_b = gs[i]
        probs_b = pt[i]
        probs = probs_b.astype(f32)
        weighted = probs * nt(values, g_b)
        delta = jnp.sum(weighted, axis=0, keepdims=True)
        ds = (weighted - probs * delta).astype(bf16)
        dk[i] = turn_back(nn(ds, qs[i]), cosk[...], sink[...]).astype(bf16)
        dv[i] = nn(probs_b, g_b).astype(bf16)
        dq = tn(keys, ds).T * HEAD_DIM**-0.5
        for g in range(GROUP):
            dqp[
                pl.ds(pl.multiple_of(b * ROWS, ROWS), ROWS),
                pl.ds(pl.multiple_of((h * GROUP + g) * 128, 128), 128),
            ] = turn_back(dq[g * ROWS : (g + 1) * ROWS], cosq[...], sinq[...]).astype(bf16)
        return carry

    lax.fori_loop(0, PAIRS, attend, 0)
    for c in range(N_CTX):
        at = slice(c * ROWS, (c + 1) * ROWS)
        for b in range(BATCH):
            k = [dk[b * 3 + h, at, :] for h in range(3)]
            v = [dv[b * 3 + h, at, :] for h in range(3)]
            dkv[c, b * ROWS : (b + 1) * ROWS, :] = jnp.concatenate(
                [k[0] + k[1], k[2] + v[0], v[1] + v[2]], axis=1
            )


def project_grads_kernel(
    dkv, dqp, nrow, xall, xown, gain, wq, wkv, pr, sq, gain_grad,
    query_part, keep, give,
    dw, raw,
):
    dw[...] = jnp.zeros(dw.shape, f32)

    def one(c, term):
        x = xall[c].astype(f32)
        scaled = x * rho_of(x)
        packed = dkv[c]
        dw[...] += tn((scaled * gain[...]).astype(bf16), packed)
        return term + jnp.sum(nt(packed, wkv[...]) * scaled, axis=0, keepdims=True)

    term = lax.fori_loop(0, N_CTX, one, jnp.zeros((1, D), f32))
    dq = dqp[...]
    part = nt(dq, wq[...])
    query_part[...] = part
    x = xown[...].astype(f32)
    term = term + jnp.sum(part * (x * rho_of(x)), axis=0, keepdims=True)
    rows = tn(pr[...], dw[...].astype(bf16)).astype(bf16)
    raw[...] = tn(nrow[...], nt(dq, sq[:, :PAD_Q]).astype(bf16)) + nt(rows, sq[:, PAD_Q:])
    row = lax.broadcasted_iota(jnp.int32, (16, 128), 0)
    ends = jnp.zeros((16, 128), f32)
    for n, values in enumerate((term, gain_grad[...])):
        wide = jnp.concatenate([values, jnp.zeros((1, 64), f32)], axis=1)
        for j in range(5):
            ends = jnp.where(row == 4 + n * 5 + j, wide[:, j * 128 : (j + 1) * 128], ends)
    for who, ref in enumerate((keep, give)):
        for zx in range(N_ZX):
            at = who * HALF + zx * SLOT_ROWS
            for c in range(N_CTX):
                values = raw[at : at + SLOT_ROWS, c * 128 : (c + 1) * 128]
                ref[c * N_ZX + zx] = jnp.concatenate(
                    [values[:32], values[32:] + ends], axis=0
                ).astype(bf16)


def input_kernel(dkv, query_part, xown, gain, wkv, middle_grad, out):
    total = dkv[0].astype(f32)
    for c in range(1, N_CTX):
        total = total + dkv[c].astype(f32)
    normed_grad = query_part[...] + nt(total.astype(bf16), wkv[...])
    grad, _ = norm_back(xown[...].astype(f32), gain[...], normed_grad)
    out[...] = middle_grad[...] + grad


def call(kernel, outs, scratch, *args, place=None):
    specs = [pl.BlockSpec(memory_space=pltpu.VMEM)] * len(args)
    if place is not None:
        specs = [pl.BlockSpec(memory_space=pltpu.SMEM)] + specs
        args = (place,) + args
    shapes = [jax.ShapeDtypeStruct(s, t) for s, t in outs]
    return pl.pallas_call(
        kernel,
        out_shape=shapes,
        in_specs=specs,
        out_specs=[pl.BlockSpec(memory_space=pltpu.VMEM)] * len(shapes),
        scratch_shapes=[pltpu.VMEM(s, t) for s, t in scratch],
        compiler_params=pltpu.CompilerParams(vmem_limit_bytes=60 * 1024 * 1024),
        cost_estimate=pl.CostEstimate(flops=1, bytes_accessed=1, transcendentals=0),
    )(*args)


def rotary_tables(positions):
    inverse_freq = theta ** (-(jnp.arange(HEAD_DIM // 2, dtype=f32) * 2.0) / HEAD_DIM)
    angles = positions.astype(f32)[:, None] * inverse_freq[None, :]
    return (
        jnp.concatenate([jnp.cos(angles)] * 4, axis=-1),
        jnp.concatenate([jnp.sin(angles)] * 4, axis=-1),
    )


def placements(core):
    def ones(rows, columns, wanted):
        return (wanted[:, None] == jnp.arange(columns)[None, :]).astype(bf16)

    def row(n):
        dp = n // 36
        return (dp % 2 ^ core) * HALF + dp // 2 * SLOT_ROWS + n % 36

    pr = ones(D, PAD_D, row(jnp.arange(D)))
    raw = jnp.arange(RAW)
    c, l = raw // 128, raw % 128
    q = jnp.where(l < 72, c * 72 + l, -1)
    k = jnp.where((l >= 72) & (l < 96), c * 24 + l - 72, -1)
    v = jnp.where((l >= 96) & (l < 120), c * 24 + l - 96, -1)
    head = q // HEAD_DIM
    upper = head // GROUP % 2
    padded = jnp.where(q < 0, -1, head * 128 + upper * HEAD_DIM + q % HEAD_DIM)
    target = jnp.where(k >= 0, PAD_Q + k, jnp.where(v >= 0, PAD_Q + KV + v, padded))
    sq = ones(RAW, PAD_Q + 2 * KV, target)
    so = ones(RAW, D, q)
    place = jnp.arange(PAD_Q)
    head, l = place // 128, place % 128
    upper = 1 - head // GROUP % 2
    inside = l // HEAD_DIM == upper
    n = head * HEAD_DIM + l % HEAD_DIM
    po = ones(PAD_Q, PAD_D, jnp.where(inside, row(n), -1))
    return pr, sq, so, po


def exchange(slots):
    return lax.all_to_all(slots, EVERY, 0, 0, tiled=True, axis_index_groups=SAME_CORE)


def swap(x):
    return lax.ppermute(x, EVERY, OTHER_CORE)


def pad_rows(x):
    return jnp.pad(x, ((0, SLOT_ROWS - x.shape[0]), (0, 0)))


def body(
    inputs,
    segments,
    cotangent,
    attention_gain,
    query_weight,
    key_weight,
    value_weight,
    out_weight,
    swiglu_gain,
    gate_weight,
    up_weight,
    down_weight,
):
    ctx, dp = lax.axis_index("ctx"), lax.axis_index("dp")
    place = jnp.stack([dp % 2, ctx, dp // 2]).astype(jnp.int32)
    down = down_weight[0]
    gate, up = gate_weight[0], up_weight[0]
    zero = functools.partial(jnp.zeros, dtype=bf16)
    head = jnp.concatenate(
        [
            jnp.concatenate([query_weight[0], key_weight[0], value_weight[0], zero((36, 8))], axis=1),
            segments.astype(bf16),
            zero((10, 128)),
        ],
        axis=0,
    )
    head_mine = exchange(jnp.broadcast_to(head[None], (SLOTS, SLOT_ROWS, 128)))
    main = jnp.concatenate([down[:48, :64], down[48:, :64]], axis=1)
    extra = jnp.concatenate([down[:48, 64:], down[48:, 64:]], axis=1)
    feed = jnp.concatenate(
        [
            jnp.concatenate(
                [
                    out_weight[0],
                    extra[:36],
                    jnp.concatenate([extra[36:], zero((24, 16))], axis=0),
                    zero((36, 24)),
                    gate[:, :128],
                    up[:, :128],
                    gate[:, 128:],
                    up[:, 128:],
                ],
                axis=1,
            ),
            jnp.concatenate([main[12 * j : 12 * j + 12] for j in range(4)], axis=1),
        ],
        axis=0,
    )
    xown = inputs.reshape(OWN, D)
    cot = cotangent.reshape(OWN, D)
    sent, head_mine = lax.optimization_barrier(
        (jnp.broadcast_to(xown[None], (N_CTX, OWN, D)), head_mine)
    )
    head_other = swap(head_mine)
    xall = lax.all_to_all(sent, "ctx", 0, 0, tiled=True)
    cosk, sink = rotary_tables(jnp.arange(SEQ, dtype=jnp.int32))
    cosq, sinq = rotary_tables(ctx * ROWS + jnp.arange(ROWS, dtype=jnp.int32))
    pr, sq, so, po = placements(dp % 2)
    slots = jnp.broadcast_to(feed[None], (SLOTS, SLOT_ROWS, 512))
    slots, xall, head_other, cosk, sink, cosq, sinq, pr, sq, so, po = lax.optimization_barrier(
        (slots, xall, head_other, cosk, sink, cosq, sinq, pr, sq, so, po)
    )
    feed_mine = exchange(slots)

    wq, wkv, nrow, qs, kvs, pt, mixr = call(
        attend_kernel,
        [
            ((D, PAD_Q), bf16),
            ((D, 2 * KV), bf16),
            ((OWN, PAD_D), bf16),
            ((PAIRS, STACK, 128), bf16),
            ((BATCH, SEQ, 2 * KV), bf16),
            ((PAIRS, SEQ, STACK), bf16),
            ((OWN, PAD_D), bf16),
        ],
        [
            ((PAD_D, RAW), bf16),
            ((D, RAW), bf16),
            ((BATCH, SEQ, ROWS), f32),
            ((OWN, PAD_Q), bf16),
        ],
        head_mine, head_other, xall, xown, attention_gain, segments.astype(f32),
        cosk, sink, cosq, sinq, pr, sq, po,
        place=place,
    )
    feed_mine, mixr = lax.optimization_barrier((feed_mine, mixr))
    feed_other = swap(feed_mine)
    down_mine, wo = call(
        unpack_kernel,
        [((HALF * 2, RAW), bf16), ((HALF, D), bf16)],
        [((HALF, RAW), bf16)],
        feed_mine, so,
    )

    result, gs, feed_keep, feed_give, middle_grad, gain_grad = call(
        feed_kernel,
        [
            ((OWN, D), bf16),
            ((PAIRS, STACK, 128), bf16),
            ((SLOTS, SLOT_ROWS, 512), bf16),
            ((SLOTS, SLOT_ROWS, 512), bf16),
            ((OWN, D), f32),
            ((1, D), f32),
        ],
        [
            ((PAD_D, RAW), f32),
            ((FF, RAW), bf16),
            ((FF, RAW), bf16),
            ((HALF, RAW), bf16),
            ((HALF * 2, RAW), bf16),
            ((HALF, D), bf16),
        ],
        feed_mine, feed_other, down_mine, xown, mixr, cot, swiglu_gain, wo, pr, so, po,
        place=place,
    )
    feed_sum = (feed_keep.astype(f32) + swap(feed_give).astype(f32)).astype(bf16)
    feed_sum, gs = lax.optimization_barrier((feed_sum, gs))
    feed_came = exchange(feed_sum)

    dkv, dqp = call(
        backward_kernel,
        [((N_CTX, OWN, 2 * KV), bf16), ((OWN, PAD_Q), bf16)],
        [((PAIRS, SEQ, 128), bf16), ((PAIRS, SEQ, 128), bf16)],
        pt, qs, kvs, gs, cosk, sink, cosq, sinq,
    )
    query_part, keep, give = call(
        project_grads_kernel,
        [
            ((OWN, D), f32),
            ((SLOTS, SLOT_ROWS, 128), bf16),
            ((SLOTS, SLOT_ROWS, 128), bf16),
        ],
        [((D, 2 * KV), f32), ((PAD_D, RAW), f32)],
        dkv, dqp, nrow, xall, xown, attention_gain, wq, wkv, pr, sq, gain_grad,
    )
    head_sum = (keep.astype(f32) + swap(give).astype(f32)).astype(bf16)
    dkv, head_sum, feed_came = lax.optimization_barrier((dkv, head_sum, feed_came))
    dkv_came = lax.all_to_all(dkv, "ctx", 0, 0, tiled=True)
    dkv_came, head_sum = lax.optimization_barrier((dkv_came, head_sum))
    head_came = exchange(head_sum)
    (input_grad,) = call(
        input_kernel,
        [((OWN, D), f32)],
        [],
        dkv_came, query_part, xown, attention_gain, wkv, middle_grad,
    )

    qkv = jnp.sum(head_came.astype(f32), axis=0)
    rest = jnp.sum(feed_came.astype(f32), axis=0)
    first_total = qkv[36:41].reshape(1, 640)[:, :D]
    second_total = qkv[41:46].reshape(1, 640)[:, :D]
    gu = rest[:36, 128:]
    gate_total = jnp.concatenate([gu[:, :128], gu[:, 256:320]], axis=1)
    up_total = jnp.concatenate([gu[:, 128:256], gu[:, 320:]], axis=1)
    main = jnp.concatenate([rest[36:, j * 128 : (j + 1) * 128] for j in range(4)], axis=0)
    extra = jnp.concatenate([rest[:36, 72:88], rest[:12, 88:104]], axis=0)
    down_total = jnp.concatenate(
        [
            jnp.concatenate([main[:, :64], extra[:, :8]], axis=1),
            jnp.concatenate([main[:, 64:], extra[:, 8:]], axis=1),
        ],
        axis=0,
    )
    return (
        result.reshape(BATCH, ROWS, D),
        input_grad.reshape(BATCH, ROWS, D),
        first_total,
        qkv[None, :36, :72],
        qkv[None, :36, 72:96],
        qkv[None, :36, 96:120],
        rest[None, :36, :72],
        second_total,
        gate_total[None],
        up_total[None],
        down_total[None],
    )


def solution(mesh):
    weight = P(None, "dp", "ctx")
    rows = P("dp", "ctx", None)
    return jax.shard_map(
        body,
        mesh=mesh,
        in_specs=(rows, P("dp", "ctx"), rows, P(), weight, weight, weight, weight, P(), weight, weight, weight),
        out_specs=(rows, rows, P(), weight, weight, weight, weight, P(), weight, weight, weight),
        check_vma=False,
    )
```

```python
import functools

import jax
import jax.numpy as jnp
from jax import lax
from jax.experimental import pallas as pl
from jax.experimental.pallas import tpu as pltpu
from jax.sharding import PartitionSpec as P

HEADS = 9
KV_HEADS = 3
HEAD_DIM = 64
GROUP = HEADS // KV_HEADS
D = 576
FF = 1536
KV = KV_HEADS * HEAD_DIM
BATCH = 2
ROWS = 128
SEQ = 1024
OWN = BATCH * ROWS
ALL = BATCH * SEQ
N_CTX = 8
N_DP = 16
N_ZX = N_DP // 2
SLOTS = N_CTX * N_ZX
SLOT_ROWS = 48
HALF = N_ZX * SLOT_ROWS
PAD_D = 2 * HALF
RAW = N_CTX * 128
PAD_Q = HEADS * 128
STACK = GROUP * ROWS
AT_SECOND, AT_FEED, AT_INNER, AT_E, AT_MIDDLE, AT_MIXED, ACTS = 0, 768, 3840, 5376, 6400, 7424, 8192
PAIRS = BATCH * KV_HEADS

eps = 1e-05
theta = 10000.0
masked = -1e30
bf16 = jnp.bfloat16
f32 = jnp.float32

EVERY = ("dp", "ctx")
SAME_CORE = [
    [(zx * 2 + core) * N_CTX + ctx for ctx in range(N_CTX) for zx in range(N_ZX)]
    for core in range(2)
]
OTHER_CORE = [
    (dp * N_CTX + ctx, (dp ^ 1) * N_CTX + ctx) for dp in range(N_DP) for ctx in range(N_CTX)
]


def nn(left, right):
    return jnp.dot(left, right, preferred_element_type=f32)


def tn(left, right):
    return lax.dot_general(left, right, (((0,), (0,)), ((), ())), preferred_element_type=f32)


def nt(left, right):
    return lax.dot_general(left, right, (((1,), (1,)), ((), ())), preferred_element_type=f32)


def halves(x):
    high = x.astype(bf16)
    return high, (x - high.astype(f32)).astype(bf16)


def rho_of(x):
    return lax.rsqrt(jnp.mean(x * x, axis=-1, keepdims=True) + eps)


def norm_back(x, gain, c):
    rho = rho_of(x)
    w = c * gain
    grad = rho * (w - x * (rho * rho * jnp.mean(w * x, axis=-1, keepdims=True)))
    return grad, jnp.sum(c * (x * rho), axis=0, keepdims=True)


def lanes(shape):
    return lax.broadcasted_iota(jnp.int32, shape, 1)


def turn(x, cosine, sine):
    first = lanes(x.shape) % HEAD_DIM < HEAD_DIM // 2
    turned = jnp.where(first, -pltpu.roll(x, 96, 1), pltpu.roll(x, 32, 1))
    return x * cosine + turned * sine


def turn_back(x, cosine, sine):
    first = lanes(x.shape) % HEAD_DIM < HEAD_DIM // 2
    w = x * sine
    turned = jnp.where(first, pltpu.roll(w, 96, 1), -pltpu.roll(w, 32, 1))
    return x * cosine + turned


def triple(x, axis):
    return jnp.concatenate([x] * GROUP, axis=axis)


def block(ref, c, start, width):
    return ref[c * N_ZX : (c + 1) * N_ZX, :, start : start + width].reshape(HALF, width)


def hidden_place(unit):
    n = unit * 16
    c, m = divmod(n, 192)
    base = (c // 2) * 384
    if m < 128:
        return base + (c % 2) * 128 + m
    return base + 256 + (c % 2) * 64 + (m - 128)


def attend_kernel(
    place, mine, other, xall, xown, gain, segq, cosk, sink, cosq, sinq, pr, sq, po,
    wq, wkv, nrow, qs, kvs, pt, mixr,
    raw, wmid, bias, mixp,
):
    ctx, zx_own = place[1], place[2]
    for c in range(N_CTX):
        raw[:HALF, c * 128 : (c + 1) * 128] = block(mine, c, 0, 128)
        raw[HALF:, c * 128 : (c + 1) * 128] = block(other, c, 0, 128)
    wmid[...] = nn(pr[...], raw[...]).astype(bf16)
    wkv[...] = nn(wmid[...], sq[:, PAD_Q:]).astype(bf16)
    wq[...] = nn(wmid[...], sq[:, :PAD_Q]).astype(bf16)

    x = xown[...].astype(f32)
    normed = (x * rho_of(x) * gain[...]).astype(bf16)
    nrow[...] = nn(normed, pr[...]).astype(bf16)
    pre = nn(normed, wq[...])
    for head in range(HEADS):
        h, g = divmod(head, GROUP)
        for b in range(BATCH):
            turned = turn(
                pre[b * ROWS : (b + 1) * ROWS, head * 128 : (head + 1) * 128], cosq[...], sinq[...]
            )
            qs[b * KV_HEADS + h, g * ROWS : (g + 1) * ROWS, :] = (
                turned.astype(bf16) * bf16(HEAD_DIM**-0.5)
            )

    low = lanes((ROWS, 128)) < HEAD_DIM

    def project(c, carry):
        at = pl.multiple_of(c * ROWS, ROWS)
        x = xall[c].astype(f32)
        normed = (x * rho_of(x) * gain[...]).astype(bf16)
        pre = nn(normed, wkv[...])
        cosine, sine = cosk[pl.ds(at, ROWS), :], sink[pl.ds(at, ROWS), :]
        ends = mine[c * N_ZX + zx_own][32:].astype(f32)
        for b in range(BATCH):
            rows = pre[b * ROWS : (b + 1) * ROWS]
            tile = rows[:, 128:256]
            kvs[b, pl.ds(at, ROWS), :128] = turn(rows[:, :128], cosine, sine).astype(bf16)
            kvs[b, pl.ds(at, ROWS), 128:256] = jnp.where(
                low, turn(tile, cosine, sine), tile
            ).astype(bf16)
            kvs[b, pl.ds(at, ROWS), 256:] = rows[:, 256:].astype(bf16)
            keys = jnp.broadcast_to(ends[4 + b : 5 + b, :], (ROWS, ROWS)).T
            key_pos = c * ROWS + lax.broadcasted_iota(jnp.int32, (ROWS, ROWS), 0)
            query_pos = ctx * ROWS + lanes((ROWS, ROWS))
            allowed = (keys == segq[b : b + 1, :]) & (key_pos <= query_pos)
            bias[b, pl.ds(at, ROWS), :] = jnp.where(allowed, 0.0, masked)
        return carry

    lax.fori_loop(0, N_CTX, project, 0)

    def attend(i, carry):
        b = i // KV_HEADS
        h = i - b * KV_HEADS
        keys = kvs[b, :, pl.ds(pl.multiple_of(h // 2 * 128, 128), 128)]
        values = kvs[b, :, pl.ds(pl.multiple_of((h + 3) // 2 * 128, 128), 128)]
        scores = nt(keys, qs[i]) + triple(bias[b], 1)
        top = jnp.max(scores, axis=0, keepdims=True)
        expo = jnp.exp(scores - top)
        total = jnp.sum(expo, axis=0, keepdims=True)
        probs = (expo * (1.0 / total)).astype(bf16)
        pt[i] = probs
        mixed = tn(values, probs).T.astype(bf16)
        for g in range(GROUP):
            mixp[
                pl.ds(pl.multiple_of(b * ROWS, ROWS), ROWS),
                pl.ds(pl.multiple_of((h * GROUP + g) * 128, 128), 128),
            ] = mixed[g * ROWS : (g + 1) * ROWS]
        return carry

    lax.fori_loop(0, PAIRS, attend, 0)
    mixr[...] = nn(mixp[...], po[...]).astype(bf16)


def unpack(mine, down, oraw):
    lane = lanes((SLOT_ROWS, 128))
    for c in range(N_CTX):
        oraw[:, c * 128 : (c + 1) * 128] = block(mine, c, 0, 128)

    def one(zx, carry):
        at = pl.multiple_of(zx * 96, 96)
        for c in range(N_CTX):
            o = mine[c * N_ZX + zx, :, :128].astype(f32)
            t = jnp.concatenate(
                [o[36:]]
                + [
                    mine[c * N_ZX + zx, 32:, j * 128 : (j + 1) * 128].astype(f32)[4:]
                    for j in range(1, 4)
                ],
                axis=0,
            )
            e = jnp.concatenate([o[:36], pltpu.roll(o[:16], 112, 1)[:12]], axis=0)
            first = jnp.where(lane < 64, t, jnp.where(lane < 72, pltpu.roll(e, 120, 1), 0.0))
            second = jnp.where(
                lane < 64,
                pltpu.roll(t, 64, 1),
                jnp.where(lane < 72, pltpu.roll(e, 112, 1), 0.0),
            )
            down[pl.ds(at, 96), c * 128 : (c + 1) * 128] = jnp.concatenate(
                [first, second], axis=0
            ).astype(bf16)
        return carry

    lax.fori_loop(0, N_ZX, one, 0)


def unpack_kernel(mine, so, down, wo, oraw):
    unpack(mine, down, oraw)
    wo[...] = nn(oraw[...], so[...]).astype(bf16)


def place_of(c, odd_dp, n):
    m = odd_dp * 96 + n
    base = (c // 2) * 384
    at = jnp.where(m < 128, base + c % 2 * 128 + m, base + 256 + c % 2 * 64 + (m - 128))
    return pl.multiple_of(at, 16)


def feed_kernel(
    place, mine, other, down_mine, xown, mixr, cot, gain, wo, pr, so, po,
    result, gs, acts, middle_grad, gain_grad,
    down, oraw, down_other, wo_other,
):
    core = place[0]
    unpack(other, down_other, oraw)
    wo_other[...] = nn(oraw[...], so[...]).astype(bf16)
    for who, ref in enumerate((down_mine, down_other)):
        for zx in range(N_ZX):
            for n in range(0, 96, 16):
                down[pl.ds(place_of(zx, who ^ core, n), 16), :] = ref[
                    zx * 96 + n : zx * 96 + n + 16, :
                ]
    mixed_r = mixr[...]
    mid = xown[...].astype(f32) + (
        nn(mixed_r[:, :HALF], wo[...]) + nn(mixed_r[:, HALF:], wo_other[...])
    )
    rho = rho_of(mid)
    second = (mid * rho * gain[...]).astype(bf16)
    second_r = nn(second, pr[...]).astype(bf16)
    e_b = cot[...]
    e_raw = nt(e_b, so[...]).astype(bf16)
    acts[:, AT_SECOND:AT_FEED] = second_r
    acts[:, AT_E:AT_MIDDLE] = e_raw
    acts[:, AT_MIXED:] = mixed_r
    low = lanes((OWN, 128)) < 64
    grad_sum = jnp.zeros((OWN, PAD_D), f32)
    result_sum = jnp.zeros((OWN, RAW), f32)
    for pair in range(N_CTX // 2):
        weights = [
            jnp.concatenate([block(ref, c, 128, 384) for ref in (mine, other)], axis=0)
            for c in (2 * pair, 2 * pair + 1)
        ]
        pre = [nn(second_r, weight) for weight in weights]
        a, u, t, a2, u2, t2 = (pre[i // 3][:, i % 3 * 128 : (i % 3 + 1) * 128] for i in range(6))
        gate = jnp.concatenate([a, a2, jnp.where(low, t, pltpu.roll(t2, 64, 1))], axis=1)
        up = jnp.concatenate([u, u2, jnp.where(low, pltpu.roll(t, 64, 1), t2)], axis=1)
        logistic = 1.0 / (1.0 + jnp.exp(-gate))
        silu = gate * logistic
        inner = (silu * up).astype(bf16)
        rows = down[pair * 384 : (pair + 1) * 384, :]
        result_sum += nn(inner, rows)
        inner_grad = nt(e_raw, rows)
        gate_grad = inner_grad * up * (logistic * (1.0 + gate * (1.0 - logistic)))
        up_grad = inner_grad * silu
        a, a2, gt = (gate_grad[:, i * 128 : (i + 1) * 128] for i in range(3))
        u, u2, ut = (up_grad[:, i * 128 : (i + 1) * 128] for i in range(3))
        t = jnp.where(low, gt, pltpu.roll(ut, 64, 1))
        t2 = jnp.where(low, pltpu.roll(gt, 64, 1), ut)
        for k, tiles in enumerate(((a, u, t), (a2, u2, t2))):
            grads = jnp.concatenate(tiles, axis=1).astype(bf16)
            grad_sum += nt(grads, weights[k])
            at = AT_FEED + (2 * pair + k) * 384
            acts[:, at : at + 384] = grads
        acts[:, AT_INNER + pair * 384 : AT_INNER + (pair + 1) * 384] = inner

    high, rest = halves(result_sum)
    result[...] = (mid + (nn(high, so[...]) + nn(rest, so[...]))).astype(bf16)
    high, rest = halves(grad_sum)
    second_grad = nt(high, pr[...]) + nt(rest, pr[...])
    norm_grad, gain_term = norm_back(mid, gain[...], second_grad)
    gain_grad[...] = gain_term
    total = e_b.astype(f32) + norm_grad
    middle_grad[...] = total
    middle_b = total.astype(bf16)
    acts[:, AT_MIDDLE:AT_MIXED] = nt(middle_b, so[...]).astype(bf16)
    back = jnp.concatenate([nt(middle_b, wo[...]), nt(middle_b, wo_other[...])], axis=1)
    back = nt(back.astype(bf16), po[...]).astype(bf16)
    for head in range(HEADS):
        h, g = divmod(head, GROUP)
        for b in range(BATCH):
            gs[b * KV_HEADS + h, g * ROWS : (g + 1) * ROWS, :] = back[
                b * ROWS : (b + 1) * ROWS, head * 128 : (head + 1) * 128
            ]


def terms_kernel(place, acts, acts_other, slots, d1, dd):
    core = place[0]

    def both(start, width):
        return jnp.concatenate(
            [acts[:, start : start + width], acts_other[:, start : start + width]], axis=0
        )

    def both_rows(start):
        own, other = start, start + HALF
        return jnp.concatenate(
            [acts[:, own : own + HALF], acts_other[:, other : other + HALF]], axis=0
        )

    slots[:, :, :128] = jnp.zeros((SLOTS, SLOT_ROWS, 128), bf16)
    left = both_rows(AT_SECOND)
    for c in range(N_CTX):
        terms = tn(left, both(AT_FEED + c * 384, 384)).astype(bf16)
        slots[c * N_ZX : (c + 1) * N_ZX, :, 256:] = terms.reshape(N_ZX, SLOT_ROWS, 384)
    d1[...] = tn(both_rows(AT_MIXED), both(AT_MIDDLE, RAW))
    e_raw = both(AT_E, RAW)
    for pair in range(N_CTX // 2):
        dd_pair = tn(both(AT_INNER + pair * 384, 384), e_raw).astype(bf16)
        for unit in range(pair * 24, pair * 24 + 24):
            at = hidden_place(unit) - pair * 384
            dd[unit * 16 : unit * 16 + 16, :] = dd_pair[at : at + 16, :]

    lane = lanes((SLOT_ROWS, 128))

    def pack(zx, carry):
        row = pl.multiple_of(zx * SLOT_ROWS, SLOT_ROWS)
        at = pl.multiple_of((2 * zx + core) * 96, 16)
        for c in range(N_CTX):
            slot = c * N_ZX + zx
            first = dd[pl.ds(at, 48), c * 128 : (c + 1) * 128].astype(f32)
            second = dd[pl.ds(at + 48, 48), c * 128 : (c + 1) * 128].astype(f32)
            t = jnp.where(lane < 64, first, pltpu.roll(second, 64, 1))
            own = d1[pl.ds(row, SLOT_ROWS), c * 128 : (c + 1) * 128]
            e = jnp.where(
                lane < 72,
                own,
                jnp.where(lane < 80, pltpu.roll(first, 8, 1), pltpu.roll(second, 16, 1)),
            )
            rest = pltpu.roll(e[32:], 16, 1)[4:]
            head = jnp.concatenate([rest, e[12:36]], axis=0)
            head = jnp.where(lane[:36] < 88, e[:36], jnp.where(lane[:36] < 104, head, 0.0))
            slots[slot, :, 128:256] = jnp.concatenate([head, t[:12]], axis=0).astype(bf16)
            for j in range(3):
                at_lane = 256 + j * 128
                g = slots[slot, 32:, at_lane : at_lane + 128].astype(f32)
                slots[slot, 32:, at_lane : at_lane + 128] = jnp.concatenate(
                    [g[:4], t[12 * j + 12 : 12 * j + 24]], axis=0
                ).astype(bf16)
        return carry

    lax.fori_loop(0, N_ZX, pack, 0)


def backward_kernel(
    pt, qs, kvs, gs, cosk, sink, cosq, sinq,
    dkv, dqp,
    dk, dv,
):
    def attend(i, carry):
        b = i // KV_HEADS
        h = i - b * KV_HEADS
        keys = kvs[b, :, pl.ds(pl.multiple_of(h // 2 * 128, 128), 128)]
        values = kvs[b, :, pl.ds(pl.multiple_of((h + 3) // 2 * 128, 128), 128)]
        g_b = gs[i]
        probs_b = pt[i]
        probs = probs_b.astype(f32)
        weighted = probs * nt(values, g_b)
        delta = jnp.sum(weighted, axis=0, keepdims=True)
        ds = (weighted - probs * delta).astype(bf16)
        dk[i] = turn_back(nn(ds, qs[i]), cosk[...], sink[...]).astype(bf16)
        dv[i] = nn(probs_b, g_b).astype(bf16)
        dq = tn(keys, ds).T * HEAD_DIM**-0.5
        for g in range(GROUP):
            dqp[
                pl.ds(pl.multiple_of(b * ROWS, ROWS), ROWS),
                pl.ds(pl.multiple_of((h * GROUP + g) * 128, 128), 128),
            ] = turn_back(dq[g * ROWS : (g + 1) * ROWS], cosq[...], sinq[...]).astype(bf16)
        return carry

    lax.fori_loop(0, PAIRS, attend, 0, unroll=True)
    for c in range(N_CTX):
        at = slice(c * ROWS, (c + 1) * ROWS)
        for b in range(BATCH):
            k = [dk[b * 3 + h, at, :] for h in range(3)]
            v = [dv[b * 3 + h, at, :] for h in range(3)]
            dkv[c, b * ROWS : (b + 1) * ROWS, :] = jnp.concatenate(
                [k[0] + k[1], k[2] + v[0], v[1] + v[2]], axis=1
            )


def project_grads_kernel(
    dkv, dqp, nrow, xall, xown, gain, wq, wkv, pr, sq, gain_grad,
    query_part, keep, give,
    dw, raw,
):
    dw[...] = jnp.zeros(dw.shape, f32)

    def one(c, term):
        x = xall[c].astype(f32)
        scaled = x * rho_of(x)
        packed = dkv[c]
        dw[...] += tn((scaled * gain[...]).astype(bf16), packed)
        return term + jnp.sum(nt(packed, wkv[...]) * scaled, axis=0, keepdims=True)

    term = lax.fori_loop(0, N_CTX, one, jnp.zeros((1, D), f32))
    dq = dqp[...]
    part = nt(dq, wq[...])
    query_part[...] = part
    x = xown[...].astype(f32)
    term = term + jnp.sum(part * (x * rho_of(x)), axis=0, keepdims=True)
    rows = tn(pr[...], dw[...].astype(bf16)).astype(bf16)
    raw[...] = tn(nrow[...], nt(dq, sq[:, :PAD_Q]).astype(bf16)) + nt(rows, sq[:, PAD_Q:])
    row = lax.broadcasted_iota(jnp.int32, (16, 128), 0)
    ends = jnp.zeros((16, 128), f32)
    for n, values in enumerate((term, gain_grad[...])):
        wide = jnp.concatenate([values, jnp.zeros((1, 64), f32)], axis=1)
        for j in range(5):
            ends = jnp.where(row == 4 + n * 5 + j, wide[:, j * 128 : (j + 1) * 128], ends)
    for who, ref in enumerate((keep, give)):
        for zx in range(N_ZX):
            at = who * HALF + zx * SLOT_ROWS
            for c in range(N_CTX):
                values = raw[at : at + SLOT_ROWS, c * 128 : (c + 1) * 128]
                ref[c * N_ZX + zx] = jnp.concatenate(
                    [values[:32], values[32:] + ends], axis=0
                ).astype(bf16)


def input_kernel(dkv, query_part, xown, gain, wkv, middle_grad, out):
    total = dkv[0].astype(f32)
    for c in range(1, N_CTX):
        total = total + dkv[c].astype(f32)
    normed_grad = query_part[...] + nt(total.astype(bf16), wkv[...])
    grad, _ = norm_back(xown[...].astype(f32), gain[...], normed_grad)
    out[...] = middle_grad[...] + grad


def call(kernel, outs, scratch, *args, place=None):
    specs = [pl.BlockSpec(memory_space=pltpu.VMEM)] * len(args)
    if place is not None:
        specs = [pl.BlockSpec(memory_space=pltpu.SMEM)] + specs
        args = (place,) + args
    shapes = [jax.ShapeDtypeStruct(s, t) for s, t in outs]
    return pl.pallas_call(
        kernel,
        out_shape=shapes,
        in_specs=specs,
        out_specs=[pl.BlockSpec(memory_space=pltpu.VMEM)] * len(shapes),
        scratch_shapes=[pltpu.VMEM(s, t) for s, t in scratch],
        compiler_params=pltpu.CompilerParams(vmem_limit_bytes=60 * 1024 * 1024),
        cost_estimate=pl.CostEstimate(flops=1, bytes_accessed=1, transcendentals=0),
    )(*args)


def rotary_tables(positions):
    inverse_freq = theta ** (-(jnp.arange(HEAD_DIM // 2, dtype=f32) * 2.0) / HEAD_DIM)
    angles = positions.astype(f32)[:, None] * inverse_freq[None, :]
    return (
        jnp.concatenate([jnp.cos(angles)] * 4, axis=-1),
        jnp.concatenate([jnp.sin(angles)] * 4, axis=-1),
    )


def placements(core):
    def ones(rows, columns, wanted):
        return (wanted[:, None] == jnp.arange(columns)[None, :]).astype(bf16)

    def row(n):
        dp = n // 36
        return (dp % 2 ^ core) * HALF + dp // 2 * SLOT_ROWS + n % 36

    pr = ones(D, PAD_D, row(jnp.arange(D)))
    raw = jnp.arange(RAW)
    c, l = raw // 128, raw % 128
    q = jnp.where(l < 72, c * 72 + l, -1)
    k = jnp.where((l >= 72) & (l < 96), c * 24 + l - 72, -1)
    v = jnp.where((l >= 96) & (l < 120), c * 24 + l - 96, -1)
    head = q // HEAD_DIM
    upper = head // GROUP % 2
    padded = jnp.where(q < 0, -1, head * 128 + upper * HEAD_DIM + q % HEAD_DIM)
    target = jnp.where(k >= 0, PAD_Q + k, jnp.where(v >= 0, PAD_Q + KV + v, padded))
    sq = ones(RAW, PAD_Q + 2 * KV, target)
    so = ones(RAW, D, q)
    place = jnp.arange(PAD_Q)
    head, l = place // 128, place % 128
    upper = 1 - head // GROUP % 2
    inside = l // HEAD_DIM == upper
    n = head * HEAD_DIM + l % HEAD_DIM
    po = ones(PAD_Q, PAD_D, jnp.where(inside, row(n), -1))
    return pr, sq, so, po


def exchange(slots):
    return lax.all_to_all(slots, EVERY, 0, 0, tiled=True, axis_index_groups=SAME_CORE)


def swap(x):
    return lax.ppermute(x, EVERY, OTHER_CORE)


def pad_rows(x):
    return jnp.pad(x, ((0, SLOT_ROWS - x.shape[0]), (0, 0)))


def body(
    inputs,
    segments,
    cotangent,
    attention_gain,
    query_weight,
    key_weight,
    value_weight,
    out_weight,
    swiglu_gain,
    gate_weight,
    up_weight,
    down_weight,
):
    ctx, dp = lax.axis_index("ctx"), lax.axis_index("dp")
    place = jnp.stack([dp % 2, ctx, dp // 2]).astype(jnp.int32)
    down = down_weight[0]
    gate, up = gate_weight[0], up_weight[0]
    zero = functools.partial(jnp.zeros, dtype=bf16)
    head = jnp.concatenate(
        [
            jnp.concatenate([query_weight[0], key_weight[0], value_weight[0], zero((36, 8))], axis=1),
            segments.astype(bf16),
            zero((10, 128)),
        ],
        axis=0,
    )
    head_mine = exchange(jnp.broadcast_to(head[None], (SLOTS, SLOT_ROWS, 128)))
    main = jnp.concatenate([down[:48, :64], down[48:, :64]], axis=1)
    extra = jnp.concatenate([down[:48, 64:], down[48:, 64:]], axis=1)
    feed = jnp.concatenate(
        [
            jnp.concatenate(
                [
                    out_weight[0],
                    extra[:36],
                    jnp.concatenate([extra[36:], zero((24, 16))], axis=0),
                    zero((36, 24)),
                    gate[:, :128],
                    up[:, :128],
                    gate[:, 128:],
                    up[:, 128:],
                ],
                axis=1,
            ),
            jnp.concatenate([main[12 * j : 12 * j + 12] for j in range(4)], axis=1),
        ],
        axis=0,
    )
    xown = inputs.reshape(OWN, D)
    cot = cotangent.reshape(OWN, D)
    sent, head_mine = lax.optimization_barrier(
        (jnp.broadcast_to(xown[None], (N_CTX, OWN, D)), head_mine)
    )
    head_other = swap(head_mine)
    xall = lax.all_to_all(sent, "ctx", 0, 0, tiled=True)
    cosk, sink = rotary_tables(jnp.arange(SEQ, dtype=jnp.int32))
    cosq, sinq = rotary_tables(ctx * ROWS + jnp.arange(ROWS, dtype=jnp.int32))
    pr, sq, so, po = placements(dp % 2)
    slots = jnp.broadcast_to(feed[None], (SLOTS, SLOT_ROWS, 512))
    slots, xall, head_other, cosk, sink, cosq, sinq, pr, sq, so, po = lax.optimization_barrier(
        (slots, xall, head_other, cosk, sink, cosq, sinq, pr, sq, so, po)
    )
    feed_mine = exchange(slots)

    wq, wkv, nrow, qs, kvs, pt, mixr = call(
        attend_kernel,
        [
            ((D, PAD_Q), bf16),
            ((D, 2 * KV), bf16),
            ((OWN, PAD_D), bf16),
            ((PAIRS, STACK, 128), bf16),
            ((BATCH, SEQ, 2 * KV), bf16),
            ((PAIRS, SEQ, STACK), bf16),
            ((OWN, PAD_D), bf16),
        ],
        [
            ((PAD_D, RAW), bf16),
            ((D, RAW), bf16),
            ((BATCH, SEQ, ROWS), f32),
            ((OWN, PAD_Q), bf16),
        ],
        head_mine, head_other, xall, xown, attention_gain, segments.astype(f32),
        cosk, sink, cosq, sinq, pr, sq, po,
        place=place,
    )
    feed_mine, mixr = lax.optimization_barrier((feed_mine, mixr))
    feed_other = swap(feed_mine)
    down_mine, wo = call(
        unpack_kernel,
        [((HALF * 2, RAW), bf16), ((HALF, D), bf16)],
        [((HALF, RAW), bf16)],
        feed_mine, so,
    )

    result, gs, acts, middle_grad, gain_grad = call(
        feed_kernel,
        [
            ((OWN, D), bf16),
            ((PAIRS, STACK, 128), bf16),
            ((OWN, ACTS), bf16),
            ((OWN, D), f32),
            ((1, D), f32),
        ],
        [
            ((FF, RAW), bf16),
            ((HALF, RAW), bf16),
            ((HALF * 2, RAW), bf16),
            ((HALF, D), bf16),
        ],
        feed_mine, feed_other, down_mine, xown, mixr, cot, swiglu_gain, wo, pr, so, po,
        place=place,
    )
    acts_other = swap(acts)
    dkv, dqp = call(
        backward_kernel,
        [((N_CTX, OWN, 2 * KV), bf16), ((OWN, PAD_Q), bf16)],
        [((PAIRS, SEQ, 128), bf16), ((PAIRS, SEQ, 128), bf16)],
        pt, qs, kvs, gs, cosk, sink, cosq, sinq,
    )
    dkv_came = lax.all_to_all(dkv, "ctx", 0, 0, tiled=True)
    acts_other, dkv = lax.optimization_barrier((acts_other, dkv))
    (slots,) = call(
        terms_kernel,
        [((SLOTS, SLOT_ROWS, 640), bf16)],
        [((HALF, RAW), f32), ((FF, RAW), bf16)],
        acts, acts_other,
        place=place,
    )
    query_part, keep, give = call(
        project_grads_kernel,
        [
            ((OWN, D), f32),
            ((SLOTS, SLOT_ROWS, 128), bf16),
            ((SLOTS, SLOT_ROWS, 128), bf16),
        ],
        [((D, 2 * KV), f32), ((PAD_D, RAW), f32)],
        dkv, dqp, nrow, xall, xown, attention_gain, wq, wkv, pr, sq, gain_grad,
    )
    keep, give, slots, dkv_came = lax.optimization_barrier((keep, give, slots, dkv_came))
    head_sum = (keep.astype(f32) + swap(give).astype(f32)).astype(bf16)
    came = exchange(lax.dynamic_update_slice(slots, head_sum, (0, 0, 0)))
    (input_grad,) = call(
        input_kernel,
        [((OWN, D), f32)],
        [],
        dkv_came, query_part, xown, attention_gain, wkv, middle_grad,
    )

    total = jnp.sum(came.astype(f32), axis=0)
    qkv, rest = total[:, :128], total[:, 128:]
    first_total = qkv[36:41].reshape(1, 640)[:, :D]
    second_total = qkv[41:46].reshape(1, 640)[:, :D]
    gu = rest[:36, 128:]
    gate_total = jnp.concatenate([gu[:, :128], gu[:, 256:320]], axis=1)
    up_total = jnp.concatenate([gu[:, 128:256], gu[:, 320:]], axis=1)
    main = jnp.concatenate([rest[36:, j * 128 : (j + 1) * 128] for j in range(4)], axis=0)
    extra = jnp.concatenate([rest[:36, 72:88], rest[:12, 88:104]], axis=0)
    down_total = jnp.concatenate(
        [
            jnp.concatenate([main[:, :64], extra[:, :8]], axis=1),
            jnp.concatenate([main[:, 64:], extra[:, 8:]], axis=1),
        ],
        axis=0,
    )
    return (
        result.reshape(BATCH, ROWS, D),
        input_grad.reshape(BATCH, ROWS, D),
        first_total,
        qkv[None, :36, :72],
        qkv[None, :36, 72:96],
        qkv[None, :36, 96:120],
        rest[None, :36, :72],
        second_total,
        gate_total[None],
        up_total[None],
        down_total[None],
    )


def solution(mesh):
    weight = P(None, "dp", "ctx")
    rows = P("dp", "ctx", None)
    return jax.shard_map(
        body,
        mesh=mesh,
        in_specs=(rows, P("dp", "ctx"), rows, P(), weight, weight, weight, weight, P(), weight, weight, weight),
        out_specs=(rows, rows, P(), weight, weight, weight, weight, P(), weight, weight, weight),
        check_vma=False,
    )
```

```python
import functools

import jax
import jax.numpy as jnp
from jax import lax
from jax.experimental import pallas as pl
from jax.experimental.pallas import tpu as pltpu
from jax.sharding import PartitionSpec as P

HEADS = 9
KV_HEADS = 3
HEAD_DIM = 64
GROUP = HEADS // KV_HEADS
D = 576
FF = 1536
KV = KV_HEADS * HEAD_DIM
BATCH = 2
ROWS = 128
SEQ = 1024
OWN = BATCH * ROWS
ALL = BATCH * SEQ
N_CTX = 8
N_DP = 16
N_ZX = N_DP // 2
SLOTS = N_CTX * N_ZX
SLOT_ROWS = 48
HALF = N_ZX * SLOT_ROWS
PAD_D = 2 * HALF
RAW = N_CTX * 128
PAD_Q = HEADS * 128
STACK = GROUP * ROWS
AT_SECOND, AT_FEED, AT_INNER, AT_E, AT_MIDDLE, AT_MIXED, ACTS = 0, 768, 3840, 5376, 6400, 7424, 8192
PAIRS = BATCH * KV_HEADS

eps = 1e-05
theta = 10000.0
masked = -1e30
bf16 = jnp.bfloat16
f32 = jnp.float32

EVERY = ("dp", "ctx")
SAME_CORE = [
    [(zx * 2 + core) * N_CTX + ctx for ctx in range(N_CTX) for zx in range(N_ZX)]
    for core in range(2)
]
OTHER_CORE = [
    (dp * N_CTX + ctx, (dp ^ 1) * N_CTX + ctx) for dp in range(N_DP) for ctx in range(N_CTX)
]


def nn(left, right):
    return jnp.dot(left, right, preferred_element_type=f32)


def tn(left, right):
    return lax.dot_general(left, right, (((0,), (0,)), ((), ())), preferred_element_type=f32)


def nt(left, right):
    return lax.dot_general(left, right, (((1,), (1,)), ((), ())), preferred_element_type=f32)


def halves(x):
    high = x.astype(bf16)
    return high, (x - high.astype(f32)).astype(bf16)


def rho_of(x):
    return lax.rsqrt(jnp.mean(x * x, axis=-1, keepdims=True) + eps)


def norm_back(x, gain, c):
    rho = rho_of(x)
    w = c * gain
    grad = rho * (w - x * (rho * rho * jnp.mean(w * x, axis=-1, keepdims=True)))
    return grad, jnp.sum(c * (x * rho), axis=0, keepdims=True)


def lanes(shape):
    return lax.broadcasted_iota(jnp.int32, shape, 1)


def turn(x, cosine, sine):
    first = lanes(x.shape) % HEAD_DIM < HEAD_DIM // 2
    turned = jnp.where(first, -pltpu.roll(x, 96, 1), pltpu.roll(x, 32, 1))
    return x * cosine + turned * sine


def turn_back(x, cosine, sine):
    first = lanes(x.shape) % HEAD_DIM < HEAD_DIM // 2
    w = x * sine
    turned = jnp.where(first, pltpu.roll(w, 96, 1), -pltpu.roll(w, 32, 1))
    return x * cosine + turned


def triple(x, axis):
    return jnp.concatenate([x] * GROUP, axis=axis)


def block(ref, c, start, width):
    return ref[c * N_ZX : (c + 1) * N_ZX, :, start : start + width].reshape(HALF, width)


def hidden_place(unit):
    n = unit * 16
    c, m = divmod(n, 192)
    base = (c // 2) * 384
    if m < 128:
        return base + (c % 2) * 128 + m
    return base + 256 + (c % 2) * 64 + (m - 128)


def attend_kernel(
    place, mine, other, xall, xown, gain, segq, cosk, sink, cosq, sinq, pr, sq, po,
    wq, wkv, nrow, qs, kvs, pt, mixr, xrow,
    raw, wmid, bias, mixp,
):
    ctx, zx_own = place[1], place[2]
    for c in range(N_CTX):
        raw[:HALF, c * 128 : (c + 1) * 128] = block(mine, c, 0, 128)
        raw[HALF:, c * 128 : (c + 1) * 128] = block(other, c, 0, 128)
    wmid[...] = nn(pr[...], raw[...]).astype(bf16)
    wkv[...] = nn(wmid[...], sq[:, PAD_Q:]).astype(bf16)
    wq[...] = nn(wmid[...], sq[:, :PAD_Q]).astype(bf16)

    x = xown[...].astype(f32)
    normed = (x * rho_of(x) * gain[...]).astype(bf16)
    nrow[...] = nn(normed, pr[...]).astype(bf16)
    pre = nn(normed, wq[...])
    for head in range(HEADS):
        h, g = divmod(head, GROUP)
        for b in range(BATCH):
            turned = turn(
                pre[b * ROWS : (b + 1) * ROWS, head * 128 : (head + 1) * 128], cosq[...], sinq[...]
            )
            qs[b * KV_HEADS + h, g * ROWS : (g + 1) * ROWS, :] = (
                turned.astype(bf16) * bf16(HEAD_DIM**-0.5)
            )

    low = lanes((ROWS, 128)) < HEAD_DIM

    def project(c, carry):
        at = pl.multiple_of(c * ROWS, ROWS)
        x = jnp.concatenate([xall[c, b].astype(f32).T for b in range(BATCH)], axis=0)
        xrow[c] = x.astype(bf16)
        normed = (x * rho_of(x) * gain[...]).astype(bf16)
        pre = nn(normed, wkv[...])
        cosine, sine = cosk[pl.ds(at, ROWS), :], sink[pl.ds(at, ROWS), :]
        ends = mine[c * N_ZX + zx_own][32:].astype(f32)
        for b in range(BATCH):
            rows = pre[b * ROWS : (b + 1) * ROWS]
            tile = rows[:, 128:256]
            kvs[b, pl.ds(at, ROWS), :128] = turn(rows[:, :128], cosine, sine).astype(bf16)
            kvs[b, pl.ds(at, ROWS), 128:256] = jnp.where(
                low, turn(tile, cosine, sine), tile
            ).astype(bf16)
            kvs[b, pl.ds(at, ROWS), 256:] = rows[:, 256:].astype(bf16)
            keys = jnp.broadcast_to(ends[4 + b : 5 + b, :], (ROWS, ROWS)).T
            key_pos = c * ROWS + lax.broadcasted_iota(jnp.int32, (ROWS, ROWS), 0)
            query_pos = ctx * ROWS + lanes((ROWS, ROWS))
            allowed = (keys == segq[b : b + 1, :]) & (key_pos <= query_pos)
            bias[b, pl.ds(at, ROWS), :] = jnp.where(allowed, 0.0, masked)
        return carry

    lax.fori_loop(0, N_CTX, project, 0)

    def attend(i, carry):
        b = i // KV_HEADS
        h = i - b * KV_HEADS
        keys = kvs[b, :, pl.ds(pl.multiple_of(h // 2 * 128, 128), 128)]
        values = kvs[b, :, pl.ds(pl.multiple_of((h + 3) // 2 * 128, 128), 128)]
        scores = nt(keys, qs[i]) + triple(bias[b], 1)
        top = jnp.max(scores, axis=0, keepdims=True)
        expo = jnp.exp(scores - top)
        total = jnp.sum(expo, axis=0, keepdims=True)
        probs = (expo * (1.0 / total)).astype(bf16)
        pt[i] = probs
        mixed = tn(values, probs).T.astype(bf16)
        for g in range(GROUP):
            mixp[
                pl.ds(pl.multiple_of(b * ROWS, ROWS), ROWS),
                pl.ds(pl.multiple_of((h * GROUP + g) * 128, 128), 128),
            ] = mixed[g * ROWS : (g + 1) * ROWS]
        return carry

    lax.fori_loop(0, PAIRS, attend, 0)
    mixr[...] = nn(mixp[...], po[...]).astype(bf16)


def unpack(mine, down, oraw):
    lane = lanes((SLOT_ROWS, 128))
    for c in range(N_CTX):
        oraw[:, c * 128 : (c + 1) * 128] = block(mine, c, 0, 128)

    def one(zx, carry):
        at = pl.multiple_of(zx * 96, 96)
        for c in range(N_CTX):
            o = mine[c * N_ZX + zx, :, :128].astype(f32)
            t = jnp.concatenate(
                [o[36:]]
                + [
                    mine[c * N_ZX + zx, 32:, j * 128 : (j + 1) * 128].astype(f32)[4:]
                    for j in range(1, 4)
                ],
                axis=0,
            )
            e = jnp.concatenate([o[:36], pltpu.roll(o[:16], 112, 1)[:12]], axis=0)
            first = jnp.where(lane < 64, t, jnp.where(lane < 72, pltpu.roll(e, 120, 1), 0.0))
            second = jnp.where(
                lane < 64,
                pltpu.roll(t, 64, 1),
                jnp.where(lane < 72, pltpu.roll(e, 112, 1), 0.0),
            )
            down[pl.ds(at, 96), c * 128 : (c + 1) * 128] = jnp.concatenate(
                [first, second], axis=0
            ).astype(bf16)
        return carry

    lax.fori_loop(0, N_ZX, one, 0)


def unpack_kernel(mine, so, down, wo, oraw):
    unpack(mine, down, oraw)
    wo[...] = nn(oraw[...], so[...]).astype(bf16)


def place_of(c, odd_dp, n):
    m = odd_dp * 96 + n
    base = (c // 2) * 384
    at = jnp.where(m < 128, base + c % 2 * 128 + m, base + 256 + c % 2 * 64 + (m - 128))
    return pl.multiple_of(at, 16)


def feed_kernel(
    place, mine, other, down_mine, xown, mixr, cot, gain, wo, pr, so, po,
    result, gs, acts, middle_grad, gain_grad,
    down, oraw, down_other, wo_other,
):
    core = place[0]
    unpack(other, down_other, oraw)
    wo_other[...] = nn(oraw[...], so[...]).astype(bf16)
    for who, ref in enumerate((down_mine, down_other)):
        for zx in range(N_ZX):
            for n in range(0, 96, 16):
                down[pl.ds(place_of(zx, who ^ core, n), 16), :] = ref[
                    zx * 96 + n : zx * 96 + n + 16, :
                ]
    mixed_r = mixr[...]
    mid = xown[...].astype(f32) + (
        nn(mixed_r[:, :HALF], wo[...]) + nn(mixed_r[:, HALF:], wo_other[...])
    )
    rho = rho_of(mid)
    second = (mid * rho * gain[...]).astype(bf16)
    second_r = nn(second, pr[...]).astype(bf16)
    e_b = cot[...]
    e_raw = nt(e_b, so[...]).astype(bf16)
    acts[:, AT_SECOND:AT_FEED] = second_r
    acts[:, AT_E:AT_MIDDLE] = e_raw
    acts[:, AT_MIXED:] = mixed_r
    low = lanes((OWN, 128)) < 64
    grad_sum = jnp.zeros((OWN, PAD_D), f32)
    result_sum = jnp.zeros((OWN, RAW), f32)
    for pair in range(N_CTX // 2):
        weights = [
            jnp.concatenate([block(ref, c, 128, 384) for ref in (mine, other)], axis=0)
            for c in (2 * pair, 2 * pair + 1)
        ]
        pre = [nn(second_r, weight) for weight in weights]
        a, u, t, a2, u2, t2 = (pre[i // 3][:, i % 3 * 128 : (i % 3 + 1) * 128] for i in range(6))
        gate = jnp.concatenate([a, a2, jnp.where(low, t, pltpu.roll(t2, 64, 1))], axis=1)
        up = jnp.concatenate([u, u2, jnp.where(low, pltpu.roll(t, 64, 1), t2)], axis=1)
        logistic = 1.0 / (1.0 + jnp.exp(-gate))
        silu = gate * logistic
        inner = (silu * up).astype(bf16)
        rows = down[pair * 384 : (pair + 1) * 384, :]
        result_sum += nn(inner, rows)
        inner_grad = nt(e_raw, rows)
        gate_grad = inner_grad * up * (logistic * (1.0 + gate * (1.0 - logistic)))
        up_grad = inner_grad * silu
        a, a2, gt = (gate_grad[:, i * 128 : (i + 1) * 128] for i in range(3))
        u, u2, ut = (up_grad[:, i * 128 : (i + 1) * 128] for i in range(3))
        t = jnp.where(low, gt, pltpu.roll(ut, 64, 1))
        t2 = jnp.where(low, pltpu.roll(gt, 64, 1), ut)
        for k, tiles in enumerate(((a, u, t), (a2, u2, t2))):
            grads = jnp.concatenate(tiles, axis=1).astype(bf16)
            grad_sum += nt(grads, weights[k])
            at = AT_FEED + (2 * pair + k) * 384
            acts[:, at : at + 384] = grads
        acts[:, AT_INNER + pair * 384 : AT_INNER + (pair + 1) * 384] = inner

    high, rest = halves(result_sum)
    result[...] = (mid + (nn(high, so[...]) + nn(rest, so[...]))).astype(bf16)
    high, rest = halves(grad_sum)
    second_grad = nt(high, pr[...]) + nt(rest, pr[...])
    norm_grad, gain_term = norm_back(mid, gain[...], second_grad)
    gain_grad[...] = gain_term
    total = e_b.astype(f32) + norm_grad
    middle_grad[...] = total
    middle_b = total.astype(bf16)
    acts[:, AT_MIDDLE:AT_MIXED] = nt(middle_b, so[...]).astype(bf16)
    back = jnp.concatenate([nt(middle_b, wo[...]), nt(middle_b, wo_other[...])], axis=1)
    back = nt(back.astype(bf16), po[...]).astype(bf16)
    for head in range(HEADS):
        h, g = divmod(head, GROUP)
        for b in range(BATCH):
            gs[b * KV_HEADS + h, g * ROWS : (g + 1) * ROWS, :] = back[
                b * ROWS : (b + 1) * ROWS, head * 128 : (head + 1) * 128
            ]


def terms_kernel(place, acts, acts_other, slots, d1, dd):
    core = place[0]

    def both(start, width):
        return jnp.concatenate(
            [acts[:, start : start + width], acts_other[:, start : start + width]], axis=0
        )

    def both_rows(start):
        own, other = start, start + HALF
        return jnp.concatenate(
            [acts[:, own : own + HALF], acts_other[:, other : other + HALF]], axis=0
        )

    slots[:, :, :128] = jnp.zeros((SLOTS, SLOT_ROWS, 128), bf16)
    left = both_rows(AT_SECOND)
    for c in range(N_CTX):
        terms = tn(left, both(AT_FEED + c * 384, 384)).astype(bf16)
        slots[c * N_ZX : (c + 1) * N_ZX, :, 256:] = terms.reshape(N_ZX, SLOT_ROWS, 384)
    d1[...] = tn(both_rows(AT_MIXED), both(AT_MIDDLE, RAW))
    e_raw = both(AT_E, RAW)
    for pair in range(N_CTX // 2):
        dd_pair = tn(both(AT_INNER + pair * 384, 384), e_raw).astype(bf16)
        for unit in range(pair * 24, pair * 24 + 24):
            at = hidden_place(unit) - pair * 384
            dd[unit * 16 : unit * 16 + 16, :] = dd_pair[at : at + 16, :]

    lane = lanes((SLOT_ROWS, 128))

    def pack(zx, carry):
        row = pl.multiple_of(zx * SLOT_ROWS, SLOT_ROWS)
        at = pl.multiple_of((2 * zx + core) * 96, 16)
        for c in range(N_CTX):
            slot = c * N_ZX + zx
            first = dd[pl.ds(at, 48), c * 128 : (c + 1) * 128].astype(f32)
            second = dd[pl.ds(at + 48, 48), c * 128 : (c + 1) * 128].astype(f32)
            t = jnp.where(lane < 64, first, pltpu.roll(second, 64, 1))
            own = d1[pl.ds(row, SLOT_ROWS), c * 128 : (c + 1) * 128]
            e = jnp.where(
                lane < 72,
                own,
                jnp.where(lane < 80, pltpu.roll(first, 8, 1), pltpu.roll(second, 16, 1)),
            )
            rest = pltpu.roll(e[32:], 16, 1)[4:]
            head = jnp.concatenate([rest, e[12:36]], axis=0)
            head = jnp.where(lane[:36] < 88, e[:36], jnp.where(lane[:36] < 104, head, 0.0))
            slots[slot, :, 128:256] = jnp.concatenate([head, t[:12]], axis=0).astype(bf16)
            for j in range(3):
                at_lane = 256 + j * 128
                g = slots[slot, 32:, at_lane : at_lane + 128].astype(f32)
                slots[slot, 32:, at_lane : at_lane + 128] = jnp.concatenate(
                    [g[:4], t[12 * j + 12 : 12 * j + 24]], axis=0
                ).astype(bf16)
        return carry

    lax.fori_loop(0, N_ZX, pack, 0)


def backward_kernel(
    pt, qs, kvs, gs, cosk, sink, cosq, sinq,
    dkv, dqp,
    dk, dv,
):
    def attend(i, carry):
        b = i // KV_HEADS
        h = i - b * KV_HEADS
        keys = kvs[b, :, pl.ds(pl.multiple_of(h // 2 * 128, 128), 128)]
        values = kvs[b, :, pl.ds(pl.multiple_of((h + 3) // 2 * 128, 128), 128)]
        g_b = gs[i]
        probs_b = pt[i]
        probs = probs_b.astype(f32)
        weighted = probs * nt(values, g_b)
        delta = jnp.sum(weighted, axis=0, keepdims=True)
        ds = (weighted - probs * delta).astype(bf16)
        dk[i] = turn_back(nn(ds, qs[i]), cosk[...], sink[...]).astype(bf16)
        dv[i] = nn(probs_b, g_b).astype(bf16)
        dq = tn(keys, ds).T * HEAD_DIM**-0.5
        for g in range(GROUP):
            dqp[
                pl.ds(pl.multiple_of(b * ROWS, ROWS), ROWS),
                pl.ds(pl.multiple_of((h * GROUP + g) * 128, 128), 128),
            ] = turn_back(dq[g * ROWS : (g + 1) * ROWS], cosq[...], sinq[...]).astype(bf16)
        return carry

    lax.fori_loop(0, PAIRS, attend, 0, unroll=True)
    for c in range(N_CTX):
        at = slice(c * ROWS, (c + 1) * ROWS)
        for b in range(BATCH):
            k = [dk[b * 3 + h, at, :] for h in range(3)]
            v = [dv[b * 3 + h, at, :] for h in range(3)]
            dkv[c, b * ROWS : (b + 1) * ROWS, :] = jnp.concatenate(
                [k[0] + k[1], k[2] + v[0], v[1] + v[2]], axis=1
            )


def project_grads_kernel(
    dkv, dqp, nrow, xall, xown, gain, wq, wkv, pr, sq, gain_grad,
    query_part, keep, give,
    dw, raw,
):
    dw[...] = jnp.zeros(dw.shape, f32)

    def one(c, term):
        x = xall[c].astype(f32)
        scaled = x * rho_of(x)
        packed = dkv[c]
        dw[...] += tn((scaled * gain[...]).astype(bf16), packed)
        return term + jnp.sum(nt(packed, wkv[...]) * scaled, axis=0, keepdims=True)

    term = lax.fori_loop(0, N_CTX, one, jnp.zeros((1, D), f32), unroll=True)
    dq = dqp[...]
    part = nt(dq, wq[...])
    query_part[...] = part
    x = xown[...].astype(f32)
    term = term + jnp.sum(part * (x * rho_of(x)), axis=0, keepdims=True)
    rows = tn(pr[...], dw[...].astype(bf16)).astype(bf16)
    raw[...] = tn(nrow[...], nt(dq, sq[:, :PAD_Q]).astype(bf16)) + nt(rows, sq[:, PAD_Q:])
    row = lax.broadcasted_iota(jnp.int32, (16, 128), 0)
    ends = jnp.zeros((16, 128), f32)
    for n, values in enumerate((term, gain_grad[...])):
        wide = jnp.concatenate([values, jnp.zeros((1, 64), f32)], axis=1)
        for j in range(5):
            ends = jnp.where(row == 4 + n * 5 + j, wide[:, j * 128 : (j + 1) * 128], ends)
    for who, ref in enumerate((keep, give)):
        for zx in range(N_ZX):
            at = who * HALF + zx * SLOT_ROWS
            for c in range(N_CTX):
                values = raw[at : at + SLOT_ROWS, c * 128 : (c + 1) * 128]
                ref[c * N_ZX + zx] = jnp.concatenate(
                    [values[:32], values[32:] + ends], axis=0
                ).astype(bf16)


def input_kernel(dkv, query_part, xown, gain, wkv, middle_grad, out):
    total = dkv[0].astype(f32)
    for c in range(1, N_CTX):
        total = total + dkv[c].astype(f32)
    normed_grad = query_part[...] + nt(total.astype(bf16), wkv[...])
    grad, _ = norm_back(xown[...].astype(f32), gain[...], normed_grad)
    out[...] = middle_grad[...] + grad


def spread_kernel(x, feed, sent, slots):
    for c in range(N_CTX):
        sent[c] = x[...]
    for n in range(SLOTS):
        slots[n] = feed[...]


def sum_kernel(
    came, first_gain, second_gain, query, key, value, out, gate, up, down, total
):
    step = pl.program_id(0)

    @pl.when(step == 0)
    def _():
        total[...] = jnp.zeros(total.shape, f32)

    total[...] += jnp.sum(came[...].astype(f32), axis=0)

    @pl.when(step == pl.num_programs(0) - 1)
    def _():
        def tile(n):
            return total[:, n * 128 : (n + 1) * 128]

        qkv, o = tile(0), tile(1)
        for n, ref in enumerate((first_gain, second_gain)):
            for j in range(5):
                width = min(128, D - j * 128)
                ref[:, j * 128 : j * 128 + width] = qkv[36 + n * 5 + j : 37 + n * 5 + j, :width]
        query[...] = qkv[:36, :72]
        out[...] = o[:36, :72]
        turned = jnp.concatenate([qkv, jnp.zeros((80, 128), f32)], axis=0).T
        key[...] = turned[72:96, :36]
        value[...] = turned[96:120, :36]
        a, b, t = (tile(n)[:36] for n in (2, 3, 4))
        gate[:, :128] = a
        gate[:, 128:] = t[:, :64]
        up[:, :128] = b
        up[:, 128:] = pltpu.roll(t, 64, 1)[:, :64]
        t = jnp.concatenate([tile(n)[36:] for n in range(1, 5)], axis=0)
        e = jnp.concatenate([o[:36], pltpu.roll(o[:16], 112, 1)[:12]], axis=0)
        low = lanes((SLOT_ROWS, 128)) < 64
        halves_of_down = [
            jnp.where(low, t, pltpu.roll(e, 120, 1)),
            jnp.where(low, pltpu.roll(t, 64, 1), pltpu.roll(e, 112, 1)),
            jnp.zeros((32, 128), f32),
        ]
        down[...] = jnp.concatenate(halves_of_down, axis=0).T[:72, :96]


def call(kernel, outs, scratch, *args, place=None):
    specs = [pl.BlockSpec(memory_space=pltpu.VMEM)] * len(args)
    if place is not None:
        specs = [pl.BlockSpec(memory_space=pltpu.SMEM)] + specs
        args = (place,) + args
    shapes = [jax.ShapeDtypeStruct(s, t) for s, t in outs]
    return pl.pallas_call(
        kernel,
        out_shape=shapes,
        in_specs=specs,
        out_specs=[pl.BlockSpec(memory_space=pltpu.VMEM)] * len(shapes),
        scratch_shapes=[pltpu.VMEM(s, t) for s, t in scratch],
        compiler_params=pltpu.CompilerParams(vmem_limit_bytes=60 * 1024 * 1024),
        cost_estimate=pl.CostEstimate(flops=1, bytes_accessed=1, transcendentals=0),
    )(*args)


def rotary_tables(positions):
    inverse_freq = theta ** (-(jnp.arange(HEAD_DIM // 2, dtype=f32) * 2.0) / HEAD_DIM)
    angles = positions.astype(f32)[:, None] * inverse_freq[None, :]
    return (
        jnp.concatenate([jnp.cos(angles)] * 4, axis=-1),
        jnp.concatenate([jnp.sin(angles)] * 4, axis=-1),
    )


def placements(core):
    def ones(rows, columns, wanted):
        return (wanted[:, None] == jnp.arange(columns)[None, :]).astype(bf16)

    def row(n):
        dp = n // 36
        return (dp % 2 ^ core) * HALF + dp // 2 * SLOT_ROWS + n % 36

    pr = ones(D, PAD_D, row(jnp.arange(D)))
    raw = jnp.arange(RAW)
    c, l = raw // 128, raw % 128
    q = jnp.where(l < 72, c * 72 + l, -1)
    k = jnp.where((l >= 72) & (l < 96), c * 24 + l - 72, -1)
    v = jnp.where((l >= 96) & (l < 120), c * 24 + l - 96, -1)
    head = q // HEAD_DIM
    upper = head // GROUP % 2
    padded = jnp.where(q < 0, -1, head * 128 + upper * HEAD_DIM + q % HEAD_DIM)
    target = jnp.where(k >= 0, PAD_Q + k, jnp.where(v >= 0, PAD_Q + KV + v, padded))
    sq = ones(RAW, PAD_Q + 2 * KV, target)
    so = ones(RAW, D, q)
    place = jnp.arange(PAD_Q)
    head, l = place // 128, place % 128
    upper = 1 - head // GROUP % 2
    inside = l // HEAD_DIM == upper
    n = head * HEAD_DIM + l % HEAD_DIM
    po = ones(PAD_Q, PAD_D, jnp.where(inside, row(n), -1))
    return pr, sq, so, po


def exchange(slots):
    return lax.all_to_all(slots, EVERY, 0, 0, tiled=True, axis_index_groups=SAME_CORE)


def swap(x):
    return lax.ppermute(x, EVERY, OTHER_CORE)


def pad_rows(x):
    return jnp.pad(x, ((0, SLOT_ROWS - x.shape[0]), (0, 0)))


def body(
    inputs,
    segments,
    cotangent,
    attention_gain,
    query_weight,
    key_weight,
    value_weight,
    out_weight,
    swiglu_gain,
    gate_weight,
    up_weight,
    down_weight,
):
    ctx, dp = lax.axis_index("ctx"), lax.axis_index("dp")
    place = jnp.stack([dp % 2, ctx, dp // 2]).astype(jnp.int32)
    down = down_weight[0]
    gate, up = gate_weight[0], up_weight[0]
    zero = functools.partial(jnp.zeros, dtype=bf16)
    head = jnp.concatenate(
        [
            jnp.concatenate([query_weight[0], key_weight[0], value_weight[0], zero((36, 8))], axis=1),
            segments.astype(bf16),
            zero((10, 128)),
        ],
        axis=0,
    )
    head_mine = exchange(jnp.broadcast_to(head[None], (SLOTS, SLOT_ROWS, 128)))
    main = jnp.concatenate([down[:48, :64], down[48:, :64]], axis=1)
    extra = jnp.concatenate([down[:48, 64:], down[48:, 64:]], axis=1)
    feed = jnp.concatenate(
        [
            jnp.concatenate(
                [
                    out_weight[0],
                    extra[:36],
                    jnp.concatenate([extra[36:], zero((24, 16))], axis=0),
                    zero((36, 24)),
                    gate[:, :128],
                    up[:, :128],
                    gate[:, 128:],
                    up[:, 128:],
                ],
                axis=1,
            ),
            jnp.concatenate([main[12 * j : 12 * j + 12] for j in range(4)], axis=1),
        ],
        axis=0,
    )
    xown = inputs.reshape(OWN, D)
    cot = cotangent.reshape(OWN, D)
    sent, slots = call(
        spread_kernel,
        [((N_CTX, BATCH, D, ROWS), bf16), ((SLOTS, SLOT_ROWS, 512), bf16)],
        [],
        inputs.transpose(0, 2, 1), feed,
    )
    sent, head_mine = lax.optimization_barrier((sent, head_mine))
    head_other = swap(head_mine)
    xall = lax.all_to_all(sent, "ctx", 0, 0, tiled=True)
    cosk, sink = rotary_tables(jnp.arange(SEQ, dtype=jnp.int32))
    cosq, sinq = rotary_tables(ctx * ROWS + jnp.arange(ROWS, dtype=jnp.int32))
    pr, sq, so, po = placements(dp % 2)
    slots, xall, head_other, cosk, sink, cosq, sinq, pr, sq, so, po = lax.optimization_barrier(
        (slots, xall, head_other, cosk, sink, cosq, sinq, pr, sq, so, po)
    )
    feed_mine = exchange(slots)

    wq, wkv, nrow, qs, kvs, pt, mixr, xrow = call(
        attend_kernel,
        [
            ((D, PAD_Q), bf16),
            ((D, 2 * KV), bf16),
            ((OWN, PAD_D), bf16),
            ((PAIRS, STACK, 128), bf16),
            ((BATCH, SEQ, 2 * KV), bf16),
            ((PAIRS, SEQ, STACK), bf16),
            ((OWN, PAD_D), bf16),
            ((N_CTX, OWN, D), bf16),
        ],
        [
            ((PAD_D, RAW), bf16),
            ((D, RAW), bf16),
            ((BATCH, SEQ, ROWS), f32),
            ((OWN, PAD_Q), bf16),
        ],
        head_mine, head_other, xall, xown, attention_gain, segments.astype(f32),
        cosk, sink, cosq, sinq, pr, sq, po,
        place=place,
    )
    feed_mine, mixr = lax.optimization_barrier((feed_mine, mixr))
    feed_other = swap(feed_mine)
    down_mine, wo = call(
        unpack_kernel,
        [((HALF * 2, RAW), bf16), ((HALF, D), bf16)],
        [((HALF, RAW), bf16)],
        feed_mine, so,
    )

    result, gs, acts, middle_grad, gain_grad = call(
        feed_kernel,
        [
            ((OWN, D), bf16),
            ((PAIRS, STACK, 128), bf16),
            ((OWN, ACTS), bf16),
            ((OWN, D), f32),
            ((1, D), f32),
        ],
        [
            ((FF, RAW), bf16),
            ((HALF, RAW), bf16),
            ((HALF * 2, RAW), bf16),
            ((HALF, D), bf16),
        ],
        feed_mine, feed_other, down_mine, xown, mixr, cot, swiglu_gain, wo, pr, so, po,
        place=place,
    )
    acts_other = swap(acts)
    dkv, dqp = call(
        backward_kernel,
        [((N_CTX, OWN, 2 * KV), bf16), ((OWN, PAD_Q), bf16)],
        [((PAIRS, SEQ, 128), bf16), ((PAIRS, SEQ, 128), bf16)],
        pt, qs, kvs, gs, cosk, sink, cosq, sinq,
    )
    dkv_came = lax.all_to_all(dkv, "ctx", 0, 0, tiled=True)
    acts_other, dkv = lax.optimization_barrier((acts_other, dkv))
    (slots,) = call(
        terms_kernel,
        [((SLOTS, SLOT_ROWS, 640), bf16)],
        [((HALF, RAW), f32), ((FF, RAW), bf16)],
        acts, acts_other,
        place=place,
    )
    query_part, keep, give = call(
        project_grads_kernel,
        [
            ((OWN, D), f32),
            ((SLOTS, SLOT_ROWS, 128), bf16),
            ((SLOTS, SLOT_ROWS, 128), bf16),
        ],
        [((D, 2 * KV), f32), ((PAD_D, RAW), f32)],
        dkv, dqp, nrow, xrow, xown, attention_gain, wq, wkv, pr, sq, gain_grad,
    )
    keep, give, slots, dkv_came = lax.optimization_barrier((keep, give, slots, dkv_came))
    head_sum = (keep.astype(f32) + swap(give).astype(f32)).astype(bf16)
    came = exchange(lax.dynamic_update_slice(slots, head_sum, (0, 0, 0)))
    (input_grad,) = call(
        input_kernel,
        [((OWN, D), f32)],
        [],
        dkv_came, query_part, xown, attention_gain, wkv, middle_grad,
    )

    first_total, second_total, query, key, value, out, gate_total, up_total, down_total = (
        pl.pallas_call(
            sum_kernel,
            grid=(4,),
            in_specs=[pl.BlockSpec((SLOTS // 4, SLOT_ROWS, 640), lambda i: (i, 0, 0))],
            out_specs=[pl.BlockSpec(memory_space=pltpu.VMEM)] * 9,
            out_shape=[
                jax.ShapeDtypeStruct(shape, f32)
                for shape in (
                    (1, D), (1, D), (36, 72), (24, 36), (24, 36), (36, 72), (36, 192), (36, 192), (72, 96),
                )
            ],
            scratch_shapes=[pltpu.VMEM((SLOT_ROWS, 640), f32)],
            compiler_params=pltpu.CompilerParams(vmem_limit_bytes=16 * 1024 * 1024),
        )(came)
    )
    return (
        result.reshape(BATCH, ROWS, D),
        input_grad.reshape(BATCH, ROWS, D),
        first_total,
        query[None],
        key.T[None],
        value.T[None],
        out[None],
        second_total,
        gate_total[None],
        up_total[None],
        down_total.T[None],
    )


def solution(mesh):
    weight = P(None, "dp", "ctx")
    rows = P("dp", "ctx", None)
    return jax.shard_map(
        body,
        mesh=mesh,
        in_specs=(rows, P("dp", "ctx"), rows, P(), weight, weight, weight, weight, P(), weight, weight, weight),
        out_specs=(rows, rows, P(), weight, weight, weight, weight, P(), weight, weight, weight),
        check_vma=False,
    )
```

```python
import functools

import jax
import jax.numpy as jnp
from jax import lax
from jax.experimental import pallas as pl
from jax.experimental.pallas import tpu as pltpu
from jax.sharding import PartitionSpec as P

HEADS = 9
KV_HEADS = 3
HEAD_DIM = 64
GROUP = HEADS // KV_HEADS
D = 576
FF = 1536
KV = KV_HEADS * HEAD_DIM
BATCH = 2
ROWS = 128
SEQ = 1024
OWN = BATCH * ROWS
ALL = BATCH * SEQ
N_CTX = 8
N_DP = 16
N_ZX = N_DP // 2
SLOTS = N_CTX * N_ZX
SLOT_ROWS = 48
HALF = N_ZX * SLOT_ROWS
PAD_D = 2 * HALF
RAW = N_CTX * 128
PAD_Q = HEADS * 128
STACK = GROUP * ROWS
AT_SECOND, AT_FEED, AT_INNER, AT_E, AT_MIDDLE, AT_MIXED, ACTS = 0, 768, 3840, 5376, 6400, 7424, 8192
PAIRS = BATCH * KV_HEADS

eps = 1e-05
theta = 10000.0
masked = -1e30
bf16 = jnp.bfloat16
f32 = jnp.float32

EVERY = ("dp", "ctx")
SAME_CORE = [
    [(zx * 2 + core) * N_CTX + ctx for ctx in range(N_CTX) for zx in range(N_ZX)]
    for core in range(2)
]
OTHER_CORE = [
    (dp * N_CTX + ctx, (dp ^ 1) * N_CTX + ctx) for dp in range(N_DP) for ctx in range(N_CTX)
]


def nn(left, right):
    return jnp.dot(left, right, preferred_element_type=f32)


def tn(left, right):
    return lax.dot_general(left, right, (((0,), (0,)), ((), ())), preferred_element_type=f32)


def nt(left, right):
    return lax.dot_general(left, right, (((1,), (1,)), ((), ())), preferred_element_type=f32)


def halves(x):
    high = x.astype(bf16)
    return high, (x - high.astype(f32)).astype(bf16)


def rho_of(x):
    return lax.rsqrt(jnp.mean(x * x, axis=-1, keepdims=True) + eps)


def norm_back(x, gain, c):
    rho = rho_of(x)
    w = c * gain
    grad = rho * (w - x * (rho * rho * jnp.mean(w * x, axis=-1, keepdims=True)))
    return grad, jnp.sum(c * (x * rho), axis=0, keepdims=True)


def lanes(shape):
    return lax.broadcasted_iota(jnp.int32, shape, 1)


def turn(x, cosine, sine):
    first = lanes(x.shape) % HEAD_DIM < HEAD_DIM // 2
    turned = jnp.where(first, -pltpu.roll(x, 96, 1), pltpu.roll(x, 32, 1))
    return x * cosine + turned * sine


def turn_back(x, cosine, sine):
    first = lanes(x.shape) % HEAD_DIM < HEAD_DIM // 2
    w = x * sine
    turned = jnp.where(first, pltpu.roll(w, 96, 1), -pltpu.roll(w, 32, 1))
    return x * cosine + turned


def triple(x, axis):
    return jnp.concatenate([x] * GROUP, axis=axis)


def block(ref, c, start, width):
    return ref[c * N_ZX : (c + 1) * N_ZX, :, start : start + width].reshape(HALF, width)


def hidden_place(unit):
    n = unit * 16
    c, m = divmod(n, 192)
    base = (c // 2) * 384
    if m < 128:
        return base + (c % 2) * 128 + m
    return base + 256 + (c % 2) * 64 + (m - 128)


def attend_kernel(
    place, mine, other, xall, xown, gain, segq, cosk, sink, cosq, sinq, pr, sq, po,
    wq, wkv, nrow, qs, kvs, pt, mixr, xrow,
    raw, wmid, bias, mixp,
):
    ctx, zx_own = place[1], place[2]
    for c in range(N_CTX):
        raw[:HALF, c * 128 : (c + 1) * 128] = block(mine, c, 0, 128)
        raw[HALF:, c * 128 : (c + 1) * 128] = block(other, c, 0, 128)
    wmid[...] = nn(pr[...], raw[...]).astype(bf16)
    wkv[...] = nn(wmid[...], sq[:, PAD_Q:]).astype(bf16)
    wq[...] = nn(wmid[...], sq[:, :PAD_Q]).astype(bf16)

    x = xown[...].astype(f32)
    normed = (x * rho_of(x) * gain[...]).astype(bf16)
    nrow[...] = nn(normed, pr[...]).astype(bf16)
    pre = nn(normed, wq[...])
    for head in range(HEADS):
        h, g = divmod(head, GROUP)
        for b in range(BATCH):
            turned = turn(
                pre[b * ROWS : (b + 1) * ROWS, head * 128 : (head + 1) * 128], cosq[...], sinq[...]
            )
            qs[b * KV_HEADS + h, g * ROWS : (g + 1) * ROWS, :] = (
                turned.astype(bf16) * bf16(HEAD_DIM**-0.5)
            )

    low = lanes((ROWS, 128)) < HEAD_DIM

    def project(c, carry):
        at = pl.multiple_of(c * ROWS, ROWS)
        x = jnp.concatenate([xall[c, b].astype(f32).T for b in range(BATCH)], axis=0)
        xrow[c] = x.astype(bf16)
        normed = (x * rho_of(x) * gain[...]).astype(bf16)
        pre = nn(normed, wkv[...])
        cosine, sine = cosk[pl.ds(at, ROWS), :], sink[pl.ds(at, ROWS), :]
        ends = mine[c * N_ZX + zx_own][32:].astype(f32)
        for b in range(BATCH):
            rows = pre[b * ROWS : (b + 1) * ROWS]
            tile = rows[:, 128:256]
            kvs[b, pl.ds(at, ROWS), :128] = turn(rows[:, :128], cosine, sine).astype(bf16)
            kvs[b, pl.ds(at, ROWS), 128:256] = jnp.where(
                low, turn(tile, cosine, sine), tile
            ).astype(bf16)
            kvs[b, pl.ds(at, ROWS), 256:] = rows[:, 256:].astype(bf16)
            keys = jnp.broadcast_to(ends[4 + b : 5 + b, :], (ROWS, ROWS)).T
            key_pos = c * ROWS + lax.broadcasted_iota(jnp.int32, (ROWS, ROWS), 0)
            query_pos = ctx * ROWS + lanes((ROWS, ROWS))
            allowed = (keys == segq[b : b + 1, :]) & (key_pos <= query_pos)
            bias[b, pl.ds(at, ROWS), :] = jnp.where(allowed, 0.0, masked)
        return carry

    lax.fori_loop(0, N_CTX, project, 0)

    def attend(i, carry):
        b = i // KV_HEADS
        h = i - b * KV_HEADS
        keys = kvs[b, :, pl.ds(pl.multiple_of(h // 2 * 128, 128), 128)]
        values = kvs[b, :, pl.ds(pl.multiple_of((h + 3) // 2 * 128, 128), 128)]
        scores = nt(keys, qs[i]) + triple(bias[b], 1)
        top = jnp.max(scores, axis=0, keepdims=True)
        expo = jnp.exp(scores - top)
        total = jnp.sum(expo, axis=0, keepdims=True)
        probs = (expo * (1.0 / total)).astype(bf16)
        pt[i] = probs
        mixed = tn(values, probs).T.astype(bf16)
        for g in range(GROUP):
            mixp[
                pl.ds(pl.multiple_of(b * ROWS, ROWS), ROWS),
                pl.ds(pl.multiple_of((h * GROUP + g) * 128, 128), 128),
            ] = mixed[g * ROWS : (g + 1) * ROWS]
        return carry

    lax.fori_loop(0, PAIRS, attend, 0)
    mixr[...] = nn(mixp[...], po[...]).astype(bf16)


def unpack(mine, down, oraw):
    lane = lanes((SLOT_ROWS, 128))
    for c in range(N_CTX):
        oraw[:, c * 128 : (c + 1) * 128] = block(mine, c, 0, 128)

    def one(zx, carry):
        at = pl.multiple_of(zx * 96, 96)
        for c in range(N_CTX):
            o = mine[c * N_ZX + zx, :, :128].astype(f32)
            t = jnp.concatenate(
                [o[36:]]
                + [
                    mine[c * N_ZX + zx, 32:, j * 128 : (j + 1) * 128].astype(f32)[4:]
                    for j in range(1, 4)
                ],
                axis=0,
            )
            e = jnp.concatenate([o[:36], pltpu.roll(o[:16], 112, 1)[:12]], axis=0)
            first = jnp.where(lane < 64, t, jnp.where(lane < 72, pltpu.roll(e, 120, 1), 0.0))
            second = jnp.where(
                lane < 64,
                pltpu.roll(t, 64, 1),
                jnp.where(lane < 72, pltpu.roll(e, 112, 1), 0.0),
            )
            down[pl.ds(at, 96), c * 128 : (c + 1) * 128] = jnp.concatenate(
                [first, second], axis=0
            ).astype(bf16)
        return carry

    lax.fori_loop(0, N_ZX, one, 0)


def unpack_kernel(mine, so, down, wo, oraw):
    unpack(mine, down, oraw)
    wo[...] = nn(oraw[...], so[...]).astype(bf16)


def place_of(c, odd_dp, n):
    m = odd_dp * 96 + n
    base = (c // 2) * 384
    at = jnp.where(m < 128, base + c % 2 * 128 + m, base + 256 + c % 2 * 64 + (m - 128))
    return pl.multiple_of(at, 16)


def feed_kernel(
    place, mine, other, down_mine, xown, mixr, cot, gain, wo, pr, so, po,
    result, gs, acts, middle_grad, gain_grad,
    down, oraw, down_other, wo_other,
):
    core = place[0]
    unpack(other, down_other, oraw)
    wo_other[...] = nn(oraw[...], so[...]).astype(bf16)
    for who, ref in enumerate((down_mine, down_other)):
        for zx in range(N_ZX):
            for n in range(0, 96, 16):
                down[pl.ds(place_of(zx, who ^ core, n), 16), :] = ref[
                    zx * 96 + n : zx * 96 + n + 16, :
                ]
    mixed_r = mixr[...]
    mid = xown[...].astype(f32) + (
        nn(mixed_r[:, :HALF], wo[...]) + nn(mixed_r[:, HALF:], wo_other[...])
    )
    rho = rho_of(mid)
    second = (mid * rho * gain[...]).astype(bf16)
    second_r = nn(second, pr[...]).astype(bf16)
    e_b = cot[...]
    e_raw = nt(e_b, so[...]).astype(bf16)
    acts[:, AT_SECOND:AT_FEED] = second_r
    acts[:, AT_E:AT_MIDDLE] = e_raw
    acts[:, AT_MIXED:] = mixed_r
    low = lanes((OWN, 128)) < 64
    grad_sum = jnp.zeros((OWN, PAD_D), f32)
    result_sum = jnp.zeros((OWN, RAW), f32)
    for pair in range(N_CTX // 2):
        weights = [
            jnp.concatenate([block(ref, c, 128, 384) for ref in (mine, other)], axis=0)
            for c in (2 * pair, 2 * pair + 1)
        ]
        pre = [nn(second_r, weight) for weight in weights]
        a, u, t, a2, u2, t2 = (pre[i // 3][:, i % 3 * 128 : (i % 3 + 1) * 128] for i in range(6))
        gate = jnp.concatenate([a, a2, jnp.where(low, t, pltpu.roll(t2, 64, 1))], axis=1)
        up = jnp.concatenate([u, u2, jnp.where(low, pltpu.roll(t, 64, 1), t2)], axis=1)
        logistic = 1.0 / (1.0 + jnp.exp(-gate))
        silu = gate * logistic
        inner = (silu * up).astype(bf16)
        rows = down[pair * 384 : (pair + 1) * 384, :]
        result_sum += nn(inner, rows)
        inner_grad = nt(e_raw, rows)
        gate_grad = inner_grad * up * (logistic * (1.0 + gate * (1.0 - logistic)))
        up_grad = inner_grad * silu
        a, a2, gt = (gate_grad[:, i * 128 : (i + 1) * 128] for i in range(3))
        u, u2, ut = (up_grad[:, i * 128 : (i + 1) * 128] for i in range(3))
        t = jnp.where(low, gt, pltpu.roll(ut, 64, 1))
        t2 = jnp.where(low, pltpu.roll(gt, 64, 1), ut)
        for k, tiles in enumerate(((a, u, t), (a2, u2, t2))):
            grads = jnp.concatenate(tiles, axis=1).astype(bf16)
            grad_sum += nt(grads, weights[k])
            at = AT_FEED + (2 * pair + k) * 384
            acts[:, at : at + 384] = grads
        acts[:, AT_INNER + pair * 384 : AT_INNER + (pair + 1) * 384] = inner

    high, rest = halves(result_sum)
    result[...] = (mid + (nn(high, so[...]) + nn(rest, so[...]))).astype(bf16)
    high, rest = halves(grad_sum)
    second_grad = nt(high, pr[...]) + nt(rest, pr[...])
    norm_grad, gain_term = norm_back(mid, gain[...], second_grad)
    gain_grad[...] = gain_term
    total = e_b.astype(f32) + norm_grad
    middle_grad[...] = total
    middle_b = total.astype(bf16)
    acts[:, AT_MIDDLE:AT_MIXED] = nt(middle_b, so[...]).astype(bf16)
    back = jnp.concatenate([nt(middle_b, wo[...]), nt(middle_b, wo_other[...])], axis=1)
    back = nt(back.astype(bf16), po[...]).astype(bf16)
    for head in range(HEADS):
        h, g = divmod(head, GROUP)
        for b in range(BATCH):
            gs[b * KV_HEADS + h, g * ROWS : (g + 1) * ROWS, :] = back[
                b * ROWS : (b + 1) * ROWS, head * 128 : (head + 1) * 128
            ]


def terms_kernel(place, acts, acts_other, slots, d1, dd):
    core = place[0]

    def both(start, width):
        return jnp.concatenate(
            [acts[:, start : start + width], acts_other[:, start : start + width]], axis=0
        )

    def both_rows(start):
        own, other = start, start + HALF
        return jnp.concatenate(
            [acts[:, own : own + HALF], acts_other[:, other : other + HALF]], axis=0
        )

    slots[:, :, :128] = jnp.zeros((SLOTS, SLOT_ROWS, 128), bf16)
    left = both_rows(AT_SECOND)
    for c in range(N_CTX):
        terms = tn(left, both(AT_FEED + c * 384, 384)).astype(bf16)
        slots[c * N_ZX : (c + 1) * N_ZX, :, 256:] = terms.reshape(N_ZX, SLOT_ROWS, 384)
    d1[...] = tn(both_rows(AT_MIXED), both(AT_MIDDLE, RAW))
    e_raw = both(AT_E, RAW)
    for pair in range(N_CTX // 2):
        dd_pair = tn(both(AT_INNER + pair * 384, 384), e_raw).astype(bf16)
        for unit in range(pair * 24, pair * 24 + 24):
            at = hidden_place(unit) - pair * 384
            dd[unit * 16 : unit * 16 + 16, :] = dd_pair[at : at + 16, :]

    lane = lanes((SLOT_ROWS, 128))

    def pack(zx, carry):
        row = pl.multiple_of(zx * SLOT_ROWS, SLOT_ROWS)
        at = pl.multiple_of((2 * zx + core) * 96, 16)
        for c in range(N_CTX):
            slot = c * N_ZX + zx
            first = dd[pl.ds(at, 48), c * 128 : (c + 1) * 128].astype(f32)
            second = dd[pl.ds(at + 48, 48), c * 128 : (c + 1) * 128].astype(f32)
            t = jnp.where(lane < 64, first, pltpu.roll(second, 64, 1))
            own = d1[pl.ds(row, SLOT_ROWS), c * 128 : (c + 1) * 128]
            e = jnp.where(
                lane < 72,
                own,
                jnp.where(lane < 80, pltpu.roll(first, 8, 1), pltpu.roll(second, 16, 1)),
            )
            rest = pltpu.roll(e[32:], 16, 1)[4:]
            head = jnp.concatenate([rest, e[12:36]], axis=0)
            head = jnp.where(lane[:36] < 88, e[:36], jnp.where(lane[:36] < 104, head, 0.0))
            slots[slot, :, 128:256] = jnp.concatenate([head, t[:12]], axis=0).astype(bf16)
            for j in range(3):
                at_lane = 256 + j * 128
                g = slots[slot, 32:, at_lane : at_lane + 128].astype(f32)
                slots[slot, 32:, at_lane : at_lane + 128] = jnp.concatenate(
                    [g[:4], t[12 * j + 12 : 12 * j + 24]], axis=0
                ).astype(bf16)
        return carry

    lax.fori_loop(0, N_ZX, pack, 0)


def backward_kernel(
    pt, qs, kvs, gs, cosk, sink, cosq, sinq,
    dkv, dqp,
    dk, dv,
):
    def attend(i, carry):
        b = i // KV_HEADS
        h = i - b * KV_HEADS
        keys = kvs[b, :, pl.ds(pl.multiple_of(h // 2 * 128, 128), 128)]
        values = kvs[b, :, pl.ds(pl.multiple_of((h + 3) // 2 * 128, 128), 128)]
        g_b = gs[i]
        probs_b = pt[i]
        probs = probs_b.astype(f32)
        weighted = probs * nt(values, g_b)
        delta = jnp.sum(weighted, axis=0, keepdims=True)
        ds = (weighted - probs * delta).astype(bf16)
        dk[i] = turn_back(nn(ds, qs[i]), cosk[...], sink[...]).astype(bf16)
        dv[i] = nn(probs_b, g_b).astype(bf16)
        dq = tn(keys, ds).T * HEAD_DIM**-0.5
        for g in range(GROUP):
            dqp[
                pl.ds(pl.multiple_of(b * ROWS, ROWS), ROWS),
                pl.ds(pl.multiple_of((h * GROUP + g) * 128, 128), 128),
            ] = turn_back(dq[g * ROWS : (g + 1) * ROWS], cosq[...], sinq[...]).astype(bf16)
        return carry

    lax.fori_loop(0, PAIRS, attend, 0, unroll=True)
    for c in range(N_CTX):
        at = slice(c * ROWS, (c + 1) * ROWS)
        for b in range(BATCH):
            k = [dk[b * 3 + h, at, :] for h in range(3)]
            v = [dv[b * 3 + h, at, :] for h in range(3)]
            dkv[c, b * ROWS : (b + 1) * ROWS, :] = jnp.concatenate(
                [k[0] + k[1], k[2] + v[0], v[1] + v[2]], axis=1
            )


def project_grads_kernel(
    dkv, dqp, nrow, xall, xown, gain, wq, wkv, pr, sq, gain_grad,
    query_part, keep, give,
    dw, raw,
):
    dw[...] = jnp.zeros(dw.shape, f32)

    def one(c, term):
        x = xall[c].astype(f32)
        scaled = x * rho_of(x)
        packed = dkv[c]
        dw[...] += tn((scaled * gain[...]).astype(bf16), packed)
        return term + jnp.sum(nt(packed, wkv[...]) * scaled, axis=0, keepdims=True)

    term = lax.fori_loop(0, N_CTX, one, jnp.zeros((1, D), f32), unroll=True)
    dq = dqp[...]
    part = nt(dq, wq[...])
    query_part[...] = part
    x = xown[...].astype(f32)
    term = term + jnp.sum(part * (x * rho_of(x)), axis=0, keepdims=True)
    rows = tn(pr[...], dw[...].astype(bf16)).astype(bf16)
    raw[...] = tn(nrow[...], nt(dq, sq[:, :PAD_Q]).astype(bf16)) + nt(rows, sq[:, PAD_Q:])
    row = lax.broadcasted_iota(jnp.int32, (16, 128), 0)
    ends = jnp.zeros((16, 128), f32)
    for n, values in enumerate((term, gain_grad[...])):
        wide = jnp.concatenate([values, jnp.zeros((1, 64), f32)], axis=1)
        for j in range(5):
            ends = jnp.where(row == 4 + n * 5 + j, wide[:, j * 128 : (j + 1) * 128], ends)
    for who, ref in enumerate((keep, give)):
        for zx in range(N_ZX):
            at = who * HALF + zx * SLOT_ROWS
            for c in range(N_CTX):
                values = raw[at : at + SLOT_ROWS, c * 128 : (c + 1) * 128]
                ref[c * N_ZX + zx] = jnp.concatenate(
                    [values[:32], values[32:] + ends], axis=0
                ).astype(bf16)


def input_kernel(dkv, query_part, xown, gain, wkv, middle_grad, out):
    total = dkv[0].astype(f32)
    for c in range(1, N_CTX):
        total = total + dkv[c].astype(f32)
    normed_grad = query_part[...] + nt(total.astype(bf16), wkv[...])
    grad, _ = norm_back(xown[...].astype(f32), gain[...], normed_grad)
    out[...] = middle_grad[...] + grad


def head_kernel(query, key, value, segs, slots, wide, tall):
    wide[...] = jnp.zeros(wide.shape, f32)
    tall[...] = jnp.zeros(tall.shape, f32)
    wide[:36, :72] = query[...].astype(f32)
    wide[36:38, :] = segs[...].astype(f32)
    tall[72:96, :36] = key[...].astype(f32)
    tall[96:120, :36] = value[...].astype(f32)
    head = (wide[...] + tall[...].T[:SLOT_ROWS]).astype(bf16)
    for n in range(SLOTS):
        slots[n] = head


def spread_kernel(x, feed, sent, slots):
    for c in range(N_CTX):
        sent[c] = x[...]
    for n in range(SLOTS):
        slots[n] = feed[...]


def sum_kernel(
    came, first_gain, second_gain, query, key, value, out, gate, up, down, total
):
    step = pl.program_id(0)

    @pl.when(step == 0)
    def _():
        total[...] = jnp.zeros(total.shape, f32)

    total[...] += jnp.sum(came[...].astype(f32), axis=0)

    @pl.when(step == pl.num_programs(0) - 1)
    def _():
        def tile(n):
            return total[:, n * 128 : (n + 1) * 128]

        qkv, o = tile(0), tile(1)
        for n, ref in enumerate((first_gain, second_gain)):
            for j in range(5):
                width = min(128, D - j * 128)
                ref[:, j * 128 : j * 128 + width] = qkv[36 + n * 5 + j : 37 + n * 5 + j, :width]
        query[:, 0, :] = qkv[:36, :72]
        out[:, 0, :] = o[:36, :72]
        turned = jnp.concatenate([qkv, jnp.zeros((80, 128), f32)], axis=0).T
        key[...] = turned[72:96, :36]
        value[...] = turned[96:120, :36]
        a, b, t = (tile(n)[:36] for n in (2, 3, 4))
        gate[:, 0, :128] = a
        gate[:, 0, 128:] = t[:, :64]
        up[:, 0, :128] = b
        up[:, 0, 128:] = pltpu.roll(t, 64, 1)[:, :64]
        t = jnp.concatenate([tile(n)[36:] for n in range(1, 5)], axis=0)
        e = jnp.concatenate([o[:36], pltpu.roll(o[:16], 112, 1)[:12]], axis=0)
        low = lanes((SLOT_ROWS, 128)) < 64
        halves_of_down = [
            jnp.where(low, t, pltpu.roll(e, 120, 1)),
            jnp.where(low, pltpu.roll(t, 64, 1), pltpu.roll(e, 112, 1)),
            jnp.zeros((32, 128), f32),
        ]
        down[...] = jnp.concatenate(halves_of_down, axis=0).T[:72, :96]


def call(kernel, outs, scratch, *args, place=None):
    specs = [pl.BlockSpec(memory_space=pltpu.VMEM)] * len(args)
    if place is not None:
        specs = [pl.BlockSpec(memory_space=pltpu.SMEM)] + specs
        args = (place,) + args
    shapes = [jax.ShapeDtypeStruct(s, t) for s, t in outs]
    return pl.pallas_call(
        kernel,
        out_shape=shapes,
        in_specs=specs,
        out_specs=[pl.BlockSpec(memory_space=pltpu.VMEM)] * len(shapes),
        scratch_shapes=[pltpu.VMEM(s, t) for s, t in scratch],
        compiler_params=pltpu.CompilerParams(vmem_limit_bytes=60 * 1024 * 1024),
        cost_estimate=pl.CostEstimate(flops=1, bytes_accessed=1, transcendentals=0),
    )(*args)


def rotary_tables(positions):
    inverse_freq = theta ** (-(jnp.arange(HEAD_DIM // 2, dtype=f32) * 2.0) / HEAD_DIM)
    angles = positions.astype(f32)[:, None] * inverse_freq[None, :]
    return (
        jnp.concatenate([jnp.cos(angles)] * 4, axis=-1),
        jnp.concatenate([jnp.sin(angles)] * 4, axis=-1),
    )


def placements(core):
    def ones(rows, columns, wanted):
        return (wanted[:, None] == jnp.arange(columns)[None, :]).astype(bf16)

    def row(n):
        dp = n // 36
        return (dp % 2 ^ core) * HALF + dp // 2 * SLOT_ROWS + n % 36

    pr = ones(D, PAD_D, row(jnp.arange(D)))
    raw = jnp.arange(RAW)
    c, l = raw // 128, raw % 128
    q = jnp.where(l < 72, c * 72 + l, -1)
    k = jnp.where((l >= 72) & (l < 96), c * 24 + l - 72, -1)
    v = jnp.where((l >= 96) & (l < 120), c * 24 + l - 96, -1)
    head = q // HEAD_DIM
    upper = head // GROUP % 2
    padded = jnp.where(q < 0, -1, head * 128 + upper * HEAD_DIM + q % HEAD_DIM)
    target = jnp.where(k >= 0, PAD_Q + k, jnp.where(v >= 0, PAD_Q + KV + v, padded))
    sq = ones(RAW, PAD_Q + 2 * KV, target)
    so = ones(RAW, D, q)
    place = jnp.arange(PAD_Q)
    head, l = place // 128, place % 128
    upper = 1 - head // GROUP % 2
    inside = l // HEAD_DIM == upper
    n = head * HEAD_DIM + l % HEAD_DIM
    po = ones(PAD_Q, PAD_D, jnp.where(inside, row(n), -1))
    return pr, sq, so, po


def exchange(slots):
    return lax.all_to_all(slots, EVERY, 0, 0, tiled=True, axis_index_groups=SAME_CORE)


def swap(x):
    return lax.ppermute(x, EVERY, OTHER_CORE)


def pad_rows(x):
    return jnp.pad(x, ((0, SLOT_ROWS - x.shape[0]), (0, 0)))


def body(
    inputs,
    segments,
    cotangent,
    attention_gain,
    query_weight,
    key_weight,
    value_weight,
    out_weight,
    swiglu_gain,
    gate_weight,
    up_weight,
    down_weight,
):
    ctx, dp = lax.axis_index("ctx"), lax.axis_index("dp")
    place = jnp.stack([dp % 2, ctx, dp // 2]).astype(jnp.int32)
    down = down_weight[0]
    gate, up = gate_weight[0], up_weight[0]
    zero = functools.partial(jnp.zeros, dtype=bf16)
    (head,) = call(
        head_kernel,
        [((SLOTS, SLOT_ROWS, 128), bf16)],
        [((SLOT_ROWS, 128), f32), ((128, 128), f32)],
        query_weight[0], key_weight[0].T, value_weight[0].T, segments,
    )
    head_mine = exchange(head)
    main = jnp.concatenate([down[:48, :64], down[48:, :64]], axis=1)
    extra = jnp.concatenate([down[:48, 64:], down[48:, 64:]], axis=1)
    feed = jnp.concatenate(
        [
            jnp.concatenate(
                [
                    out_weight[0],
                    extra[:36],
                    jnp.concatenate([extra[36:], zero((24, 16))], axis=0),
                    zero((36, 24)),
                    gate[:, :128],
                    up[:, :128],
                    gate[:, 128:],
                    up[:, 128:],
                ],
                axis=1,
            ),
            jnp.concatenate([main[12 * j : 12 * j + 12] for j in range(4)], axis=1),
        ],
        axis=0,
    )
    xown = inputs.reshape(OWN, D)
    cot = cotangent.reshape(OWN, D)
    sent, slots = call(
        spread_kernel,
        [((N_CTX, BATCH, D, ROWS), bf16), ((SLOTS, SLOT_ROWS, 512), bf16)],
        [],
        inputs.transpose(0, 2, 1), feed,
    )
    sent, head_mine = lax.optimization_barrier((sent, head_mine))
    head_other = swap(head_mine)
    xall = lax.all_to_all(sent, "ctx", 0, 0, tiled=True)
    cosk, sink = rotary_tables(jnp.arange(SEQ, dtype=jnp.int32))
    cosq, sinq = rotary_tables(ctx * ROWS + jnp.arange(ROWS, dtype=jnp.int32))
    pr, sq, so, po = placements(dp % 2)
    slots, xall, head_other, cosk, sink, cosq, sinq, pr, sq, so, po = lax.optimization_barrier(
        (slots, xall, head_other, cosk, sink, cosq, sinq, pr, sq, so, po)
    )
    feed_mine = exchange(slots)

    wq, wkv, nrow, qs, kvs, pt, mixr, xrow = call(
        attend_kernel,
        [
            ((D, PAD_Q), bf16),
            ((D, 2 * KV), bf16),
            ((OWN, PAD_D), bf16),
            ((PAIRS, STACK, 128), bf16),
            ((BATCH, SEQ, 2 * KV), bf16),
            ((PAIRS, SEQ, STACK), bf16),
            ((OWN, PAD_D), bf16),
            ((N_CTX, OWN, D), bf16),
        ],
        [
            ((PAD_D, RAW), bf16),
            ((D, RAW), bf16),
            ((BATCH, SEQ, ROWS), f32),
            ((OWN, PAD_Q), bf16),
        ],
        head_mine, head_other, xall, xown, attention_gain, segments.astype(f32),
        cosk, sink, cosq, sinq, pr, sq, po,
        place=place,
    )
    feed_mine, mixr = lax.optimization_barrier((feed_mine, mixr))
    feed_other = swap(feed_mine)
    down_mine, wo = call(
        unpack_kernel,
        [((HALF * 2, RAW), bf16), ((HALF, D), bf16)],
        [((HALF, RAW), bf16)],
        feed_mine, so,
    )

    result, gs, acts, middle_grad, gain_grad = call(
        feed_kernel,
        [
            ((OWN, D), bf16),
            ((PAIRS, STACK, 128), bf16),
            ((OWN, ACTS), bf16),
            ((OWN, D), f32),
            ((1, D), f32),
        ],
        [
            ((FF, RAW), bf16),
            ((HALF, RAW), bf16),
            ((HALF * 2, RAW), bf16),
            ((HALF, D), bf16),
        ],
        feed_mine, feed_other, down_mine, xown, mixr, cot, swiglu_gain, wo, pr, so, po,
        place=place,
    )
    acts_other = swap(acts)
    dkv, dqp = call(
        backward_kernel,
        [((N_CTX, OWN, 2 * KV), bf16), ((OWN, PAD_Q), bf16)],
        [((PAIRS, SEQ, 128), bf16), ((PAIRS, SEQ, 128), bf16)],
        pt, qs, kvs, gs, cosk, sink, cosq, sinq,
    )
    dkv_came = lax.all_to_all(dkv, "ctx", 0, 0, tiled=True)
    acts_other, dkv = lax.optimization_barrier((acts_other, dkv))
    (slots,) = call(
        terms_kernel,
        [((SLOTS, SLOT_ROWS, 640), bf16)],
        [((HALF, RAW), f32), ((FF, RAW), bf16)],
        acts, acts_other,
        place=place,
    )
    query_part, keep, give = call(
        project_grads_kernel,
        [
            ((OWN, D), f32),
            ((SLOTS, SLOT_ROWS, 128), bf16),
            ((SLOTS, SLOT_ROWS, 128), bf16),
        ],
        [((D, 2 * KV), f32), ((PAD_D, RAW), f32)],
        dkv, dqp, nrow, xrow, xown, attention_gain, wq, wkv, pr, sq, gain_grad,
    )
    keep, give, slots, dkv_came = lax.optimization_barrier((keep, give, slots, dkv_came))
    head_sum = (keep.astype(f32) + swap(give).astype(f32)).astype(bf16)
    came = exchange(lax.dynamic_update_slice(slots, head_sum, (0, 0, 0)))
    (input_grad,) = call(
        input_kernel,
        [((OWN, D), f32)],
        [],
        dkv_came, query_part, xown, attention_gain, wkv, middle_grad,
    )

    first_total, second_total, query, key, value, out, gate_total, up_total, down_total = (
        pl.pallas_call(
            sum_kernel,
            grid=(4,),
            in_specs=[pl.BlockSpec((SLOTS // 4, SLOT_ROWS, 640), lambda i: (i, 0, 0))],
            out_specs=[pl.BlockSpec(memory_space=pltpu.VMEM)] * 9,
            out_shape=[
                jax.ShapeDtypeStruct(shape, f32)
                for shape in (
                    (1, D), (1, D), (36, 1, 72), (24, 36), (24, 36), (36, 1, 72), (36, 1, 192), (36, 1, 192), (72, 96),
                )
            ],
            scratch_shapes=[pltpu.VMEM((SLOT_ROWS, 640), f32)],
            compiler_params=pltpu.CompilerParams(vmem_limit_bytes=16 * 1024 * 1024),
        )(came)
    )
    return (
        result.reshape(BATCH, ROWS, D),
        input_grad.reshape(BATCH, ROWS, D),
        first_total,
        query.transpose(1, 0, 2),
        key.T[None],
        value.T[None],
        out.transpose(1, 0, 2),
        second_total,
        gate_total.transpose(1, 0, 2),
        up_total.transpose(1, 0, 2),
        down_total.T[None],
    )


def solution(mesh):
    weight = P(None, "dp", "ctx")
    rows = P("dp", "ctx", None)
    return jax.shard_map(
        body,
        mesh=mesh,
        in_specs=(rows, P("dp", "ctx"), rows, P(), weight, weight, weight, weight, P(), weight, weight, weight),
        out_specs=(rows, rows, P(), weight, weight, weight, weight, P(), weight, weight, weight),
        check_vma=False,
    )
```

```python
import functools

import jax
import jax.numpy as jnp
from jax import lax
from jax.experimental import pallas as pl
from jax.experimental.pallas import tpu as pltpu
from jax.sharding import PartitionSpec as P

HEADS = 9
KV_HEADS = 3
HEAD_DIM = 64
GROUP = HEADS // KV_HEADS
D = 576
FF = 1536
KV = KV_HEADS * HEAD_DIM
BATCH = 2
ROWS = 128
SEQ = 1024
OWN = BATCH * ROWS
ALL = BATCH * SEQ
N_CTX = 8
N_DP = 16
N_ZX = N_DP // 2
SLOTS = N_CTX * N_ZX
SLOT_ROWS = 48
HALF = N_ZX * SLOT_ROWS
PAD_D = 2 * HALF
RAW = N_CTX * 128
PAD_Q = HEADS * 128
STACK = GROUP * ROWS
AT_SECOND, AT_FEED, AT_INNER, AT_E, AT_MIDDLE, AT_MIXED, ACTS = 0, 768, 3840, 5376, 6400, 7424, 8192
PAIRS = BATCH * KV_HEADS

eps = 1e-05
theta = 10000.0
masked = -1e30
bf16 = jnp.bfloat16
f32 = jnp.float32

EVERY = ("dp", "ctx")
SAME_CORE = [
    [(zx * 2 + core) * N_CTX + ctx for ctx in range(N_CTX) for zx in range(N_ZX)]
    for core in range(2)
]
OTHER_CORE = [
    (dp * N_CTX + ctx, (dp ^ 1) * N_CTX + ctx) for dp in range(N_DP) for ctx in range(N_CTX)
]


def nn(left, right):
    return jnp.dot(left, right, preferred_element_type=f32)


def tn(left, right):
    return lax.dot_general(left, right, (((0,), (0,)), ((), ())), preferred_element_type=f32)


def nt(left, right):
    return lax.dot_general(left, right, (((1,), (1,)), ((), ())), preferred_element_type=f32)


def halves(x):
    high = x.astype(bf16)
    return high, (x - high.astype(f32)).astype(bf16)


def rho_of(x):
    return lax.rsqrt(jnp.mean(x * x, axis=-1, keepdims=True) + eps)


def norm_back(x, gain, c):
    rho = rho_of(x)
    w = c * gain
    grad = rho * (w - x * (rho * rho * jnp.mean(w * x, axis=-1, keepdims=True)))
    return grad, jnp.sum(c * (x * rho), axis=0, keepdims=True)


def lanes(shape):
    return lax.broadcasted_iota(jnp.int32, shape, 1)


def turn(x, cosine, sine):
    first = lanes(x.shape) % HEAD_DIM < HEAD_DIM // 2
    turned = jnp.where(first, -pltpu.roll(x, 96, 1), pltpu.roll(x, 32, 1))
    return x * cosine + turned * sine


def turn_back(x, cosine, sine):
    first = lanes(x.shape) % HEAD_DIM < HEAD_DIM // 2
    w = x * sine
    turned = jnp.where(first, pltpu.roll(w, 96, 1), -pltpu.roll(w, 32, 1))
    return x * cosine + turned


def triple(x, axis):
    return jnp.concatenate([x] * GROUP, axis=axis)


def block(ref, c, start, width):
    return ref[c * N_ZX : (c + 1) * N_ZX, :, start : start + width].reshape(HALF, width)


def hidden_place(unit):
    n = unit * 16
    c, m = divmod(n, 192)
    base = (c // 2) * 384
    if m < 128:
        return base + (c % 2) * 128 + m
    return base + 256 + (c % 2) * 64 + (m - 128)


def attend_kernel(
    place, mine, other, xall, xown, gain, segq, cosk, sink, cosq, sinq, pr, sq, po,
    wq, wkv, nrow, qs, kvs, pt, mixr, xrow,
    raw, wmid, bias, mixp,
):
    ctx, zx_own = place[1], place[2]
    for c in range(N_CTX):
        raw[:HALF, c * 128 : (c + 1) * 128] = block(mine, c, 0, 128)
        raw[HALF:, c * 128 : (c + 1) * 128] = block(other, c, 0, 128)
    wmid[...] = nn(pr[...], raw[...]).astype(bf16)
    wkv[...] = nn(wmid[...], sq[:, PAD_Q:]).astype(bf16)
    wq[...] = nn(wmid[...], sq[:, :PAD_Q]).astype(bf16)

    x = xown[...].astype(f32)
    normed = (x * rho_of(x) * gain[...]).astype(bf16)
    nrow[...] = nn(normed, pr[...]).astype(bf16)
    pre = nn(normed, wq[...])
    for head in range(HEADS):
        h, g = divmod(head, GROUP)
        for b in range(BATCH):
            turned = turn(
                pre[b * ROWS : (b + 1) * ROWS, head * 128 : (head + 1) * 128], cosq[...], sinq[...]
            )
            qs[b * KV_HEADS + h, g * ROWS : (g + 1) * ROWS, :] = (
                turned.astype(bf16) * bf16(HEAD_DIM**-0.5)
            )

    low = lanes((ROWS, 128)) < HEAD_DIM

    def project(c, carry):
        at = pl.multiple_of(c * ROWS, ROWS)
        x = jnp.concatenate([xall[c, b].astype(f32).T for b in range(BATCH)], axis=0)
        xrow[c] = x.astype(bf16)
        normed = (x * rho_of(x) * gain[...]).astype(bf16)
        pre = nn(normed, wkv[...])
        cosine, sine = cosk[pl.ds(at, ROWS), :], sink[pl.ds(at, ROWS), :]
        ends = mine[c * N_ZX + zx_own][32:].astype(f32)
        for b in range(BATCH):
            rows = pre[b * ROWS : (b + 1) * ROWS]
            tile = rows[:, 128:256]
            kvs[b, pl.ds(at, ROWS), :128] = turn(rows[:, :128], cosine, sine).astype(bf16)
            kvs[b, pl.ds(at, ROWS), 128:256] = jnp.where(
                low, turn(tile, cosine, sine), tile
            ).astype(bf16)
            kvs[b, pl.ds(at, ROWS), 256:] = rows[:, 256:].astype(bf16)
            keys = jnp.broadcast_to(ends[4 + b : 5 + b, :], (ROWS, ROWS)).T
            key_pos = c * ROWS + lax.broadcasted_iota(jnp.int32, (ROWS, ROWS), 0)
            query_pos = ctx * ROWS + lanes((ROWS, ROWS))
            allowed = (keys == segq[b : b + 1, :]) & (key_pos <= query_pos)
            bias[b, pl.ds(at, ROWS), :] = jnp.where(allowed, 0.0, masked)
        return carry

    lax.fori_loop(0, N_CTX, project, 0)

    def attend(i, carry):
        b = i // KV_HEADS
        h = i - b * KV_HEADS
        keys = kvs[b, :, pl.ds(pl.multiple_of(h // 2 * 128, 128), 128)]
        values = kvs[b, :, pl.ds(pl.multiple_of((h + 3) // 2 * 128, 128), 128)]
        scores = nt(keys, qs[i]) + triple(bias[b], 1)
        top = jnp.max(scores, axis=0, keepdims=True)
        expo = jnp.exp(scores - top)
        total = jnp.sum(expo, axis=0, keepdims=True)
        probs = (expo * (1.0 / total)).astype(bf16)
        pt[i] = probs
        mixed = tn(values, probs).T.astype(bf16)
        for g in range(GROUP):
            mixp[
                pl.ds(pl.multiple_of(b * ROWS, ROWS), ROWS),
                pl.ds(pl.multiple_of((h * GROUP + g) * 128, 128), 128),
            ] = mixed[g * ROWS : (g + 1) * ROWS]
        return carry

    lax.fori_loop(0, PAIRS, attend, 0)
    mixr[...] = nn(mixp[...], po[...]).astype(bf16)


def unpack(mine, down, oraw):
    lane = lanes((SLOT_ROWS, 128))
    for c in range(N_CTX):
        oraw[:, c * 128 : (c + 1) * 128] = block(mine, c, 0, 128)

    def one(zx, carry):
        at = pl.multiple_of(zx * 96, 96)
        for c in range(N_CTX):
            o = mine[c * N_ZX + zx, :, :128].astype(f32)
            t = jnp.concatenate(
                [o[36:]]
                + [
                    mine[c * N_ZX + zx, 32:, j * 128 : (j + 1) * 128].astype(f32)[4:]
                    for j in range(1, 4)
                ],
                axis=0,
            )
            e = jnp.concatenate([o[:36], pltpu.roll(o[:16], 112, 1)[:12]], axis=0)
            first = jnp.where(lane < 64, t, jnp.where(lane < 72, pltpu.roll(e, 120, 1), 0.0))
            second = jnp.where(
                lane < 64,
                pltpu.roll(t, 64, 1),
                jnp.where(lane < 72, pltpu.roll(e, 112, 1), 0.0),
            )
            down[pl.ds(at, 96), c * 128 : (c + 1) * 128] = jnp.concatenate(
                [first, second], axis=0
            ).astype(bf16)
        return carry

    lax.fori_loop(0, N_ZX, one, 0)


def unpack_kernel(mine, so, down, wo, oraw):
    unpack(mine, down, oraw)
    wo[...] = nn(oraw[...], so[...]).astype(bf16)


def place_of(c, odd_dp, n):
    m = odd_dp * 96 + n
    base = (c // 2) * 384
    at = jnp.where(m < 128, base + c % 2 * 128 + m, base + 256 + c % 2 * 64 + (m - 128))
    return pl.multiple_of(at, 16)


def feed_kernel(
    place, mine, other, down_mine, xown, mixr, cot, gain, wo, pr, so, po,
    result, gs, acts, middle_grad, gain_grad,
    down, oraw, down_other, wo_other,
):
    core = place[0]
    unpack(other, down_other, oraw)
    wo_other[...] = nn(oraw[...], so[...]).astype(bf16)
    for who, ref in enumerate((down_mine, down_other)):
        for zx in range(N_ZX):
            for n in range(0, 96, 16):
                down[pl.ds(place_of(zx, who ^ core, n), 16), :] = ref[
                    zx * 96 + n : zx * 96 + n + 16, :
                ]
    mixed_r = mixr[...]
    mid = xown[...].astype(f32) + (
        nn(mixed_r[:, :HALF], wo[...]) + nn(mixed_r[:, HALF:], wo_other[...])
    )
    rho = rho_of(mid)
    second = (mid * rho * gain[...]).astype(bf16)
    second_r = nn(second, pr[...]).astype(bf16)
    e_b = cot[...]
    e_raw = nt(e_b, so[...]).astype(bf16)
    acts[:, AT_SECOND:AT_FEED] = second_r
    acts[:, AT_E:AT_MIDDLE] = e_raw
    acts[:, AT_MIXED:] = mixed_r
    low = lanes((OWN, 128)) < 64
    grad_sum = jnp.zeros((OWN, PAD_D), f32)
    result_sum = jnp.zeros((OWN, RAW), f32)
    for pair in range(N_CTX // 2):
        weights = [
            jnp.concatenate([block(ref, c, 128, 384) for ref in (mine, other)], axis=0)
            for c in (2 * pair, 2 * pair + 1)
        ]
        pre = [nn(second_r, weight) for weight in weights]
        a, u, t, a2, u2, t2 = (pre[i // 3][:, i % 3 * 128 : (i % 3 + 1) * 128] for i in range(6))
        gate = jnp.concatenate([a, a2, jnp.where(low, t, pltpu.roll(t2, 64, 1))], axis=1)
        up = jnp.concatenate([u, u2, jnp.where(low, pltpu.roll(t, 64, 1), t2)], axis=1)
        logistic = 1.0 / (1.0 + jnp.exp(-gate))
        silu = gate * logistic
        inner = (silu * up).astype(bf16)
        rows = down[pair * 384 : (pair + 1) * 384, :]
        result_sum += nn(inner, rows)
        inner_grad = nt(e_raw, rows)
        gate_grad = inner_grad * up * (logistic * (1.0 + gate * (1.0 - logistic)))
        up_grad = inner_grad * silu
        a, a2, gt = (gate_grad[:, i * 128 : (i + 1) * 128] for i in range(3))
        u, u2, ut = (up_grad[:, i * 128 : (i + 1) * 128] for i in range(3))
        t = jnp.where(low, gt, pltpu.roll(ut, 64, 1))
        t2 = jnp.where(low, pltpu.roll(gt, 64, 1), ut)
        for k, tiles in enumerate(((a, u, t), (a2, u2, t2))):
            grads = jnp.concatenate(tiles, axis=1).astype(bf16)
            grad_sum += nt(grads, weights[k])
            at = AT_FEED + (2 * pair + k) * 384
            acts[:, at : at + 384] = grads
        acts[:, AT_INNER + pair * 384 : AT_INNER + (pair + 1) * 384] = inner

    high, rest = halves(result_sum)
    result[...] = (mid + (nn(high, so[...]) + nn(rest, so[...]))).astype(bf16)
    high, rest = halves(grad_sum)
    second_grad = nt(high, pr[...]) + nt(rest, pr[...])
    norm_grad, gain_term = norm_back(mid, gain[...], second_grad)
    gain_grad[...] = gain_term
    total = e_b.astype(f32) + norm_grad
    middle_grad[...] = total
    middle_b = total.astype(bf16)
    acts[:, AT_MIDDLE:AT_MIXED] = nt(middle_b, so[...]).astype(bf16)
    back = jnp.concatenate([nt(middle_b, wo[...]), nt(middle_b, wo_other[...])], axis=1)
    back = nt(back.astype(bf16), po[...]).astype(bf16)
    for head in range(HEADS):
        h, g = divmod(head, GROUP)
        for b in range(BATCH):
            gs[b * KV_HEADS + h, g * ROWS : (g + 1) * ROWS, :] = back[
                b * ROWS : (b + 1) * ROWS, head * 128 : (head + 1) * 128
            ]


def terms_kernel(place, acts, acts_other, slots, d1, dd):
    core = place[0]

    def both(start, width):
        return jnp.concatenate(
            [acts[:, start : start + width], acts_other[:, start : start + width]], axis=0
        )

    def both_rows(start):
        own, other = start, start + HALF
        return jnp.concatenate(
            [acts[:, own : own + HALF], acts_other[:, other : other + HALF]], axis=0
        )

    slots[:, :, :128] = jnp.zeros((SLOTS, SLOT_ROWS, 128), bf16)
    left = both_rows(AT_SECOND)
    for c in range(N_CTX):
        terms = tn(left, both(AT_FEED + c * 384, 384)).astype(bf16)
        slots[c * N_ZX : (c + 1) * N_ZX, :, 256:] = terms.reshape(N_ZX, SLOT_ROWS, 384)
    d1[...] = tn(both_rows(AT_MIXED), both(AT_MIDDLE, RAW))
    e_raw = both(AT_E, RAW)
    for pair in range(N_CTX // 2):
        dd_pair = tn(both(AT_INNER + pair * 384, 384), e_raw).astype(bf16)
        for unit in range(pair * 24, pair * 24 + 24):
            at = hidden_place(unit) - pair * 384
            dd[unit * 16 : unit * 16 + 16, :] = dd_pair[at : at + 16, :]

    lane = lanes((SLOT_ROWS, 128))

    def pack(zx, carry):
        row = pl.multiple_of(zx * SLOT_ROWS, SLOT_ROWS)
        at = pl.multiple_of((2 * zx + core) * 96, 16)
        for c in range(N_CTX):
            slot = c * N_ZX + zx
            first = dd[pl.ds(at, 48), c * 128 : (c + 1) * 128].astype(f32)
            second = dd[pl.ds(at + 48, 48), c * 128 : (c + 1) * 128].astype(f32)
            t = jnp.where(lane < 64, first, pltpu.roll(second, 64, 1))
            own = d1[pl.ds(row, SLOT_ROWS), c * 128 : (c + 1) * 128]
            e = jnp.where(
                lane < 72,
                own,
                jnp.where(lane < 80, pltpu.roll(first, 8, 1), pltpu.roll(second, 16, 1)),
            )
            rest = pltpu.roll(e[32:], 16, 1)[4:]
            head = jnp.concatenate([rest, e[12:36]], axis=0)
            head = jnp.where(lane[:36] < 88, e[:36], jnp.where(lane[:36] < 104, head, 0.0))
            slots[slot, :, 128:256] = jnp.concatenate([head, t[:12]], axis=0).astype(bf16)
            for j in range(3):
                at_lane = 256 + j * 128
                g = slots[slot, 32:, at_lane : at_lane + 128].astype(f32)
                slots[slot, 32:, at_lane : at_lane + 128] = jnp.concatenate(
                    [g[:4], t[12 * j + 12 : 12 * j + 24]], axis=0
                ).astype(bf16)
        return carry

    lax.fori_loop(0, N_ZX, pack, 0)


def backward_kernel(
    pt, qs, kvs, gs, cosk, sink, cosq, sinq,
    dkv, dqp,
    dk, dv,
):
    def attend(i, carry):
        b = i // KV_HEADS
        h = i - b * KV_HEADS
        keys = kvs[b, :, pl.ds(pl.multiple_of(h // 2 * 128, 128), 128)]
        values = kvs[b, :, pl.ds(pl.multiple_of((h + 3) // 2 * 128, 128), 128)]
        g_b = gs[i]
        probs_b = pt[i]
        probs = probs_b.astype(f32)
        weighted = probs * nt(values, g_b)
        delta = jnp.sum(weighted, axis=0, keepdims=True)
        ds = (weighted - probs * delta).astype(bf16)
        dk[i] = turn_back(nn(ds, qs[i]), cosk[...], sink[...]).astype(bf16)
        dv[i] = nn(probs_b, g_b).astype(bf16)
        dq = tn(keys, ds).T * HEAD_DIM**-0.5
        for g in range(GROUP):
            dqp[
                pl.ds(pl.multiple_of(b * ROWS, ROWS), ROWS),
                pl.ds(pl.multiple_of((h * GROUP + g) * 128, 128), 128),
            ] = turn_back(dq[g * ROWS : (g + 1) * ROWS], cosq[...], sinq[...]).astype(bf16)
        return carry

    lax.fori_loop(0, PAIRS, attend, 0, unroll=True)
    for c in range(N_CTX):
        at = slice(c * ROWS, (c + 1) * ROWS)
        for b in range(BATCH):
            k = [dk[b * 3 + h, at, :] for h in range(3)]
            v = [dv[b * 3 + h, at, :] for h in range(3)]
            dkv[c, b * ROWS : (b + 1) * ROWS, :] = jnp.concatenate(
                [k[0] + k[1], k[2] + v[0], v[1] + v[2]], axis=1
            )


def project_grads_kernel(
    dkv, dqp, nrow, xall, xown, gain, wq, wkv, pr, sq, gain_grad,
    query_part, keep, give,
    dw, raw,
):
    dw[...] = jnp.zeros(dw.shape, f32)

    def one(c, term):
        x = xall[c].astype(f32)
        scaled = x * rho_of(x)
        packed = dkv[c]
        dw[...] += tn((scaled * gain[...]).astype(bf16), packed)
        return term + jnp.sum(nt(packed, wkv[...]) * scaled, axis=0, keepdims=True)

    term = lax.fori_loop(0, N_CTX, one, jnp.zeros((1, D), f32), unroll=True)
    dq = dqp[...]
    part = nt(dq, wq[...])
    query_part[...] = part
    x = xown[...].astype(f32)
    term = term + jnp.sum(part * (x * rho_of(x)), axis=0, keepdims=True)
    rows = tn(pr[...], dw[...].astype(bf16)).astype(bf16)
    raw[...] = tn(nrow[...], nt(dq, sq[:, :PAD_Q]).astype(bf16)) + nt(rows, sq[:, PAD_Q:])
    row = lax.broadcasted_iota(jnp.int32, (16, 128), 0)
    ends = jnp.zeros((16, 128), f32)
    for n, values in enumerate((term, gain_grad[...])):
        wide = jnp.concatenate([values, jnp.zeros((1, 64), f32)], axis=1)
        for j in range(5):
            ends = jnp.where(row == 4 + n * 5 + j, wide[:, j * 128 : (j + 1) * 128], ends)
    for who, ref in enumerate((keep, give)):
        for zx in range(N_ZX):
            at = who * HALF + zx * SLOT_ROWS
            for c in range(N_CTX):
                values = raw[at : at + SLOT_ROWS, c * 128 : (c + 1) * 128]
                ref[c * N_ZX + zx] = jnp.concatenate(
                    [values[:32], values[32:] + ends], axis=0
                ).astype(bf16)


def input_kernel(dkv, query_part, xown, gain, wkv, middle_grad, out):
    total = dkv[0].astype(f32)
    for c in range(1, N_CTX):
        total = total + dkv[c].astype(f32)
    normed_grad = query_part[...] + nt(total.astype(bf16), wkv[...])
    grad, _ = norm_back(xown[...].astype(f32), gain[...], normed_grad)
    out[...] = middle_grad[...] + grad


def head_kernel(query, key, value, segs, slots, wide, tall):
    wide[...] = jnp.zeros(wide.shape, f32)
    tall[...] = jnp.zeros(tall.shape, f32)
    wide[:36, :72] = query[...].astype(f32)
    wide[36:38, :] = segs[...].astype(f32)
    tall[72:96, :36] = key[...].astype(f32)
    tall[96:120, :36] = value[...].astype(f32)
    head = (wide[...] + tall[...].T[:SLOT_ROWS]).astype(bf16)
    for n in range(SLOTS):
        slots[n] = head


def spread_kernel(x, feed, sent, slots):
    for c in range(N_CTX):
        sent[c] = x[...]
    for n in range(SLOTS):
        slots[n] = feed[...]


def sum_kernel(
    came, first_gain, second_gain, query, key, value, out, gate, up, down, total
):
    step = pl.program_id(0)

    @pl.when(step == 0)
    def _():
        total[...] = jnp.zeros(total.shape, f32)

    total[...] += jnp.sum(came[...].astype(f32), axis=0)

    @pl.when(step == pl.num_programs(0) - 1)
    def _():
        def tile(n):
            return total[:, n * 128 : (n + 1) * 128]

        qkv, o = tile(0), tile(1)
        for n, ref in enumerate((first_gain, second_gain)):
            for j in range(5):
                width = min(128, D - j * 128)
                ref[:, j * 128 : j * 128 + width] = qkv[36 + n * 5 + j : 37 + n * 5 + j, :width]
        query[:, 0, :] = qkv[:36, :72]
        out[:, 0, :] = o[:36, :72]
        turned = jnp.concatenate([qkv, jnp.zeros((80, 128), f32)], axis=0).T
        key[...] = turned[72:96, :36]
        value[...] = turned[96:120, :36]
        a, b, t = (tile(n)[:36] for n in (2, 3, 4))
        gate[:, 0, :128] = a
        gate[:, 0, 128:] = t[:, :64]
        up[:, 0, :128] = b
        up[:, 0, 128:] = pltpu.roll(t, 64, 1)[:, :64]
        t = jnp.concatenate([tile(n)[36:] for n in range(1, 5)], axis=0)
        e = jnp.concatenate([o[:36], pltpu.roll(o[:16], 112, 1)[:12]], axis=0)
        low = lanes((SLOT_ROWS, 128)) < 64
        halves_of_down = [
            jnp.where(low, t, pltpu.roll(e, 120, 1)),
            jnp.where(low, pltpu.roll(t, 64, 1), pltpu.roll(e, 112, 1)),
            jnp.zeros((32, 128), f32),
        ]
        down[...] = jnp.concatenate(halves_of_down, axis=0).T[:72, :96]


def call(kernel, outs, scratch, *args, place=None):
    specs = [pl.BlockSpec(memory_space=pltpu.VMEM)] * len(args)
    if place is not None:
        specs = [pl.BlockSpec(memory_space=pltpu.SMEM)] + specs
        args = (place,) + args
    shapes = [jax.ShapeDtypeStruct(s, t) for s, t in outs]
    return pl.pallas_call(
        kernel,
        out_shape=shapes,
        in_specs=specs,
        out_specs=[pl.BlockSpec(memory_space=pltpu.VMEM)] * len(shapes),
        scratch_shapes=[pltpu.VMEM(s, t) for s, t in scratch],
        compiler_params=pltpu.CompilerParams(vmem_limit_bytes=60 * 1024 * 1024),
        cost_estimate=pl.CostEstimate(flops=1, bytes_accessed=1, transcendentals=0),
    )(*args)


def rotary_tables(positions):
    inverse_freq = theta ** (-(jnp.arange(HEAD_DIM // 2, dtype=f32) * 2.0) / HEAD_DIM)
    angles = positions.astype(f32)[:, None] * inverse_freq[None, :]
    return (
        jnp.concatenate([jnp.cos(angles)] * 4, axis=-1),
        jnp.concatenate([jnp.sin(angles)] * 4, axis=-1),
    )


def placements(core):
    def ones(rows, columns, wanted):
        return (wanted[:, None] == jnp.arange(columns)[None, :]).astype(bf16)

    def row(n):
        dp = n // 36
        return (dp % 2 ^ core) * HALF + dp // 2 * SLOT_ROWS + n % 36

    pr = ones(D, PAD_D, row(jnp.arange(D)))
    raw = jnp.arange(RAW)
    c, l = raw // 128, raw % 128
    q = jnp.where(l < 72, c * 72 + l, -1)
    k = jnp.where((l >= 72) & (l < 96), c * 24 + l - 72, -1)
    v = jnp.where((l >= 96) & (l < 120), c * 24 + l - 96, -1)
    head = q // HEAD_DIM
    upper = head // GROUP % 2
    padded = jnp.where(q < 0, -1, head * 128 + upper * HEAD_DIM + q % HEAD_DIM)
    target = jnp.where(k >= 0, PAD_Q + k, jnp.where(v >= 0, PAD_Q + KV + v, padded))
    sq = ones(RAW, PAD_Q + 2 * KV, target)
    so = ones(RAW, D, q)
    place = jnp.arange(PAD_Q)
    head, l = place // 128, place % 128
    upper = 1 - head // GROUP % 2
    inside = l // HEAD_DIM == upper
    n = head * HEAD_DIM + l % HEAD_DIM
    po = ones(PAD_Q, PAD_D, jnp.where(inside, row(n), -1))
    return pr, sq, so, po


def exchange(slots):
    return lax.all_to_all(slots, EVERY, 0, 0, tiled=True, axis_index_groups=SAME_CORE)


def swap(x):
    return lax.ppermute(x, EVERY, OTHER_CORE)


def pad_rows(x):
    return jnp.pad(x, ((0, SLOT_ROWS - x.shape[0]), (0, 0)))


def body(
    inputs,
    segments,
    cotangent,
    attention_gain,
    query_weight,
    key_weight,
    value_weight,
    out_weight,
    swiglu_gain,
    gate_weight,
    up_weight,
    down_weight,
):
    ctx, dp = lax.axis_index("ctx"), lax.axis_index("dp")
    place = jnp.stack([dp % 2, ctx, dp // 2]).astype(jnp.int32)
    down = down_weight[0]
    gate, up = gate_weight[0], up_weight[0]
    zero = functools.partial(jnp.zeros, dtype=bf16)
    (head,) = call(
        head_kernel,
        [((SLOTS, SLOT_ROWS, 128), bf16)],
        [((SLOT_ROWS, 128), f32), ((128, 128), f32)],
        query_weight[0], key_weight[0].T, value_weight[0].T, segments,
    )
    head_mine = exchange(head)
    main = jnp.concatenate([down[:48, :64], down[48:, :64]], axis=1)
    extra = jnp.concatenate([down[:48, 64:], down[48:, 64:]], axis=1)
    feed = jnp.concatenate(
        [
            jnp.concatenate(
                [
                    out_weight[0],
                    extra[:36],
                    jnp.concatenate([extra[36:], zero((24, 16))], axis=0),
                    zero((36, 24)),
                    gate[:, :128],
                    up[:, :128],
                    gate[:, 128:],
                    up[:, 128:],
                ],
                axis=1,
            ),
            jnp.concatenate([main[12 * j : 12 * j + 12] for j in range(4)], axis=1),
        ],
        axis=0,
    )
    xown = inputs.reshape(OWN, D)
    cot = cotangent.reshape(OWN, D)
    sent, slots = call(
        spread_kernel,
        [((N_CTX, BATCH, D, ROWS), bf16), ((SLOTS, SLOT_ROWS, 512), bf16)],
        [],
        inputs.transpose(0, 2, 1), feed,
    )
    sent, head_mine = lax.optimization_barrier((sent, head_mine))
    head_other = swap(head_mine)
    xall = lax.all_to_all(sent, "ctx", 0, 0, tiled=True)
    cosk, sink = rotary_tables(jnp.arange(SEQ, dtype=jnp.int32))
    cosq, sinq = rotary_tables(ctx * ROWS + jnp.arange(ROWS, dtype=jnp.int32))
    pr, sq, so, po = placements(dp % 2)
    slots, xall, head_other, cosk, sink, cosq, sinq, pr, sq, so, po = lax.optimization_barrier(
        (slots, xall, head_other, cosk, sink, cosq, sinq, pr, sq, so, po)
    )
    feed_mine = exchange(slots)

    wq, wkv, nrow, qs, kvs, pt, mixr, xrow = call(
        attend_kernel,
        [
            ((D, PAD_Q), bf16),
            ((D, 2 * KV), bf16),
            ((OWN, PAD_D), bf16),
            ((PAIRS, STACK, 128), bf16),
            ((BATCH, SEQ, 2 * KV), bf16),
            ((PAIRS, SEQ, STACK), bf16),
            ((OWN, PAD_D), bf16),
            ((N_CTX, OWN, D), bf16),
        ],
        [
            ((PAD_D, RAW), bf16),
            ((D, RAW), bf16),
            ((BATCH, SEQ, ROWS), f32),
            ((OWN, PAD_Q), bf16),
        ],
        head_mine, head_other, xall, xown, attention_gain, segments.astype(f32),
        cosk, sink, cosq, sinq, pr, sq, po,
        place=place,
    )
    feed_mine, mixr = lax.optimization_barrier((feed_mine, mixr))
    feed_other = swap(feed_mine)
    down_mine, wo = call(
        unpack_kernel,
        [((HALF * 2, RAW), bf16), ((HALF, D), bf16)],
        [((HALF, RAW), bf16)],
        feed_mine, so,
    )

    result, gs, acts, middle_grad, gain_grad = call(
        feed_kernel,
        [
            ((OWN, D), bf16),
            ((PAIRS, STACK, 128), bf16),
            ((OWN, ACTS), bf16),
            ((OWN, D), f32),
            ((1, D), f32),
        ],
        [
            ((FF, RAW), bf16),
            ((HALF, RAW), bf16),
            ((HALF * 2, RAW), bf16),
            ((HALF, D), bf16),
        ],
        feed_mine, feed_other, down_mine, xown, mixr, cot, swiglu_gain, wo, pr, so, po,
        place=place,
    )
    acts_other = swap(acts)
    dkv, dqp = call(
        backward_kernel,
        [((N_CTX, OWN, 2 * KV), bf16), ((OWN, PAD_Q), bf16)],
        [((PAIRS, SEQ, 128), bf16), ((PAIRS, SEQ, 128), bf16)],
        pt, qs, kvs, gs, cosk, sink, cosq, sinq,
    )
    dkv_came = lax.all_to_all(dkv, "ctx", 0, 0, tiled=True)
    query_part, keep, give = call(
        project_grads_kernel,
        [
            ((OWN, D), f32),
            ((SLOTS, SLOT_ROWS, 128), bf16),
            ((SLOTS, SLOT_ROWS, 128), bf16),
        ],
        [((D, 2 * KV), f32), ((PAD_D, RAW), f32)],
        dkv, dqp, nrow, xrow, xown, attention_gain, wq, wkv, pr, sq, gain_grad,
    )
    got = swap(give)
    acts_other, keep = lax.optimization_barrier((acts_other, keep))
    (slots,) = call(
        terms_kernel,
        [((SLOTS, SLOT_ROWS, 640), bf16)],
        [((HALF, RAW), f32), ((FF, RAW), bf16)],
        acts, acts_other,
        place=place,
    )
    keep, got, slots, dkv_came = lax.optimization_barrier((keep, got, slots, dkv_came))
    head_sum = (keep.astype(f32) + got.astype(f32)).astype(bf16)
    came = exchange(lax.dynamic_update_slice(slots, head_sum, (0, 0, 0)))
    (input_grad,) = call(
        input_kernel,
        [((OWN, D), f32)],
        [],
        dkv_came, query_part, xown, attention_gain, wkv, middle_grad,
    )

    first_total, second_total, query, key, value, out, gate_total, up_total, down_total = (
        pl.pallas_call(
            sum_kernel,
            grid=(4,),
            in_specs=[pl.BlockSpec((SLOTS // 4, SLOT_ROWS, 640), lambda i: (i, 0, 0))],
            out_specs=[pl.BlockSpec(memory_space=pltpu.VMEM)] * 9,
            out_shape=[
                jax.ShapeDtypeStruct(shape, f32)
                for shape in (
                    (1, D), (1, D), (36, 1, 72), (24, 36), (24, 36), (36, 1, 72), (36, 1, 192), (36, 1, 192), (72, 96),
                )
            ],
            scratch_shapes=[pltpu.VMEM((SLOT_ROWS, 640), f32)],
            compiler_params=pltpu.CompilerParams(vmem_limit_bytes=16 * 1024 * 1024),
        )(came)
    )
    return (
        result.reshape(BATCH, ROWS, D),
        input_grad.reshape(BATCH, ROWS, D),
        first_total,
        query.transpose(1, 0, 2),
        key.T[None],
        value.T[None],
        out.transpose(1, 0, 2),
        second_total,
        gate_total.transpose(1, 0, 2),
        up_total.transpose(1, 0, 2),
        down_total.T[None],
    )


def solution(mesh):
    weight = P(None, "dp", "ctx")
    rows = P("dp", "ctx", None)
    return jax.shard_map(
        body,
        mesh=mesh,
        in_specs=(rows, P("dp", "ctx"), rows, P(), weight, weight, weight, weight, P(), weight, weight, weight),
        out_specs=(rows, rows, P(), weight, weight, weight, weight, P(), weight, weight, weight),
        check_vma=False,
    )
```
